32 devices in a mesh: rep: 4 (over y, core), fsdp: 8 (over z, x).
Axes of the slice: x: 2, y: 2, z: 4, core: 2. Of those that a mesh axis runs over, the one named last changes fastest.
Arguments:
- inputs: bfloat16 [8192, 2048], P(('rep', 'fsdp')), may hold values from -18 to 18, as said below
- cotangent: bfloat16 [8192, 2048], P(('rep', 'fsdp')), may hold values from -6 to 6
- segment_ids: int32 [32, 256], P(('rep', 'fsdp')), may hold values from 0 to 3, never falling along the last dimension, each value on 1 to 128 neighbouring positions
- master_qkv: float32 [2048, 6144], P('fsdp', 'rep'), may hold values from -0.125 to 0.125
- master_out: float32 [2048, 2048], P('fsdp', 'rep'), may hold values from -0.5 to 0.5
- master_in: float32 [2048, 16384], P('fsdp', 'rep'), may hold values from -0.125 to 0.125
- master_down: float32 [8192, 2048], P('fsdp', 'rep'), may hold values from -0.09375 to 0.09375
- first_qkv: float32 [2048, 6144], P('fsdp', 'rep'), may hold values from -128 to 128
- first_out: float32 [2048, 2048], P('fsdp', 'rep'), may hold values from -16 to 16
- first_in: float32 [2048, 16384], P('fsdp', 'rep'), may hold values from -24 to 24
- first_down: float32 [8192, 2048], P('fsdp', 'rep'), may hold values from -32 to 32
- second_qkv: float32 [2048, 6144], P('fsdp', 'rep'), may hold values from 1720.32 to 6881.28
- second_out: float32 [2048, 2048], P('fsdp', 'rep'), may hold values from 38.5024 to 155.648
- second_in: float32 [2048, 16384], P('fsdp', 'rep'), may hold values from 68.8128 to 278.528
- second_down: float32 [8192, 2048], P('fsdp', 'rep'), may hold values from 155.648 to 622.592
Outputs:
- output: bfloat16 [8192, 2048], P(('rep', 'fsdp'))
- input_grad: bfloat16 [8192, 2048], P(('rep', 'fsdp'))
- grad_qkv: float32 [2048, 6144], P('fsdp', 'rep')
- grad_out: float32 [2048, 2048], P('fsdp', 'rep')
- grad_in: float32 [2048, 16384], P('fsdp', 'rep')
- grad_down: float32 [8192, 2048], P('fsdp', 'rep')
- updated_qkv: float32 [2048, 6144], P('fsdp', 'rep')
- updated_out: float32 [2048, 2048], P('fsdp', 'rep')
- updated_in: float32 [2048, 16384], P('fsdp', 'rep')
- updated_down: float32 [8192, 2048], P('fsdp', 'rep')
- moment_qkv: float32 [2048, 6144], P('fsdp', 'rep')
- moment_out: float32 [2048, 2048], P('fsdp', 'rep')
- moment_in: float32 [2048, 16384], P('fsdp', 'rep')
- moment_down: float32 [8192, 2048], P('fsdp', 'rep')
- variance_qkv: float32 [2048, 6144], P('fsdp', 'rep')
- variance_out: float32 [2048, 2048], P('fsdp', 'rep')
- variance_in: float32 [2048, 16384], P('fsdp', 'rep')
- variance_down: float32 [8192, 2048], P('fsdp', 'rep')
- narrow_qkv: bfloat16 [2048, 6144], P('fsdp', 'rep')
- narrow_out: bfloat16 [2048, 2048], P('fsdp', 'rep')
- narrow_in: bfloat16 [2048, 16384], P('fsdp', 'rep')
- narrow_down: bfloat16 [8192, 2048], P('fsdp', 'rep')
- stream_rms: float32 [2], replicated
The draws below stay inside these ranges and needn't reach their ends.
Inputs may be any that keep to these rules, and one draw needn't show every extreme that they name: `inputs`: activations whose rows differ in scale from sequence to sequence. `segment_ids`: each row is one packed sequence; segment ids never fall along it, and a document holds 1 to 128 tokens, one exactly that many.
All inputs are finite; a program needn't handle non-finite values.
Results may differ from the reference program's by a relative error of at most 0.019.
Values may be sent and summed in bfloat16 or wider, within the bound.
No kernel may reach another device: no remote copies, remote signals or barrier semaphores. Data moves between devices by JAX's collectives and lax.ppermute only.
A program may use at most 704 MiB of HBM per device.

```python
import math
import jax
import jax.numpy as jnp
import numpy as np
from jax import lax

D = 2048
HEADS = 16
HEAD_DIM = 128
FF = 8192
SEQ = 256
STEP = 10
SEQS = 32
TOKENS = 8192
REPLICAS = 4
SHARDS = 8


def draw_inputs(key, part):
    key = jax.random.fold_in(key, 11)
    owners = jnp.arange(TOKENS) // SEQ
    shard_place = (owners % SHARDS).astype(jnp.float32) / max(SHARDS - 1, 1)
    group_place = (owners // SHARDS).astype(jnp.float32) / max(REPLICAS - 1, 1)
    growth = 3.0
    noise = jax.random.truncated_normal(key, -6.0, 6.0, (TOKENS, D), jnp.float32)
    scaling = growth ** (0.5 * shard_place) * growth ** (0.5 * group_place)
    return (noise * scaling[:, None]).astype(jnp.bfloat16)


def block_scale(own_key, extent, pieces, smallest, high):
    level = 1.0
    for axis_at, parts in pieces:
        draws = jax.random.uniform(jax.random.fold_in(jax.random.fold_in(own_key, 6), axis_at), (parts,), jnp.float32, smallest / len(pieces), high / len(pieces))
        level = level * jnp.repeat(jnp.exp(draws), extent[axis_at] // parts).reshape((-1,) + (1,) * (len(extent) - 1 - axis_at))
    return level


def length_profile(amount, total, reach, skew):
    loads = [(1 << 20) // math.isqrt(standing ** skew) + 1 for standing in range(2, amount + 1)]
    rest, given = total - reach - (amount - 1), [1] * (amount - 1)
    while rest > 0:
        candidates = [i for i in range(amount - 1) if given[i] < reach]
        mass, remaining = sum([loads[i] for i in candidates]), rest
        for i in candidates:
            more = min(reach - given[i], max(1, remaining * loads[i] // mass), rest)
            given[i] = given[i] + more
            rest = rest - more
    return np.array([reach] + given)


def uneven_parts(rng, amount, total, reach, slope):
    if amount == 2:
        one = jax.random.randint(rng, (), max(1, total - reach), min(reach, total - 1) + 1)
        return jnp.stack([one, total - one])
    lengths = jnp.asarray(length_profile(amount, total, reach, slope), jnp.int32)
    pairs = (amount - 1) // 2
    source_of, receiver = lengths[1:1 + 2 * pairs:2], lengths[2:2 + 2 * pairs:2]
    room = jnp.minimum(source_of - 1, reach - receiver)
    shifted = jax.random.randint(jax.random.fold_in(rng, 1), (pairs,), 0, 1 << 20) % (room + 1)
    lengths = lengths.at[1:1 + 2 * pairs:2].set(source_of - shifted).at[2:2 + 2 * pairs:2].set(receiver + shifted)
    return lengths[jax.random.permutation(jax.random.fold_in(rng, 2), amount)]


def scatter_about(own_key, dims, scale, bound, shards=(), held_as=jnp.bfloat16):
    array = jax.random.normal(own_key, dims, jnp.float32) * scale
    if len(shards) > 0:
        array = block_scale(own_key, dims, shards, -0.22, 0.18) * array
    return jnp.clip(array, min=-bound, max=bound).astype(held_as)


def setup_inputs(seed: int = 0) -> dict:
    splits = jax.random.split(jax.random.key(seed), 16)
    inputs = draw_inputs(jax.random.fold_in(splits[15], 71), 0)
    cotangent = scatter_about(splits[1], (TOKENS, D), 1.0, 6.0, ((0, 32),))
    segment_ids = jax.vmap(lambda own: jnp.searchsorted(jnp.cumsum(uneven_parts(own, max(4, SEQ // 64), SEQ, SEQ // 2, 2)), jnp.arange(SEQ), side="right"))(jax.random.split(splits[2], SEQS)).reshape((SEQS, SEQ)).astype(jnp.int32)
    master_qkv = scatter_about(splits[3], (D, 3 * D), D ** -0.5, 0.125, ((0, 8), (1, 4)), jnp.float32)
    master_out = scatter_about(splits[4], (D, D), (D // 16) ** -0.5, 0.5, ((0, 8), (1, 4)), jnp.float32)
    master_in = scatter_about(splits[5], (D, 2 * FF), D ** -0.5, 0.125, ((0, 8), (1, 4)), jnp.float32)
    master_down = scatter_about(splits[6], (FF, D), (FF // 2) ** -0.5, 0.09375, ((0, 8), (1, 4)), jnp.float32)
    first_qkv = scatter_about(splits[7], (D, 3 * D), (0.22 * TOKENS ** 0.5), 128.0, ((0, 8), (1, 4)), jnp.float32)
    first_out = scatter_about(splits[8], (D, D), (0.033 * TOKENS ** 0.5), 16.0, ((0, 8), (1, 4)), jnp.float32)
    first_in = scatter_about(splits[9], (D, 2 * FF), (0.044 * TOKENS ** 0.5), 24.0, ((0, 8), (1, 4)), jnp.float32)
    first_down = scatter_about(splits[10], (FF, D), (0.066 * TOKENS ** 0.5), 32.0, ((0, 8), (1, 4)), jnp.float32)
    second_qkv = jnp.clip(jnp.exp(math.log(6881.28) - 1.3862944 * jax.random.uniform(splits[11], (D, 3 * D), jnp.float32) ** block_scale(splits[11], (D, 3 * D), ((0, 8), (1, 4)), -0.2, 0.2)), 1720.32, 6881.28)
    second_out = jnp.clip(jnp.exp(math.log(155.648) - 1.3968765 * jax.random.uniform(splits[12], (D, D), jnp.float32) ** block_scale(splits[12], (D, D), ((0, 8), (1, 4)), -0.2, 0.2)), 38.5024, 155.648)
    second_in = jnp.clip(jnp.exp(math.log(278.528) - 1.3981289 * jax.random.uniform(splits[13], (D, 2 * FF), jnp.float32) ** block_scale(splits[13], (D, 2 * FF), ((0, 8), (1, 4)), -0.2, 0.2)), 68.8128, 278.528)
    second_down = jnp.clip(jnp.exp(math.log(622.592) - 1.3862944 * jax.random.uniform(splits[14], (FF, D), jnp.float32) ** block_scale(splits[14], (FF, D), ((0, 8), (1, 4)), -0.2, 0.2)), 155.648, 622.592)
    return dict(inputs=inputs, cotangent=cotangent, segment_ids=segment_ids, master_qkv=master_qkv, master_out=master_out, master_in=master_in, master_down=master_down, first_qkv=first_qkv, first_out=first_out, first_in=first_in, first_down=first_down, second_qkv=second_qkv, second_out=second_out, second_in=second_in, second_down=second_down)


@jax.custom_vjp
def low(v):
    return lax.optimization_barrier(v.astype(jnp.bfloat16)).astype(jnp.float32)

@jax.custom_vjp
def low_back(v):
    return v

def low_keep(v):
    return (low(v), None)

def low_pass(kept, grad):
    return (grad,)

def back_keep(v):
    return (v, None)

def back_low(kept, grad):
    return (low(grad),)
low.defvjp(low_keep, low_pass)
low_back.defvjp(back_keep, back_low)
highest = lax.Precision.HIGHEST
beta_one = 0.9
beta_two = 0.95
rate = 0.02
rate_out = 0.08
decay = 0.1
epsilon = 1e-08

def normalize(values):
    centered = values - lax.optimization_barrier(jnp.mean(values, axis=-1, keepdims=True))
    return centered * lax.rsqrt(lax.optimization_barrier(jnp.mean(centered * centered, axis=-1, keepdims=True)) + 1e-05)

def rotate(values):
    half = values.shape[-1] // 2
    return jnp.concatenate([-values[..., half:], values[..., :half]], axis=-1)

def rotary_tables(length, size):
    half = size // 2
    freqs = 10000.0 ** (-(jnp.arange(half, dtype=jnp.float32) * 2.0) / size)
    angles = jnp.arange(length, dtype=jnp.float32)[:, None] * freqs[None, :]
    cosine = jnp.concatenate([jnp.cos(angles), jnp.cos(angles)], axis=-1)[:, None, :]
    sine = jnp.concatenate([jnp.sin(angles), jnp.sin(angles)], axis=-1)[:, None, :]
    return (cosine, sine)

def sequence_layer(source, segments, weight_qkv, weight_out, weight_in, weight_down):
    length = source.shape[0]
    width = source.shape[1]
    cosine, sine = rotary_tables(length, HEAD_DIM)
    places = jnp.arange(length)
    allowed = (segments[:, None] == segments[None, :]) & (places[None, :] <= places[:, None])
    lowered_one = low(normalize(source))
    projected = low_back(jnp.dot(lowered_one, weight_qkv, precision=highest))
    queries = projected[:, :width].reshape(length, HEADS, HEAD_DIM)
    keys = projected[:, width:2 * width].reshape(length, HEADS, HEAD_DIM)
    values = low(projected[:, 2 * width:].reshape(length, HEADS, HEAD_DIM))
    queries = low(queries * cosine + rotate(queries) * sine)
    keys = low(keys * cosine + rotate(keys) * sine)
    scores = low_back(jnp.einsum('shd,thd->hst', queries, keys, precision=highest) * HEAD_DIM ** (-0.5))
    scores = jnp.where(allowed[None], scores, -1e+30)
    probability = low(jax.nn.softmax(scores, axis=-1))
    mixed = jnp.einsum('hst,thd->shd', probability, values, precision=highest).reshape(length, width)
    mixed = low(low_back(mixed))
    stream = source + low_back(jnp.dot(mixed, weight_out, precision=highest))
    lowered_two = low(normalize(stream))
    gate_up = low_back(jnp.dot(lowered_two, weight_in, precision=highest))
    hidden = gate_up.shape[1] // 2
    active = low(jax.nn.silu(gate_up[:, :hidden]) * gate_up[:, hidden:])
    final = stream + low_back(jnp.dot(active, weight_down, precision=highest))
    return (final, stream)

def adam_step(master, gradient, first, second, step_rate):
    moment = beta_one * first + (1.0 - beta_one) * gradient
    variance = beta_two * second + (1.0 - beta_two) * gradient * gradient
    update = moment / (1.0 - beta_one ** STEP) / (jnp.sqrt(variance / (1.0 - beta_two ** STEP)) + epsilon)
    updated = master - step_rate * (update + decay * master)
    return (updated, moment, variance, updated.astype(jnp.bfloat16))

def reference(inputs, cotangent, segment_ids, master_qkv, master_out, master_in, master_down, first_qkv, first_out, first_in, first_down, second_qkv, second_out, second_in, second_down):
    copies = (low(master_qkv), low(master_out), low(master_in), low(master_down))
    per_block = math.gcd(SEQS, max(1, 4096 // SEQ))
    blocks = SEQS // per_block
    source = inputs.astype(jnp.float32).reshape(blocks, per_block, SEQ, D)
    back = cotangent.astype(jnp.float32).reshape(blocks, per_block, SEQ, D)
    segments = segment_ids.reshape(blocks, per_block, SEQ)
    layered = jax.vmap(sequence_layer, in_axes=(0, 0, None, None, None, None))

    def visit(carry, block):
        block_source, block_back, block_segments = block

        def forward(values, weight_qkv, weight_out, weight_in, weight_down):
            final, stream = layered(values, block_segments, weight_qkv, weight_out, weight_in, weight_down)
            return (final, stream)
        final, pullback, stream = jax.vjp(forward, block_source, copies[0], copies[1], copies[2], copies[3], has_aux=True)
        grads = pullback(block_back)
        totals, squares = carry
        totals = tuple((total + part for total, part in zip(totals, grads[1:])))
        squares = squares + jnp.stack([jnp.sum(stream * stream), jnp.sum(final * final)])
        return ((totals, squares), (final.astype(jnp.bfloat16), grads[0].astype(jnp.bfloat16)))
    start = (tuple((jnp.zeros_like(weight) for weight in copies)), jnp.zeros((2,), jnp.float32))
    (totals, squares), (outputs, input_grads) = lax.scan(visit, start, (source, back, segments))
    output = outputs.reshape(TOKENS, D)
    input_grad = input_grads.reshape(TOKENS, D)
    stream_rms = jnp.sqrt(squares / (TOKENS * D))
    grad_qkv, grad_out, grad_in, grad_down = totals
    updated_qkv, moment_qkv, variance_qkv, narrow_qkv = adam_step(master_qkv, grad_qkv, first_qkv, second_qkv, rate)
    updated_out, moment_out, variance_out, narrow_out = adam_step(master_out, grad_out, first_out, second_out, rate_out)
    updated_in, moment_in, variance_in, narrow_in = adam_step(master_in, grad_in, first_in, second_in, rate)
    updated_down, moment_down, variance_down, narrow_down = adam_step(master_down, grad_down, first_down, second_down, rate)
    return (output, input_grad, grad_qkv, grad_out, grad_in, grad_down, updated_qkv, updated_out, updated_in, updated_down, moment_qkv, moment_out, moment_in, moment_down, variance_qkv, variance_out, variance_in, variance_down, narrow_qkv, narrow_out, narrow_in, narrow_down, stream_rms)
```

```python
import functools

import jax
import jax.numpy as jnp
import numpy as np
from jax import lax
from jax.experimental import pallas as pl
from jax.experimental.pallas import tpu as pltpu
from jax.sharding import PartitionSpec as P

HEADS = 16
HEAD_DIM = 128
STEP = 10


beta_one = 0.9
beta_two = 0.95
rate = 0.02
rate_out = 0.08
decay = 0.1
epsilon = 1e-08


def normalize(values):
    centered = values - jnp.mean(values, axis=-1, keepdims=True)
    inverse = lax.rsqrt(jnp.mean(centered * centered, axis=-1, keepdims=True) + 1e-05)
    return (centered * inverse, inverse)


def norm_back(normed, inverse, gradient):
    first = jnp.mean(gradient, axis=-1, keepdims=True)
    second = jnp.mean(gradient * normed, axis=-1, keepdims=True)
    return inverse * (gradient - first - normed * second)


def rotate(values):
    half = values.shape[-1] // 2
    return jnp.concatenate([-values[..., half:], values[..., :half]], axis=-1)


def rotate_back(values):
    half = values.shape[-1] // 2
    return jnp.concatenate([values[..., half:], -values[..., :half]], axis=-1)


def rotary_tables(length, size):
    half = size // 2
    freqs = 10000.0 ** (-(jnp.arange(half, dtype=jnp.float32) * 2.0) / size)
    angles = jnp.arange(length, dtype=jnp.float32)[:, None] * freqs[None, :]
    cosine = jnp.concatenate([jnp.cos(angles), jnp.cos(angles)], axis=-1)[:, None, :]
    sine = jnp.concatenate([jnp.sin(angles), jnp.sin(angles)], axis=-1)[:, None, :]
    return (cosine, sine)


def group_gradient(operand, gradient):
    return lax.psum_scatter(
        lax.dot_general(
            operand, gradient, (((0,), (0,)), ((), ())), preferred_element_type=jnp.float32
        ).astype(jnp.bfloat16),
        "fsdp",
        scatter_dimension=0,
        tiled=True,
    ).astype(jnp.float32)


def adam_step(master, gradient, first, second, step_rate):
    moment = beta_one * first + (1.0 - beta_one) * gradient
    variance = beta_two * second + (1.0 - beta_two) * gradient * gradient
    update = (
        moment / (1.0 - beta_one**STEP) / (jnp.sqrt(variance / (1.0 - beta_two**STEP)) + epsilon)
    )
    updated = master - step_rate * (update + decay * master)
    return (updated, moment, variance, updated.astype(jnp.bfloat16))


def gathered_layer(
    inputs,
    cotangent,
    segment_ids,
    master_qkv,
    master_out,
    master_in,
    master_down,
    first_qkv,
    first_out,
    first_in,
    first_down,
    second_qkv,
    second_out,
    second_in,
    second_down,
):
    copies = (
        lax.all_gather(master_qkv.astype(jnp.bfloat16), "rep", axis=1, tiled=True),
        lax.all_gather(master_out.astype(jnp.bfloat16), "rep", axis=1, tiled=True),
        lax.all_gather(master_in.astype(jnp.bfloat16), "rep", axis=1, tiled=True),
        lax.all_gather(master_down.astype(jnp.bfloat16), "rep", axis=1, tiled=True),
    )

    def forward_product(operand, number):
        portion = copies[number]
        return jnp.dot(
            operand,
            lax.all_gather(portion, "fsdp", axis=0, tiled=True),
            preferred_element_type=jnp.float32,
        )

    def backward_product(gradient, number):
        return lax.dot_general(
            gradient,
            lax.all_gather(copies[number], "fsdp", axis=0, tiled=True),
            (((1,), (1,)), ((), ())),
            preferred_element_type=jnp.float32,
        )

    def weight_gradient(operand, gradient):
        return group_gradient(operand, gradient)

    length = inputs.shape[0]
    width = inputs.shape[1]
    scale = HEAD_DIM ** (-0.5)
    cosine, sine = rotary_tables(length, HEAD_DIM)
    segments = segment_ids[0]
    places = jnp.arange(length)
    allowed = (segments[:, None] == segments[None, :]) & (places[None, :] <= places[:, None])
    source = inputs.astype(jnp.float32)
    normed_one, inverse_one = normalize(source)
    lowered_one = normed_one.astype(jnp.bfloat16)
    projected = forward_product(lowered_one, 0)
    queries = projected[:, :width].reshape(length, HEADS, HEAD_DIM)
    keys = projected[:, width : 2 * width].reshape(length, HEADS, HEAD_DIM)
    values = projected[:, 2 * width :].reshape(length, HEADS, HEAD_DIM).astype(jnp.bfloat16)
    queries = (queries * cosine + rotate(queries) * sine).astype(jnp.bfloat16)
    keys = (keys * cosine + rotate(keys) * sine).astype(jnp.bfloat16)
    scores = jnp.einsum("shd,thd->hst", queries, keys, preferred_element_type=jnp.float32) * scale
    scores = jnp.where(allowed[None], scores, -1e30)
    probability = jax.nn.softmax(scores, axis=-1)
    prob_low = probability.astype(jnp.bfloat16)
    mixed = jnp.einsum("hst,thd->shd", prob_low, values, preferred_element_type=jnp.float32)
    mixed_low = mixed.reshape(length, width).astype(jnp.bfloat16)
    stream = source + forward_product(mixed_low, 1)
    normed_two, inverse_two = normalize(stream)
    lowered_two = normed_two.astype(jnp.bfloat16)
    gate_up = forward_product(lowered_two, 2)
    hidden = gate_up.shape[1] // 2
    gate = gate_up[:, :hidden]
    upper = gate_up[:, hidden:]
    sigmoid_gate = jax.nn.sigmoid(gate)
    silu_gate = gate * sigmoid_gate
    active_low = (silu_gate * upper).astype(jnp.bfloat16)
    final = stream + forward_product(active_low, 3)
    output = final.astype(jnp.bfloat16)
    summed_squares = lax.psum((jnp.sum(stream * stream), jnp.sum(final * final)), ("rep", "fsdp"))
    entries = length * width * lax.axis_size("rep") * lax.axis_size("fsdp")
    stream_rms = jnp.sqrt(jnp.stack(summed_squares) / entries)
    grad_down = weight_gradient(active_low, cotangent)
    active_grad = backward_product(cotangent, 3)
    gate_grad = active_grad * upper * sigmoid_gate * (1.0 + gate * (1.0 - sigmoid_gate))
    upper_grad = active_grad * silu_gate
    gate_up_grad = jnp.concatenate([gate_grad, upper_grad], axis=1).astype(jnp.bfloat16)
    grad_in = weight_gradient(lowered_two, gate_up_grad)
    lowered_two_grad = backward_product(gate_up_grad, 2)
    stream_grad = cotangent.astype(jnp.float32) + norm_back(
        normed_two, inverse_two, lowered_two_grad
    )
    stream_grad_low = stream_grad.astype(jnp.bfloat16)
    grad_out = weight_gradient(mixed_low, stream_grad_low)
    mixed_grad = backward_product(stream_grad_low, 1)
    mixed_grad_low = mixed_grad.reshape(length, HEADS, HEAD_DIM).astype(jnp.bfloat16)
    prob_grad = jnp.einsum(
        "shd,thd->hst", mixed_grad_low, values, preferred_element_type=jnp.float32
    )
    score_grad = probability * (
        prob_grad - jnp.sum(probability * prob_grad, axis=-1, keepdims=True)
    )
    score_grad_low = score_grad.astype(jnp.bfloat16)
    query_grad = (
        jnp.einsum("hst,thd->shd", score_grad_low, keys, preferred_element_type=jnp.float32) * scale
    )
    key_grad = (
        jnp.einsum("hst,shd->thd", score_grad_low, queries, preferred_element_type=jnp.float32)
        * scale
    )
    value_grad = jnp.einsum(
        "hst,shd->thd", prob_low, mixed_grad_low, preferred_element_type=jnp.float32
    )
    query_grad = query_grad * cosine + rotate_back(query_grad * sine)
    key_grad = key_grad * cosine + rotate_back(key_grad * sine)
    projected_grad = jnp.concatenate(
        [
            query_grad.reshape(length, width),
            key_grad.reshape(length, width),
            value_grad.reshape(length, width),
        ],
        axis=1,
    ).astype(jnp.bfloat16)
    grad_qkv = weight_gradient(lowered_one, projected_grad)
    lowered_one_grad = backward_product(projected_grad, 0)
    input_grad = (stream_grad + norm_back(normed_one, inverse_one, lowered_one_grad)).astype(
        jnp.bfloat16
    )
    summed = (
        lax.psum(grad_qkv.astype(jnp.bfloat16), "rep").astype(jnp.float32),
        lax.psum(grad_out.astype(jnp.bfloat16), "rep").astype(jnp.float32),
        lax.psum(grad_in.astype(jnp.bfloat16), "rep").astype(jnp.float32),
        lax.psum(grad_down.astype(jnp.bfloat16), "rep").astype(jnp.float32),
    )
    group = lax.axis_index("rep")
    reduced = tuple(
        (
            lax.dynamic_slice_in_dim(
                full,
                group * (full.shape[1] // lax.axis_size("rep")),
                full.shape[1] // lax.axis_size("rep"),
                1,
            )
            for full in summed
        )
    )
    updated_qkv, moment_qkv, variance_qkv, narrow_qkv = adam_step(
        master_qkv, reduced[0], first_qkv, second_qkv, rate
    )
    updated_out, moment_out, variance_out, narrow_out = adam_step(
        master_out, reduced[1], first_out, second_out, rate_out
    )
    updated_in, moment_in, variance_in, narrow_in = adam_step(
        master_in, reduced[2], first_in, second_in, rate
    )
    updated_down, moment_down, variance_down, narrow_down = adam_step(
        master_down, reduced[3], first_down, second_down, rate
    )
    return (
        output,
        input_grad,
        reduced[0],
        reduced[1],
        reduced[2],
        reduced[3],
        updated_qkv,
        updated_out,
        updated_in,
        updated_down,
        moment_qkv,
        moment_out,
        moment_in,
        moment_down,
        variance_qkv,
        variance_out,
        variance_in,
        variance_down,
        narrow_qkv,
        narrow_out,
        narrow_in,
        narrow_down,
        stream_rms,
    )


ALL = ("rep", "fsdp")
MASK_Y, MASK_C, MASK_HI, MASK_LO, MASK_X = 16, 8, 4, 2, 1
DEVICES = 32
ROWS = 256
FULL = jnp.float32
LOW = jnp.bfloat16


def swap(values, mask):
    return lax.ppermute(values, ALL, [(i, i ^ mask) for i in range(DEVICES)])


def half(values, axis, bit):
    size = values.shape[axis] // 2
    return lax.dynamic_slice_in_dim(values, bit * size, size, axis)


def columns(values, starts, width):
    return jnp.concatenate(
        [lax.dynamic_slice_in_dim(values, start, width, 1) for start in starts], axis=1
    )


def in_order(bit, mine, other, axis):
    first = jnp.where(bit == 0, mine, other)
    second = jnp.where(bit == 0, other, mine)
    return jnp.concatenate([first, second], axis=axis)


def dot(left, right):
    return jnp.dot(left, right, preferred_element_type=FULL)


def dot_back(left, right):
    return lax.dot_general(left, right, (((1,), (1,)), ((), ())), preferred_element_type=FULL)


def dot_tokens(left, right):
    return lax.dot_general(left, right, (((0,), (0,)), ((), ())), preferred_element_type=FULL)


def spread(piece):
    across = swap(piece, MASK_HI)
    pieces = {(0, 0): piece, (1, 0): across}
    pieces[0, 1] = swap(piece, MASK_X)
    pieces[1, 1] = swap(across, MASK_X)
    result = {}
    for (h, x), part in pieces.items():
        result[h, x, 0] = part
        result[h, x, 1] = swap(part, MASK_C)
    return result


def gather_tokens(values):
    rows = values.shape[0]
    cut = rows // 2
    from_y = swap(values, MASK_Y)
    from_lo = swap(values, MASK_LO)
    upper = swap(from_lo[:cut], MASK_Y)
    lower = swap(from_y[cut:], MASK_LO)
    return jnp.concatenate([values, from_y, upper, lower, from_lo], axis=0)


def sum_tokens(product, cut):
    rows = ROWS
    width = 2 * cut
    send_y = product(rows, 3 * rows, 0, cut).astype(LOW)
    got_y = swap(send_y, MASK_Y).astype(FULL)
    send_lo = product(2 * rows, 4 * rows, cut, width).astype(LOW)
    got_lo = swap(send_lo, MASK_LO).astype(FULL)
    next_lo = (product(3 * rows, 4 * rows, 0, cut) + got_y[rows:]).astype(LOW)
    last_lo = swap(next_lo, MASK_LO).astype(FULL)
    next_y = (product(rows, 2 * rows, cut, width) + got_lo[:rows]).astype(LOW)
    last_y = swap(next_y, MASK_Y).astype(FULL)
    own = product(0, rows, 0, width)
    return own + jnp.concatenate([got_y[:rows] + last_lo, got_lo[rows:] + last_y], axis=1)


def sum_rows(operand, gradient_own, gradient_other, x, hi):
    n = gradient_own.shape[1]
    for_core = dot_tokens(operand, gradient_other).astype(LOW)
    from_core = swap(for_core, MASK_C).reshape(4, 2, ROWS, n)

    def core_part(bit):
        return lax.dynamic_slice_in_dim(from_core, bit, 1, 1).reshape(4 * ROWS, n).astype(FULL)

    sent = columns(operand, [(2 * j + 1 - x) * ROWS for j in range(4)], ROWS)
    kept = columns(operand, [(2 * j + x) * ROWS for j in range(4)], ROWS)
    from_x = swap((dot_tokens(sent, gradient_own) + core_part(1 - x)).astype(LOW), MASK_X)
    core_kept = core_part(x)
    for_hi = (
        dot_tokens(half(kept, 1, 1 - hi), gradient_own)
        + half(core_kept, 0, 1 - hi)
        + half(from_x, 0, 1 - hi).astype(FULL)
    ).astype(LOW)
    from_hi = swap(for_hi, MASK_HI).astype(FULL)
    return (
        dot_tokens(half(kept, 1, hi), gradient_own)
        + half(core_kept, 0, hi)
        + half(from_x, 0, hi).astype(FULL)
        + from_hi
    )


def sum_columns(operand, gradient, c, x, hi, y):
    k = operand.shape[1] // 4
    quarter = gradient.shape[1] // 4
    other = columns(gradient, [(2 * j + 1 - c) * quarter for j in range(2)], quarter)
    own = columns(gradient, [(2 * j + c) * quarter for j in range(2)], quarter)
    from_core = swap(dot_tokens(operand, other).astype(LOW), MASK_C).reshape(2, 2, k, 2 * quarter)

    def core_part(bit):
        return (
            lax.dynamic_slice_in_dim(from_core, bit, 1, 1).reshape(2 * k, 2 * quarter).astype(FULL)
        )

    sent = columns(operand, [(2 * j + 1 - x) * k for j in range(2)], k)
    kept = columns(operand, [(2 * j + x) * k for j in range(2)], k)
    from_x = swap((dot_tokens(sent, own) + core_part(1 - x)).astype(LOW), MASK_X)
    core_kept = core_part(x)
    for_hi = (
        dot_tokens(half(kept, 1, 1 - hi), own)
        + half(core_kept, 0, 1 - hi)
        + half(from_x, 0, 1 - hi).astype(FULL)
    ).astype(LOW)
    from_hi = swap(for_hi, MASK_HI).astype(FULL)
    total = (
        dot_tokens(half(kept, 1, hi), own)
        + half(core_kept, 0, hi)
        + half(from_x, 0, hi).astype(FULL)
        + from_hi
    )
    mine = half(total, 1, y)
    theirs = swap(half(total, 1, 1 - y).astype(LOW), MASK_Y).astype(FULL)
    return in_order(y, mine, theirs, 0)


def gather_in(mine, other, y, c, hi, lo, x):
    piece = in_order(lo, mine, other, 0)
    n = piece.shape[1]
    whole = jnp.zeros((2, 2, 2, ROWS, 2 * n), LOW)
    for (h, e, o), part in spread(piece).items():
        whole = lax.dynamic_update_slice(
            whole, part.reshape(1, 2, 1, ROWS, n), (hi ^ h, 0, x ^ e, 0, (c ^ o) * n)
        )
    return whole.reshape(8 * ROWS, 2 * n)


def gather_down(weight, y, c, hi, x):
    low = weight.astype(LOW)
    mine = half(low, 0, y)
    other = swap(half(low, 0, 1 - y), MASK_Y)
    piece = in_order(y, mine, other, 1)
    k, n = mine.shape
    whole = jnp.zeros((2, 2, k, 4 * n), LOW)
    for (h, e, o), part in spread(piece).items():
        for place in range(2):
            whole = lax.dynamic_update_slice(
                whole,
                part[:, place * n : (place + 1) * n].reshape(1, 1, k, n),
                (hi ^ h, x ^ e, 0, (2 * place + (c ^ o)) * n),
            )
    return whole.reshape(4 * k, 4 * n)


def signed_tables():
    cosine, sine = rotary_tables(ROWS, HEAD_DIM)
    sign = jnp.concatenate(
        [-jnp.ones((HEAD_DIM // 2,), FULL), jnp.ones((HEAD_DIM // 2,), FULL)]
    )
    return (cosine[:, 0, :], sine[:, 0, :] * sign)


SCALE = HEAD_DIM ** (-0.5)
GROUP_HEADS = 4
GROUP_WIDTH = GROUP_HEADS * HEAD_DIM


def head_places(head):
    start = (head // 2) * 6 * HEAD_DIM + (head % 2) * HEAD_DIM
    return (start, start + 2 * HEAD_DIM, start + 4 * HEAD_DIM)


def softmax_rows(query, key, allowed):
    scores = dot_back(query, key) * SCALE
    scores = jnp.where(allowed, scores, -1e30)
    weights = jnp.exp(scores - jnp.max(scores, axis=-1, keepdims=True))
    return weights / jnp.sum(weights, axis=-1, keepdims=True)


def attend_kernel(projected, mask, cosine, sine, lowered, mixed):
    allowed = mask[...] > 0.0
    cos, sin = cosine[...], sine[...]
    for head in range(GROUP_HEADS):
        at_query, at_key, at_value = head_places(head)

        def rope(at):
            values = projected[:, at : at + HEAD_DIM]
            return (values * cos + pltpu.roll(values, HEAD_DIM // 2, 1) * sin).astype(LOW)

        query, key = rope(at_query), rope(at_key)
        value = projected[:, at_value : at_value + HEAD_DIM].astype(LOW)
        probability = softmax_rows(query, key, allowed)
        lowered[:, at_query : at_query + HEAD_DIM] = query
        lowered[:, at_key : at_key + HEAD_DIM] = key
        lowered[:, at_value : at_value + HEAD_DIM] = value
        mixed[:, head * HEAD_DIM : (head + 1) * HEAD_DIM] = dot(
            probability.astype(LOW), value
        ).astype(LOW)


def attend_back_kernel(lowered, mask, cosine, sine, mixed_grad, projected_grad):
    allowed = mask[...] > 0.0
    cos, sin = cosine[...], sine[...]
    for head in range(GROUP_HEADS):
        at_query, at_key, at_value = head_places(head)
        query = lowered[:, at_query : at_query + HEAD_DIM]
        key = lowered[:, at_key : at_key + HEAD_DIM]
        value = lowered[:, at_value : at_value + HEAD_DIM]
        grad = mixed_grad[:, head * HEAD_DIM : (head + 1) * HEAD_DIM]
        probability = softmax_rows(query, key, allowed)
        prob_grad = dot_back(grad, value)
        inner = jnp.sum(probability * prob_grad, axis=-1, keepdims=True)
        score_grad = (probability * (prob_grad - inner)).astype(LOW)
        query_grad = dot(score_grad, key) * SCALE
        key_grad = dot_tokens(score_grad, query) * SCALE
        value_grad = dot_tokens(probability.astype(LOW), grad)

        def unrope(values):
            return (values * cos - pltpu.roll(values, HEAD_DIM // 2, 1) * sin).astype(LOW)

        projected_grad[:, at_query : at_query + HEAD_DIM] = unrope(query_grad)
        projected_grad[:, at_key : at_key + HEAD_DIM] = unrope(key_grad)
        projected_grad[:, at_value : at_value + HEAD_DIM] = value_grad.astype(LOW)


def row_block(width):
    return pl.BlockSpec((ROWS, width), lambda i: (i, 0))


def whole_block(width):
    return pl.BlockSpec((ROWS, width), lambda i: (0, 0))


def attend(projected, mask, cosine, sine):
    rows = projected.shape[0]
    return pl.pallas_call(
        attend_kernel,
        grid=(rows // ROWS,),
        in_specs=[
            row_block(3 * GROUP_WIDTH),
            row_block(ROWS),
            whole_block(HEAD_DIM),
            whole_block(HEAD_DIM),
        ],
        out_specs=[row_block(3 * GROUP_WIDTH), row_block(GROUP_WIDTH)],
        out_shape=[
            jax.ShapeDtypeStruct((rows, 3 * GROUP_WIDTH), LOW),
            jax.ShapeDtypeStruct((rows, GROUP_WIDTH), LOW),
        ],
        compiler_params=pltpu.CompilerParams(vmem_limit_bytes=32 * 2**20),
        cost_estimate=pl.CostEstimate(
            flops=4 * rows * ROWS * GROUP_WIDTH,
            bytes_accessed=rows * GROUP_WIDTH * 20,
            transcendentals=rows * ROWS * GROUP_HEADS,
        ),
    )(projected, mask, cosine, sine)


def attend_back(lowered, mask, cosine, sine, mixed_grad):
    rows = lowered.shape[0]
    return pl.pallas_call(
        attend_back_kernel,
        grid=(rows // ROWS,),
        in_specs=[
            row_block(3 * GROUP_WIDTH),
            row_block(ROWS),
            whole_block(HEAD_DIM),
            whole_block(HEAD_DIM),
            row_block(GROUP_WIDTH),
        ],
        out_specs=row_block(3 * GROUP_WIDTH),
        out_shape=jax.ShapeDtypeStruct((rows, 3 * GROUP_WIDTH), LOW),
        compiler_params=pltpu.CompilerParams(vmem_limit_bytes=32 * 2**20),
        cost_estimate=pl.CostEstimate(
            flops=10 * rows * ROWS * GROUP_WIDTH,
            bytes_accessed=rows * GROUP_WIDTH * 14,
            transcendentals=rows * ROWS * GROUP_HEADS,
        ),
    )(lowered, mask, cosine, sine, mixed_grad)


def split_layer(
    inputs,
    cotangent,
    segment_ids,
    master_qkv,
    master_out,
    master_in,
    master_down,
    first_qkv,
    first_out,
    first_in,
    first_down,
    second_qkv,
    second_out,
    second_in,
    second_down,
):
    rep, fsdp = lax.axis_index("rep"), lax.axis_index("fsdp")
    y, c = rep // 2, rep % 2
    hi, lo, x = fsdp // 4, (fsdp // 2) % 2, fsdp % 2
    width = inputs.shape[1]
    unit = width // 4

    source = inputs.astype(FULL)
    normed_one, inverse_one = normalize(source)
    rows_one = gather_tokens(normed_one.astype(LOW))
    segments_y = swap(segment_ids, MASK_Y)
    segments = jnp.concatenate(
        [segment_ids, segments_y, swap(segments_y, MASK_LO), swap(segment_ids, MASK_LO)], axis=0
    )
    places = jnp.arange(ROWS)
    allowed = (segments[:, :, None] == segments[:, None, :]) & (places[None, :] <= places[:, None])
    mask = allowed.astype(FULL).reshape(4 * ROWS, ROWS)
    cosine, sine = signed_tables()

    low = master_qkv.astype(LOW)
    pair = 2 * HEAD_DIM
    pairs = low.shape[1] // pair
    kept = columns(low, [j * pair + y * HEAD_DIM for j in range(pairs)], HEAD_DIM)
    given = columns(low, [j * pair + (1 - y) * HEAD_DIM for j in range(pairs)], HEAD_DIM)
    block = kept.shape[1]
    mine = in_order(y, kept, swap(given, MASK_Y), 1)
    theirs = swap(mine, MASK_C)
    even, odd = jnp.where(c == 0, mine, theirs), jnp.where(c == 0, theirs, mine)
    all_pairs = jnp.concatenate(
        [even[:, :block], odd[:, :block], even[:, block:], odd[:, block:]], axis=1
    )

    def pair_columns(hi_bit, lo_bit):
        return columns(
            all_pairs, [(8 * j + 4 * hi_bit + 2 * lo_bit) * HEAD_DIM for j in range(3)], 2 * HEAD_DIM
        )

    weight_qkv = gather_in(
        pair_columns(c, lo), swap(pair_columns(c, 1 - lo), MASK_LO), y, c, hi, lo, x
    )

    weight_out = gather_down(master_out, y, c, hi, x)

    low = master_in.astype(LOW)

    def unit_columns(lo_bit, y_bit):
        return columns(low, [(4 * lo_bit + 2 * j + y_bit) * unit for j in range(2)], unit)

    weight_a = gather_in(
        unit_columns(lo, y), swap(unit_columns(1 - lo, y), MASK_LO), y, c, hi, lo, x
    )
    weight_b = gather_in(
        swap(unit_columns(lo, 1 - y), MASK_Y),
        swap(unit_columns(1 - lo, 1 - y), MASK_Y | MASK_LO),
        y,
        c,
        hi,
        lo,
        x,
    )
    weight_down = gather_down(master_down, y, c, hi, x)

    projected = dot(rows_one, weight_qkv)
    lowered, mixed_low = attend(projected, mask, cosine, sine)
    stream = source + sum_tokens(
        lambda a, b, l, h: dot(mixed_low[a:b], weight_out[:, l:h]), width // 2
    )
    normed_two, inverse_two = normalize(stream)
    rows_two = gather_tokens(normed_two.astype(LOW))

    product_a, product_b = dot(rows_two, weight_a), dot(rows_two, weight_b)
    gate = jnp.where(y == 0, product_a, product_b)
    upper = jnp.where(y == 0, product_b, product_a)
    sigmoid_gate = jax.nn.sigmoid(gate)
    silu_gate = gate * sigmoid_gate
    active_low = (silu_gate * upper).astype(LOW)
    final = stream + sum_tokens(
        lambda a, b, l, h: dot(active_low[a:b], weight_down[:, l:h]), width // 2
    )
    output = final.astype(LOW)
    summed_squares = lax.psum((jnp.sum(stream * stream), jnp.sum(final * final)), ALL)
    stream_rms = jnp.sqrt(jnp.stack(summed_squares) / (ROWS * width * DEVICES))

    rows_cotangent = gather_tokens(cotangent)
    grad_down = sum_columns(active_low, rows_cotangent, c, x, hi, y)
    active_grad = dot_back(rows_cotangent, weight_down)
    gate_grad = active_grad * upper * sigmoid_gate * (1.0 + gate * (1.0 - sigmoid_gate))
    upper_grad = active_grad * silu_gate
    grad_a = jnp.where(y == 0, gate_grad, upper_grad).astype(LOW)
    grad_b = jnp.where(y == 0, upper_grad, gate_grad).astype(LOW)
    lowered_two_grad = sum_tokens(
        lambda a, b, l, h: (
            dot_back(grad_a[a:b], weight_a[l:h]) + dot_back(grad_b[a:b], weight_b[l:h])
        ),
        width // 2,
    )
    total_a = sum_rows(rows_two, half(grad_a, 1, c), half(grad_a, 1, 1 - c), x, hi)
    total_b = sum_rows(rows_two, half(grad_b, 1, c), half(grad_b, 1, 1 - c), x, hi)
    kept = half(total_a, 0, lo)
    from_lo = swap(half(total_a, 0, 1 - lo).astype(LOW), MASK_LO).astype(FULL)
    from_y = swap(half(total_b, 0, lo).astype(LOW), MASK_Y).astype(FULL)
    from_both = swap(half(total_b, 0, 1 - lo).astype(LOW), MASK_Y | MASK_LO).astype(FULL)

    def lo_rows(mine, other, bit):
        return jnp.where(lo == bit, mine, other)

    blocks = []
    for bit in range(2):
        mine, other = lo_rows(kept, from_lo, bit), lo_rows(from_y, from_both, bit)
        even, odd = jnp.where(y == 0, mine, other), jnp.where(y == 0, other, mine)
        for j in range(2):
            blocks += [even[:, j * unit : (j + 1) * unit], odd[:, j * unit : (j + 1) * unit]]
    grad_in = jnp.concatenate(blocks, axis=1)

    stream_grad = cotangent.astype(FULL) + norm_back(normed_two, inverse_two, lowered_two_grad)
    rows_stream = gather_tokens(stream_grad.astype(LOW))

    mixed_grad_low = dot_back(rows_stream, weight_out).astype(LOW)
    grad_out = sum_columns(mixed_low, rows_stream, c, x, hi, y)
    projected_grad = attend_back(lowered, mask, cosine, sine, mixed_grad_low)
    lowered_one_grad = sum_tokens(
        lambda a, b, l, h: dot_back(projected_grad[a:b], weight_qkv[l:h]), width // 2
    )
    input_grad = (stream_grad + norm_back(normed_one, inverse_one, lowered_one_grad)).astype(LOW)
    total = sum_rows(
        rows_one, half(projected_grad, 1, c), half(projected_grad, 1, 1 - c), x, hi
    ).astype(LOW)
    kept, given = half(total, 0, lo), half(total, 0, 1 - lo)
    got = swap(given, MASK_LO)
    even, odd = jnp.where(lo == 0, kept, got), jnp.where(lo == 0, got, kept)
    core_pairs = jnp.concatenate(
        [
            part[:, j * pair : (j + 1) * pair]
            for j in range(3)
            for part in (even, odd)
        ],
        axis=1,
    )
    other_pairs = swap(core_pairs, MASK_C)
    even, odd = (
        jnp.where(c == 0, core_pairs, other_pairs),
        jnp.where(c == 0, other_pairs, core_pairs),
    )
    all_pairs = jnp.concatenate(
        [
            part[:, j * 2 * pair : (j + 1) * 2 * pair]
            for j in range(3)
            for part in (even, odd)
        ],
        axis=1,
    )
    mine = lax.dynamic_slice_in_dim(all_pairs, (2 * y + c) * block, block, 1)
    given = lax.dynamic_slice_in_dim(all_pairs, (2 * (1 - y) + c) * block, block, 1)
    got = swap(given, MASK_Y)
    even, odd = jnp.where(y == 0, mine, got), jnp.where(y == 0, got, mine)
    grad_qkv = jnp.concatenate(
        [
            part[:, j * HEAD_DIM : (j + 1) * HEAD_DIM]
            for j in range(pairs)
            for part in (even, odd)
        ],
        axis=1,
    ).astype(FULL)

    grads = (grad_qkv, grad_out, grad_in, grad_down)
    masters = (master_qkv, master_out, master_in, master_down)
    firsts = (first_qkv, first_out, first_in, first_down)
    seconds = (second_qkv, second_out, second_in, second_down)
    rates = (rate, rate_out, rate, rate)
    steps = [adam_step(*parts) for parts in zip(masters, grads, firsts, seconds, rates)]
    updated, moments, variances, narrows = zip(*steps)
    return (output, input_grad, *grads, *updated, *moments, *variances, *narrows, stream_rms)


def solution(mesh):
    shards = split_layer if tuple(mesh.shape.values()) == (4, 8) else gathered_layer
    return jax.shard_map(
        shards,
        mesh=mesh,
        in_specs=(
            P(("rep", "fsdp"), None),
            P(("rep", "fsdp"), None),
            P(("rep", "fsdp"), None),
            P("fsdp", "rep"),
            P("fsdp", "rep"),
            P("fsdp", "rep"),
            P("fsdp", "rep"),
            P("fsdp", "rep"),
            P("fsdp", "rep"),
            P("fsdp", "rep"),
            P("fsdp", "rep"),
            P("fsdp", "rep"),
            P("fsdp", "rep"),
            P("fsdp", "rep"),
            P("fsdp", "rep"),
        ),
        out_specs=(
            P(("rep", "fsdp"), None),
            P(("rep", "fsdp"), None),
            P("fsdp", "rep"),
            P("fsdp", "rep"),
            P("fsdp", "rep"),
            P("fsdp", "rep"),
            P("fsdp", "rep"),
            P("fsdp", "rep"),
            P("fsdp", "rep"),
            P("fsdp", "rep"),
            P("fsdp", "rep"),
            P("fsdp", "rep"),
            P("fsdp", "rep"),
            P("fsdp", "rep"),
            P("fsdp", "rep"),
            P("fsdp", "rep"),
            P("fsdp", "rep"),
            P("fsdp", "rep"),
            P("fsdp", "rep"),
            P("fsdp", "rep"),
            P("fsdp", "rep"),
            P("fsdp", "rep"),
            P(),
        ),
        check_vma=False,
    )
```

```python
import functools

import jax
import jax.numpy as jnp
import numpy as np
from jax import lax
from jax.experimental import pallas as pl
from jax.experimental.pallas import tpu as pltpu
from jax.sharding import PartitionSpec as P

HEADS = 16
HEAD_DIM = 128
STEP = 10


beta_one = 0.9
beta_two = 0.95
rate = 0.02
rate_out = 0.08
decay = 0.1
epsilon = 1e-08


def normalize(values):
    centered = values - jnp.mean(values, axis=-1, keepdims=True)
    inverse = lax.rsqrt(jnp.mean(centered * centered, axis=-1, keepdims=True) + 1e-05)
    return (centered * inverse, inverse)


def norm_back(normed, inverse, gradient):
    first = jnp.mean(gradient, axis=-1, keepdims=True)
    second = jnp.mean(gradient * normed, axis=-1, keepdims=True)
    return inverse * (gradient - first - normed * second)


def rotate(values):
    half = values.shape[-1] // 2
    return jnp.concatenate([-values[..., half:], values[..., :half]], axis=-1)


def rotate_back(values):
    half = values.shape[-1] // 2
    return jnp.concatenate([values[..., half:], -values[..., :half]], axis=-1)


def rotary_tables(length, size):
    half = size // 2
    freqs = 10000.0 ** (-(jnp.arange(half, dtype=jnp.float32) * 2.0) / size)
    angles = jnp.arange(length, dtype=jnp.float32)[:, None] * freqs[None, :]
    cosine = jnp.concatenate([jnp.cos(angles), jnp.cos(angles)], axis=-1)[:, None, :]
    sine = jnp.concatenate([jnp.sin(angles), jnp.sin(angles)], axis=-1)[:, None, :]
    return (cosine, sine)


def group_gradient(operand, gradient):
    return lax.psum_scatter(
        lax.dot_general(
            operand, gradient, (((0,), (0,)), ((), ())), preferred_element_type=jnp.float32
        ).astype(jnp.bfloat16),
        "fsdp",
        scatter_dimension=0,
        tiled=True,
    ).astype(jnp.float32)


def adam_step(master, gradient, first, second, step_rate):
    moment = beta_one * first + (1.0 - beta_one) * gradient
    variance = beta_two * second + (1.0 - beta_two) * gradient * gradient
    update = (
        moment / (1.0 - beta_one**STEP) / (jnp.sqrt(variance / (1.0 - beta_two**STEP)) + epsilon)
    )
    updated = master - step_rate * (update + decay * master)
    return (updated, moment, variance, updated.astype(jnp.bfloat16))


def gathered_layer(
    inputs,
    cotangent,
    segment_ids,
    master_qkv,
    master_out,
    master_in,
    master_down,
    first_qkv,
    first_out,
    first_in,
    first_down,
    second_qkv,
    second_out,
    second_in,
    second_down,
):
    copies = (
        lax.all_gather(master_qkv.astype(jnp.bfloat16), "rep", axis=1, tiled=True),
        lax.all_gather(master_out.astype(jnp.bfloat16), "rep", axis=1, tiled=True),
        lax.all_gather(master_in.astype(jnp.bfloat16), "rep", axis=1, tiled=True),
        lax.all_gather(master_down.astype(jnp.bfloat16), "rep", axis=1, tiled=True),
    )

    def forward_product(operand, number):
        portion = copies[number]
        return jnp.dot(
            operand,
            lax.all_gather(portion, "fsdp", axis=0, tiled=True),
            preferred_element_type=jnp.float32,
        )

    def backward_product(gradient, number):
        return lax.dot_general(
            gradient,
            lax.all_gather(copies[number], "fsdp", axis=0, tiled=True),
            (((1,), (1,)), ((), ())),
            preferred_element_type=jnp.float32,
        )

    def weight_gradient(operand, gradient):
        return group_gradient(operand, gradient)

    length = inputs.shape[0]
    width = inputs.shape[1]
    scale = HEAD_DIM ** (-0.5)
    cosine, sine = rotary_tables(length, HEAD_DIM)
    segments = segment_ids[0]
    places = jnp.arange(length)
    allowed = (segments[:, None] == segments[None, :]) & (places[None, :] <= places[:, None])
    source = inputs.astype(jnp.float32)
    normed_one, inverse_one = normalize(source)
    lowered_one = normed_one.astype(jnp.bfloat16)
    projected = forward_product(lowered_one, 0)
    queries = projected[:, :width].reshape(length, HEADS, HEAD_DIM)
    keys = projected[:, width : 2 * width].reshape(length, HEADS, HEAD_DIM)
    values = projected[:, 2 * width :].reshape(length, HEADS, HEAD_DIM).astype(jnp.bfloat16)
    queries = (queries * cosine + rotate(queries) * sine).astype(jnp.bfloat16)
    keys = (keys * cosine + rotate(keys) * sine).astype(jnp.bfloat16)
    scores = jnp.einsum("shd,thd->hst", queries, keys, preferred_element_type=jnp.float32) * scale
    scores = jnp.where(allowed[None], scores, -1e30)
    probability = jax.nn.softmax(scores, axis=-1)
    prob_low = probability.astype(jnp.bfloat16)
    mixed = jnp.einsum("hst,thd->shd", prob_low, values, preferred_element_type=jnp.float32)
    mixed_low = mixed.reshape(length, width).astype(jnp.bfloat16)
    stream = source + forward_product(mixed_low, 1)
    normed_two, inverse_two = normalize(stream)
    lowered_two = normed_two.astype(jnp.bfloat16)
    gate_up = forward_product(lowered_two, 2)
    hidden = gate_up.shape[1] // 2
    gate = gate_up[:, :hidden]
    upper = gate_up[:, hidden:]
    sigmoid_gate = jax.nn.sigmoid(gate)
    silu_gate = gate * sigmoid_gate
    active_low = (silu_gate * upper).astype(jnp.bfloat16)
    final = stream + forward_product(active_low, 3)
    output = final.astype(jnp.bfloat16)
    summed_squares = lax.psum((jnp.sum(stream * stream), jnp.sum(final * final)), ("rep", "fsdp"))
    entries = length * width * lax.axis_size("rep") * lax.axis_size("fsdp")
    stream_rms = jnp.sqrt(jnp.stack(summed_squares) / entries)
    grad_down = weight_gradient(active_low, cotangent)
    active_grad = backward_product(cotangent, 3)
    gate_grad = active_grad * upper * sigmoid_gate * (1.0 + gate * (1.0 - sigmoid_gate))
    upper_grad = active_grad * silu_gate
    gate_up_grad = jnp.concatenate([gate_grad, upper_grad], axis=1).astype(jnp.bfloat16)
    grad_in = weight_gradient(lowered_two, gate_up_grad)
    lowered_two_grad = backward_product(gate_up_grad, 2)
    stream_grad = cotangent.astype(jnp.float32) + norm_back(
        normed_two, inverse_two, lowered_two_grad
    )
    stream_grad_low = stream_grad.astype(jnp.bfloat16)
    grad_out = weight_gradient(mixed_low, stream_grad_low)
    mixed_grad = backward_product(stream_grad_low, 1)
    mixed_grad_low = mixed_grad.reshape(length, HEADS, HEAD_DIM).astype(jnp.bfloat16)
    prob_grad = jnp.einsum(
        "shd,thd->hst", mixed_grad_low, values, preferred_element_type=jnp.float32
    )
    score_grad = probability * (
        prob_grad - jnp.sum(probability * prob_grad, axis=-1, keepdims=True)
    )
    score_grad_low = score_grad.astype(jnp.bfloat16)
    query_grad = (
        jnp.einsum("hst,thd->shd", score_grad_low, keys, preferred_element_type=jnp.float32) * scale
    )
    key_grad = (
        jnp.einsum("hst,shd->thd", score_grad_low, queries, preferred_element_type=jnp.float32)
        * scale
    )
    value_grad = jnp.einsum(
        "hst,shd->thd", prob_low, mixed_grad_low, preferred_element_type=jnp.float32
    )
    query_grad = query_grad * cosine + rotate_back(query_grad * sine)
    key_grad = key_grad * cosine + rotate_back(key_grad * sine)
    projected_grad = jnp.concatenate(
        [
            query_grad.reshape(length, width),
            key_grad.reshape(length, width),
            value_grad.reshape(length, width),
        ],
        axis=1,
    ).astype(jnp.bfloat16)
    grad_qkv = weight_gradient(lowered_one, projected_grad)
    lowered_one_grad = backward_product(projected_grad, 0)
    input_grad = (stream_grad + norm_back(normed_one, inverse_one, lowered_one_grad)).astype(
        jnp.bfloat16
    )
    summed = (
        lax.psum(grad_qkv.astype(jnp.bfloat16), "rep").astype(jnp.float32),
        lax.psum(grad_out.astype(jnp.bfloat16), "rep").astype(jnp.float32),
        lax.psum(grad_in.astype(jnp.bfloat16), "rep").astype(jnp.float32),
        lax.psum(grad_down.astype(jnp.bfloat16), "rep").astype(jnp.float32),
    )
    group = lax.axis_index("rep")
    reduced = tuple(
        (
            lax.dynamic_slice_in_dim(
                full,
                group * (full.shape[1] // lax.axis_size("rep")),
                full.shape[1] // lax.axis_size("rep"),
                1,
            )
            for full in summed
        )
    )
    updated_qkv, moment_qkv, variance_qkv, narrow_qkv = adam_step(
        master_qkv, reduced[0], first_qkv, second_qkv, rate
    )
    updated_out, moment_out, variance_out, narrow_out = adam_step(
        master_out, reduced[1], first_out, second_out, rate_out
    )
    updated_in, moment_in, variance_in, narrow_in = adam_step(
        master_in, reduced[2], first_in, second_in, rate
    )
    updated_down, moment_down, variance_down, narrow_down = adam_step(
        master_down, reduced[3], first_down, second_down, rate
    )
    return (
        output,
        input_grad,
        reduced[0],
        reduced[1],
        reduced[2],
        reduced[3],
        updated_qkv,
        updated_out,
        updated_in,
        updated_down,
        moment_qkv,
        moment_out,
        moment_in,
        moment_down,
        variance_qkv,
        variance_out,
        variance_in,
        variance_down,
        narrow_qkv,
        narrow_out,
        narrow_in,
        narrow_down,
        stream_rms,
    )


ALL = ("rep", "fsdp")
MASK_Y, MASK_C, MASK_HI, MASK_E, MASK_T = 16, 8, 4, 2, 1
DEVICES = 32
ROWS = 256
FULL = jnp.float32
LOW = jnp.bfloat16


def swap(values, mask):
    return lax.ppermute(values, ALL, [(i, i ^ mask) for i in range(DEVICES)])


def half(values, axis, bit):
    size = values.shape[axis] // 2
    return lax.dynamic_slice_in_dim(values, bit * size, size, axis)


class Steps:
    def __init__(self):
        self.last = ()

    def do(self, work, *values):
        values, _ = lax.optimization_barrier((values, self.last))
        result = work(*values)
        self.last = (jax.tree.leaves(result)[0],)
        return result

    def wait(self, value):
        return self.do(lambda v: v, value)


def columns(values, starts, width):
    return jnp.concatenate(
        [lax.dynamic_slice_in_dim(values, start, width, 1) for start in starts], axis=1
    )


def in_order(bit, mine, other, axis):
    first = jnp.where(bit == 0, mine, other)
    second = jnp.where(bit == 0, other, mine)
    return jnp.concatenate([first, second], axis=axis)


def dot(left, right):
    return jnp.dot(left, right, preferred_element_type=FULL)


def dot_back(left, right):
    return lax.dot_general(left, right, (((1,), (1,)), ((), ())), preferred_element_type=FULL)


def dot_tokens(left, right):
    return lax.dot_general(left, right, (((0,), (0,)), ((), ())), preferred_element_type=FULL)


def low_dot_tokens(left, right):
    return dot_tokens(left, right).astype(LOW)


class Tokens:
    def __init__(self, values):
        self.values = values

    def send_y(self, steps):
        self.from_y = swap(steps.wait(self.values), MASK_Y)

    def send_t(self, steps):
        self.from_t = swap(steps.wait(self.values), MASK_T)

    def send(self, steps):
        self.values = steps.wait(self.values)
        self.from_y = swap(self.values, MASK_Y)
        self.from_t = swap(self.values, MASK_T)

    def second(self, steps):
        cut = ROWS // 2

        def parts(from_t, from_y):
            upper = from_t[:cut]
            if from_t.shape[0] > ROWS:
                upper = jnp.concatenate([upper, from_t[ROWS:]], axis=0)
            return upper, from_y[cut:ROWS]

        upper, lower = steps.do(parts, self.from_t, self.from_y)
        self.upper = swap(upper, MASK_Y)
        self.lower = swap(lower, MASK_T)

    def rows(self, steps):
        cut = ROWS // 2
        return steps.do(
            functools.partial(join_rows, (ROWS, ROWS, cut, cut, ROWS)),
            self.values,
            self.from_y,
            self.upper,
            self.lower,
            self.from_t,
        )


class Sum:
    def __init__(self, product, *values):
        self.product = product
        self.values = values

    def first(self, steps):
        self.give_y, self.give_t = steps.do(
            lambda *v: (self.product((1, 2), 0, LOW, *v), self.product((2, 3), 1, LOW, *v)),
            *self.values,
        )

    def release(self, steps):
        self.give_y, self.give_t = steps.do(lambda *v: v, self.give_y, self.give_t)

    def send(self):
        self.got_y = swap(self.give_y, MASK_Y)
        self.got_t = swap(self.give_t, MASK_T)

    def own(self, steps):
        self.mine = steps.do(
            lambda *v: (self.product((0, 3), 0, FULL, *v), self.product((0, 1), 1, FULL, *v)),
            *self.values,
        )

    def second(self, steps):
        give_t, give_y = steps.do(
            lambda got_y, got_t, side_0, side_1: (
                (side_0[ROWS:] + got_y[ROWS:].astype(FULL)).astype(LOW),
                (side_1[ROWS:] + got_t[:ROWS].astype(FULL)).astype(LOW),
            ),
            self.got_y,
            self.got_t,
            *self.mine,
        )
        self.last_t = swap(give_t, MASK_T)
        self.last_y = swap(give_y, MASK_Y)

    def total(self, side_0, side_1, got_y, got_t, last_t, last_y):
        return (
            side_0[:ROWS] + got_y[:ROWS].astype(FULL) + last_t.astype(FULL),
            side_1[:ROWS] + got_t[ROWS:].astype(FULL) + last_y.astype(FULL),
        )

    def parts(self):
        return (*self.mine, self.got_y, self.got_t, self.last_t, self.last_y)


class RowSum:
    def __init__(self, operand, own, other):
        self.operand, self.own, self.other = operand, own, other
        self.cut = operand.shape[1] // 4

    def core(self, steps):
        self.from_core = swap(steps.do(low_dot_tokens, self.operand, self.other), MASK_C)

    def across_x(self, steps):
        def work(operand, own, from_core):
            product = dot_tokens(operand[:, 2 * self.cut :], own)
            return (product + from_core[2 * self.cut :].astype(FULL)).astype(LOW)

        self.from_x = swap(steps.do(work, self.operand, self.own, self.from_core), MASK_E)

    def side(self, at, operand, own, from_core, from_x):
        at = slice(at * self.cut, (at + 1) * self.cut)
        return (
            dot_tokens(operand[:, at], own) + from_core[at].astype(FULL) + from_x[at].astype(FULL)
        )

    def across_hi(self, steps):
        self.from_hi = swap(
            steps.do(
                lambda *v: self.side(1, *v).astype(LOW),
                self.operand,
                self.own,
                self.from_core,
                self.from_x,
            ),
            MASK_HI,
        )

    def total(self, operand, own, from_core, from_x, from_hi):
        return self.side(0, operand, own, from_core, from_x) + from_hi.astype(FULL)

    def parts(self):
        return (self.operand, self.own, self.from_core, self.from_x, self.from_hi)


class ColumnSum:
    def __init__(self, operand, gradient, c, x, hi, y):
        self.operand, self.gradient = operand, gradient
        self.c, self.x, self.at, self.y = c, x, hi ^ c, y
        self.k = operand.shape[1] // 4
        self.n = gradient.shape[1] // 4

    def core_columns(self, gradient, bit):
        return gradient[:, bit * 2 * self.n : (bit + 1) * 2 * self.n]

    def core(self, steps):
        self.from_core = swap(
            steps.do(
                lambda operand, gradient: low_dot_tokens(
                    operand, self.core_columns(gradient, 1)
                ),
                self.operand,
                self.gradient,
            ),
            MASK_C,
        )

    def core_part(self, from_core, bit):
        parts = from_core.reshape(2, 2, self.k, 2 * self.n)
        parts = lax.dynamic_slice_in_dim(parts, bit, 1, 1)
        parts = jnp.concatenate([parts[1], parts[0]], axis=0)
        return parts.reshape(2 * self.k, 2 * self.n).astype(FULL)

    def operand_part(self, operand, bit):
        return columns(operand, [(2 * j + bit) * self.k for j in range(2)], self.k)

    def across_x(self, steps):
        x = self.x
        self.from_x = swap(
            steps.do(
                lambda operand, gradient, from_core: (
                    dot_tokens(
                        self.operand_part(operand, 1 - x), self.core_columns(gradient, 0)
                    )
                    + self.core_part(from_core, 1 - x)
                ).astype(LOW),
                self.operand,
                self.gradient,
                self.from_core,
            ),
            MASK_E,
        )

    def side(self, bit, operand, gradient, from_core, from_x):
        return (
            dot_tokens(
                half(self.operand_part(operand, self.x), 1, bit),
                self.core_columns(gradient, 0),
            )
            + half(self.core_part(from_core, self.x), 0, bit)
            + half(from_x, 0, bit).astype(FULL)
        )

    def across_hi(self, steps):
        self.from_hi = swap(
            steps.do(
                lambda *v: self.side(1 - self.at, *v).astype(LOW),
                self.operand,
                self.gradient,
                self.from_core,
                self.from_x,
            ),
            MASK_HI,
        )

    def across_y(self, steps):
        def work(from_hi, *v):
            total = self.side(self.at, *v) + from_hi.astype(FULL)
            return half(total, 1, 1 - self.y).astype(LOW), half(total, 1, self.y)

        given, self.mine = steps.do(
            work, self.from_hi, self.operand, self.gradient, self.from_core, self.from_x
        )
        self.from_y = swap(given, MASK_Y)

    def whole(self, mine, from_y):
        return in_order(self.y, mine, from_y.astype(FULL), 0)


class Spread:
    def __init__(self):
        self.mine, self.theirs = [None] * 4, [None] * 4

    def piece(self, steps, work, *values):
        self.mine[0] = steps.do(work, *values)

    def send_x(self, steps):
        self.mine[2] = swap(steps.wait(self.mine[0]), MASK_E)

    def send_hi(self, steps):
        self.mine[1] = swap(steps.wait(self.mine[0]), MASK_HI)

    def relay(self, steps):
        self.mine[1] = steps.wait(self.mine[1])
        self.mine[3] = swap(self.mine[1], MASK_E)

    def core(self, steps, at):
        self.mine[at] = steps.wait(self.mine[at])
        self.theirs[at] = swap(self.mine[at], MASK_C)


    def pieces(self):
        return [(piece, None) for piece in (*self.mine, *self.theirs)]


GROUPS = [
    [16 * y + 8 * c + 4 * hi + 2 * e + t for c in (0, 1) for hi in (0, 1) for e in (0, 1)]
    for y in (0, 1)
    for t in (0, 1)
]


class Gather:
    def __init__(self, steps, work, *values):
        piece = steps.do(work, *values)
        self.whole = lax.all_gather(piece, ALL, axis=0, tiled=True, axis_index_groups=GROUPS)

    def pieces(self):
        return [(self.whole, 5 + at) for at in range(8)]


QUARTETS = [
    [16 * y + 8 * c + 4 * hi + 2 * e + t for hi in (0, 1) for e in (0, 1)]
    for y in (0, 1)
    for c in (0, 1)
    for t in (0, 1)
]


class Scatter:
    def __init__(self, scalars, operand, gradient, placed):
        self.scalars, self.operand, self.gradient, self.placed = scalars, operand, gradient, placed

    def blocks(self, steps, side, *adds):
        return steps.do(
            lambda *v: scatter_blocks(self.scalars, self.placed, side, *v),
            self.operand,
            self.gradient,
            *adds,
        )

    def core(self, steps):
        self.from_core = swap(self.blocks(steps, 1), MASK_C)

    def send(self, steps):
        self.result = lax.psum_scatter(
            self.blocks(steps, 0, self.from_core),
            ALL,
            scatter_dimension=0,
            tiled=True,
            axis_index_groups=QUARTETS,
        )


def split_pieces(pieces):
    return [array for array, _ in pieces], tuple(base for _, base in pieces)


VMEM_LIMIT = 56 * 2**20


def compiler_params():
    return pltpu.CompilerParams(vmem_limit_bytes=VMEM_LIMIT)


def fixed(shape):
    return pl.BlockSpec(shape, lambda i, *_: (0, 0), pipeline_mode=pl.Buffered(1))


TILE = 256


def join_kernel(*refs):
    at = 0
    for ref in refs[:-1]:
        rows = ref.shape[0]
        refs[-1][at : at + rows, :] = ref[...]
        at += rows


def join_rows(sizes, *parts):
    width = parts[0].shape[1]
    tile = width // 4
    rows = sum(sizes)
    return pl.pallas_call(
        join_kernel,
        grid=(4,),
        in_specs=[pl.BlockSpec((size, tile), lambda i: (0, i)) for size in sizes],
        out_specs=pl.BlockSpec((rows, tile), lambda i: (0, i)),
        out_shape=jax.ShapeDtypeStruct((rows, width), parts[0].dtype),
        compiler_params=compiler_params(),
        cost_estimate=cost(0, 4 * rows * width),
    )(*parts)


def scatter_kernel(scalars, operand, gradient, *refs):
    total = dot_tokens(operand[...], gradient[...])
    for ref in refs[:-1]:
        total = total + ref[...].astype(FULL)
    refs[-1][...] = total.astype(refs[-1].dtype)


def scatter_blocks(scalars, placed, side, operand, gradient, *adds):
    tokens, depth = operand.shape
    block, width = depth // 4, gradient.shape[1] // 2
    out = pl.BlockSpec((block, width), lambda i, s: (s[13 + i], 0))
    return pl.pallas_call(
        scatter_kernel,
        grid_spec=pltpu.PrefetchScalarGridSpec(
            num_scalar_prefetch=1,
            grid=(4,),
            in_specs=[
                pl.BlockSpec((tokens, block), lambda i, s: (0, s[i] if placed else i)),
                pl.BlockSpec(
                    (tokens, width), lambda i, s: (0, side), pipeline_mode=pl.Buffered(1)
                ),
            ]
            + [out] * len(adds),
            out_specs=out,
        ),
        out_shape=jax.ShapeDtypeStruct((4 * block, width), LOW),
        compiler_params=compiler_params(),
        cost_estimate=cost(
            8 * tokens * block * width, 2 * (4 * tokens * block + tokens * width + 8 * block * width)
        ),
    )(scalars, operand, gradient, *adds)


def assemble_kernel(spans, places, *refs):
    step = pl.program_id(0)
    for at, piece in enumerate(refs[:-1]):

        @pl.when(step // spans == at)
        def _(piece=piece):
            refs[-1][...] = piece[...]


def assemble(places, spans, *pieces):
    rows, width = pieces[0].shape
    count = len(pieces)
    block = (rows // spans, width)

    def read(at):
        return pl.BlockSpec(block, lambda i, places: (jnp.clip(i - at * spans, 0, spans - 1), 0))

    return pl.pallas_call(
        functools.partial(assemble_kernel, spans),
        grid_spec=pltpu.PrefetchScalarGridSpec(
            num_scalar_prefetch=1,
            grid=(count * spans,),
            in_specs=[read(at) for at in range(count)],
            out_specs=pl.BlockSpec(block, lambda i, places: (places[i], 0)),
        ),
        out_shape=jax.ShapeDtypeStruct((count * rows, width), pieces[0].dtype),
        compiler_params=compiler_params(),
        cost_estimate=cost(0, count * rows * width * 4),
    )(places, *pieces)


def cost(flops, size, transcendentals=0):
    return pl.CostEstimate(flops=flops, bytes_accessed=size, transcendentals=transcendentals)


def piece_sum(rows, pieces):
    depth = pieces[0].shape[0]
    total = dot(rows[:, :depth], pieces[0][...])
    for at in range(1, len(pieces)):
        total = total + dot(rows[:, at * depth : (at + 1) * depth], pieces[at][...])
    return total


PIECE = 2 * ROWS


def piece_block(rows, width, base, place):
    def index(i, scalars):
        row, column = place(i)
        if base is not None:
            row = row + scalars[base] * (PIECE // rows)
        return (row, column)

    return pl.BlockSpec((rows, width), index)


def piece_tiles(base, side, tiles):
    return piece_block(
        PIECE, TILE, base, lambda i: (0, jnp.clip(i - side * tiles, 0, tiles - 1))
    )


def pieces_kernel(tiles, scalars, rows, *refs):
    for side in range(2):

        @pl.when(pl.program_id(0) // tiles == side)
        def _(side=side):
            refs[8][...] = piece_sum(rows, refs[4 * side : 4 * side + 4])


def product_pieces(bases, scalars, rows, *pieces):
    tokens, depth = rows.shape
    width = pieces[0].shape[1]
    tiles = width // TILE
    return pl.pallas_call(
        functools.partial(pieces_kernel, tiles),
        grid_spec=pltpu.PrefetchScalarGridSpec(
            num_scalar_prefetch=1,
            grid=(2 * tiles,),
            in_specs=[fixed(rows.shape)]
            + [piece_tiles(base, at // 4, tiles) for at, base in enumerate(bases)],
            out_specs=pl.BlockSpec((tokens, TILE), lambda i, *_: (0, i)),
        ),
        out_shape=jax.ShapeDtypeStruct((tokens, 2 * width), FULL),
        compiler_params=compiler_params(),
        cost_estimate=cost(4 * tokens * depth * width, 2 * depth * (tokens + 2 * width)),
    )(scalars, rows, *pieces)


def unit_kernel(tiles, scalars, rows, *refs):
    gate, upper, active = refs[16:]
    for side in range(2):

        @pl.when(pl.program_id(0) // tiles == side)
        def _(side=side):
            a = piece_sum(rows, refs[8 * side : 8 * side + 4])
            b = piece_sum(rows, refs[8 * side + 4 : 8 * side + 8])
            gated = jnp.where(scalars[4] == 0, a, b)
            raised = jnp.where(scalars[4] == 0, b, a)
            gate[...] = gated.astype(LOW)
            upper[...] = raised.astype(LOW)
            active[...] = (gated * jax.nn.sigmoid(gated) * raised).astype(LOW)


def unit_forward(bases, scalars, rows, *pieces):
    tokens, depth = rows.shape
    width = pieces[0].shape[1]
    tiles = width // TILE
    out = pl.BlockSpec((tokens, TILE), lambda i, *_: (0, i))
    shape = jax.ShapeDtypeStruct((tokens, 2 * width), LOW)
    return pl.pallas_call(
        functools.partial(unit_kernel, tiles),
        grid_spec=pltpu.PrefetchScalarGridSpec(
            num_scalar_prefetch=1,
            grid=(2 * tiles,),
            in_specs=[fixed(rows.shape)]
            + [piece_tiles(base, at // 8, tiles) for at, base in enumerate(bases)],
            out_specs=[out, out, out],
        ),
        out_shape=[shape, shape, shape],
        compiler_params=compiler_params(),
        cost_estimate=cost(
            8 * tokens * depth * width, 2 * depth * (tokens + 4 * width) + 12 * tokens * width
        ),
    )(scalars, rows, *pieces)


def unit_back_kernel(scalars, own, other, *refs):
    gate, upper, grad_a, grad_b = refs[8:]
    for at in range(4):

        @pl.when(pl.program_id(0) // 2 == at)
        def _(at=at):
            grad = dot_back(own[...], refs[at][...]) + dot_back(other[...], refs[4 + at][...])
            gated, raised = gate[...].astype(FULL), upper[...].astype(FULL)
            sigmoid = jax.nn.sigmoid(gated)
            gate_grad = grad * raised * sigmoid * (1.0 + gated * (1.0 - sigmoid))
            upper_grad = grad * (gated * sigmoid)
            grad_a[...] = jnp.where(scalars[4] == 0, gate_grad, upper_grad).astype(LOW)
            grad_b[...] = jnp.where(scalars[4] == 0, upper_grad, gate_grad).astype(LOW)


def unit_back(bases, scalars, rows, gate, upper, *pieces):
    tokens, depth = rows.shape
    units = gate.shape[1]
    cut = depth // 2
    shape = jax.ShapeDtypeStruct((tokens, units), LOW)
    out = pl.BlockSpec((tokens, TILE), lambda i, scalars: (0, 2 * scalars[i // 2] + i % 2))

    def half_rows(at):
        return pl.BlockSpec((tokens, cut), lambda i, *_: (0, at), pipeline_mode=pl.Buffered(1))

    def units_of(at, base):
        return piece_block(TILE, cut, base, lambda i: (jnp.clip(i - 2 * (at % 4), 0, 1), 0))

    return pl.pallas_call(
        unit_back_kernel,
        grid_spec=pltpu.PrefetchScalarGridSpec(
            num_scalar_prefetch=1,
            grid=(8,),
            in_specs=[half_rows(0), half_rows(1)] + [units_of(at, base) for at, base in enumerate(bases)] + [out, out],
            out_specs=[out, out],
        ),
        out_shape=[shape, shape],
        compiler_params=compiler_params(),
        cost_estimate=cost(
            2 * tokens * depth * units, 2 * depth * (tokens + units) + 8 * tokens * units
        ),
    )(scalars, rows, rows, *pieces, gate, upper)


def chunk_rows(left, chunk, width, place):
    return pl.BlockSpec(
        (ROWS, width), lambda i, scalars: (chunk, place(scalars)), pipeline_mode=pl.Buffered(1)
    )


def back_kernel(chunks, terms, _, *refs):
    lefts, rights, out = refs[: chunks * terms], refs[chunks * terms : -1], refs[-1]
    for at in range(2):

        @pl.when(pl.program_id(0) // 2 == at)
        def _(at=at):
            for chunk in range(chunks):
                total = dot_back(lefts[chunk * terms][...], rights[at][...])
                for term in range(1, terms):
                    left, right = lefts[chunk * terms + term], rights[2 * term + at]
                    total = total + dot_back(left[...], right[...])
                out[chunk * ROWS : (chunk + 1) * ROWS, :] = total.astype(out.dtype)


def product_back(scalars, chunks, dtype, terms):
    in_specs, values = [], []
    for chunk in chunks:
        for left, at, *_ in terms:
            in_specs.append(chunk_rows(left, chunk, left.shape[1] // 2, lambda s, at=at: at))
            values.append(left)
    depth = 0
    for left, _, *pieces in terms:
        depth += left.shape[1] // 2
        for at, (piece, base) in enumerate(pieces):
            in_specs.append(
                piece_block(
                    TILE,
                    piece.shape[1],
                    base,
                    lambda i, at=at: (jnp.clip(i - 2 * at, 0, 1), 0),
                )
            )
            values.append(piece)
    rows, width = len(chunks) * ROWS, 4 * TILE
    return pl.pallas_call(
        functools.partial(back_kernel, len(chunks), len(terms)),
        grid_spec=pltpu.PrefetchScalarGridSpec(
            num_scalar_prefetch=1,
            grid=(4,),
            in_specs=in_specs,
            out_specs=pl.BlockSpec((rows, TILE), lambda i, *_: (0, i)),
        ),
        out_shape=jax.ShapeDtypeStruct((rows, width), dtype),
        compiler_params=compiler_params(),
        cost_estimate=cost(2 * rows * depth * width, 2 * depth * (rows + width) + 4 * rows * width),
    )(scalars, *values)


def forward_kernel(chunks, _, *refs):
    lefts, rights, out = refs[: chunks * 4], refs[chunks * 4 : -1], refs[-1]
    for chunk in range(chunks):
        total = dot(lefts[4 * chunk][...], rights[0][...])
        for at in range(1, 4):
            total = total + dot(lefts[4 * chunk + at][...], rights[at][...])
        out[chunk * ROWS : (chunk + 1) * ROWS, :] = total.astype(out.dtype)


def product_forward(chunks, dtype, bases, scalars, left, *pieces):
    depth, width = PIECE, pieces[0].shape[1]
    in_specs = [
        chunk_rows(left, chunk, depth, lambda scalars, at=at: scalars[at])
        for chunk in chunks
        for at in range(4)
    ] + [piece_block(PIECE, TILE, base, lambda i: (0, i)) for base in bases]
    rows = len(chunks) * ROWS
    return pl.pallas_call(
        functools.partial(forward_kernel, len(chunks)),
        grid_spec=pltpu.PrefetchScalarGridSpec(
            num_scalar_prefetch=1,
            grid=(width // TILE,),
            in_specs=in_specs,
            out_specs=pl.BlockSpec((rows, TILE), lambda i, *_: (0, i)),
        ),
        out_shape=jax.ShapeDtypeStruct((rows, width), dtype),
        compiler_params=compiler_params(),
        cost_estimate=cost(
            8 * rows * depth * width, 8 * depth * (rows + width) + 4 * rows * width
        ),
    )(scalars, *([left] * (4 * len(chunks))), *pieces)


def signed_tables():
    cosine, sine = rotary_tables(ROWS, HEAD_DIM)
    sign = jnp.concatenate(
        [-jnp.ones((HEAD_DIM // 2,), FULL), jnp.ones((HEAD_DIM // 2,), FULL)]
    )
    return (cosine[:, 0, :], sine[:, 0, :] * sign)


SCALE = HEAD_DIM ** (-0.5)
GROUP_HEADS = 4
GROUP_WIDTH = GROUP_HEADS * HEAD_DIM


def softmax_rows(query, key, allowed):
    scores = dot_back(query, key) * SCALE
    scores = jnp.where(allowed, scores, -1e30)
    weights = jnp.exp(scores - jnp.max(scores, axis=-1, keepdims=True))
    return weights / jnp.sum(weights, axis=-1, keepdims=True)


SIDE_WIDTH = 6 * HEAD_DIM


def head_columns(side, which, head):
    start = side * SIDE_WIDTH + (2 * which + head) * HEAD_DIM
    return slice(start, start + HEAD_DIM)


def mixed_columns(side, head):
    start = (2 * side + head) * HEAD_DIM
    return slice(start, start + HEAD_DIM)


def attend_kernel(projected, mask, cosine, sine, lowered, mixed):
    allowed = mask[...] > 0.0
    cos, sin = cosine[...], sine[...]
    for side in range(2):
        for head in range(2):

            def rope(which):
                values = projected[:, head_columns(side, which, head)]
                return (values * cos + pltpu.roll(values, HEAD_DIM // 2, 1) * sin).astype(LOW)

            query, key = rope(0), rope(1)
            value = projected[:, head_columns(side, 2, head)].astype(LOW)
            probability = softmax_rows(query, key, allowed)
            lowered[:, head_columns(side, 0, head)] = query
            lowered[:, head_columns(side, 1, head)] = key
            lowered[:, head_columns(side, 2, head)] = value
            mixed[:, mixed_columns(side, head)] = dot(probability.astype(LOW), value).astype(LOW)


def attend_back_kernel(lowered, mask, cosine, sine, mixed_grad, projected_grad):
    allowed = mask[...] > 0.0
    cos, sin = cosine[...], sine[...]
    for side in range(2):
        for head in range(2):
            query = lowered[:, head_columns(side, 0, head)]
            key = lowered[:, head_columns(side, 1, head)]
            value = lowered[:, head_columns(side, 2, head)]
            grad = mixed_grad[:, mixed_columns(side, head)]
            probability = softmax_rows(query, key, allowed)
            prob_grad = dot_back(grad, value)
            inner = jnp.sum(probability * prob_grad, axis=-1, keepdims=True)
            score_grad = (probability * (prob_grad - inner)).astype(LOW)
            query_grad = dot(score_grad, key) * SCALE
            key_grad = dot_tokens(score_grad, query) * SCALE
            value_grad = dot_tokens(probability.astype(LOW), grad)

            def unrope(values):
                return (values * cos - pltpu.roll(values, HEAD_DIM // 2, 1) * sin).astype(LOW)

            projected_grad[:, head_columns(side, 0, head)] = unrope(query_grad)
            projected_grad[:, head_columns(side, 1, head)] = unrope(key_grad)
            projected_grad[:, head_columns(side, 2, head)] = value_grad.astype(LOW)


def row_block(width):
    return pl.BlockSpec((ROWS, width), lambda i: (i, 0))


def whole_block(width):
    return pl.BlockSpec((ROWS, width), lambda i: (0, 0))


def attend(projected, mask, cosine, sine):
    rows = projected.shape[0]
    return pl.pallas_call(
        attend_kernel,
        grid=(rows // ROWS,),
        in_specs=[
            row_block(2 * SIDE_WIDTH),
            row_block(ROWS),
            whole_block(HEAD_DIM),
            whole_block(HEAD_DIM),
        ],
        out_specs=[row_block(2 * SIDE_WIDTH), row_block(GROUP_WIDTH)],
        out_shape=[
            jax.ShapeDtypeStruct((rows, 2 * SIDE_WIDTH), LOW),
            jax.ShapeDtypeStruct((rows, GROUP_WIDTH), LOW),
        ],
        compiler_params=compiler_params(),
        cost_estimate=cost(
            4 * rows * ROWS * GROUP_WIDTH, rows * GROUP_WIDTH * 20, rows * ROWS * GROUP_HEADS
        ),
    )(projected, mask, cosine, sine)


def attend_back(lowered, mask, cosine, sine, mixed_grad):
    rows = lowered.shape[0]
    return pl.pallas_call(
        attend_back_kernel,
        grid=(rows // ROWS,),
        in_specs=[
            row_block(2 * SIDE_WIDTH),
            row_block(ROWS),
            whole_block(HEAD_DIM),
            whole_block(HEAD_DIM),
            row_block(GROUP_WIDTH),
        ],
        out_specs=row_block(2 * SIDE_WIDTH),
        out_shape=jax.ShapeDtypeStruct((rows, 2 * SIDE_WIDTH), LOW),
        compiler_params=compiler_params(),
        cost_estimate=cost(
            10 * rows * ROWS * GROUP_WIDTH, rows * GROUP_WIDTH * 14, rows * ROWS * GROUP_HEADS
        ),
    )(lowered, mask, cosine, sine, mixed_grad)


def split_layer(
    inputs,
    cotangent,
    segment_ids,
    master_qkv,
    master_out,
    master_in,
    master_down,
    first_qkv,
    first_out,
    first_in,
    first_down,
    second_qkv,
    second_out,
    second_in,
    second_down,
):
    rep, fsdp = lax.axis_index("rep"), lax.axis_index("fsdp")
    y, c = rep // 2, rep % 2
    hi, e, t = fsdp // 4, (fsdp // 2) % 2, fsdp % 2
    width = inputs.shape[1]
    middle = width // 2
    unit = width // 4
    pair = 2 * HEAD_DIM
    pairs = master_qkv.shape[1] // pair
    block = pairs * HEAD_DIM
    steps = Steps()

    def relative(values):
        starts = [
            4 * (hi ^ at_hi) + 2 * (e ^ at_e) + at_t
            for at_e in (0, 1)
            for at_hi in (0, 1)
            for at_t in (0, 1)
        ]
        return columns(values, [start * ROWS for start in starts], ROWS)

    def natural(values):
        starts = [
            4 * (e ^ at_e) + 2 * (hi ^ at_hi) + at_t
            for at_hi in (0, 1)
            for at_e in (0, 1)
            for at_t in (0, 1)
        ]
        return columns(values, [start * ROWS for start in starts], ROWS)

    def core_first(values):
        return columns(values, [c * unit, (2 + c) * unit, (1 - c) * unit, (3 - c) * unit], unit)

    def core_natural(own, other):
        even, odd = jnp.where(c == 0, own, other), jnp.where(c == 0, other, own)
        return jnp.concatenate(
            [even[:, :unit], odd[:, :unit], even[:, unit:], odd[:, unit:]], axis=1
        )

    places = [2 * ((hi ^ at_hi) ^ c) + (e ^ at_e) for at_e in (0, 1) for at_hi in (0, 1)]
    numbers = [
        4 * (c ^ at_c) + 2 * (hi ^ at_hi) + (e ^ at_e)
        for at_c in (0, 1)
        for at_e in (0, 1)
        for at_hi in (0, 1)
    ]
    fourths = [2 * (hi ^ at_hi) + (e ^ at_e) for at_e in (0, 1) for at_hi in (0, 1)]
    scalars = jnp.stack([*places, y, *numbers, *fourths]).astype(jnp.int32)

    def in_rows(mine, other):
        return in_order(t, mine, other, 0)

    def in_columns(mine, other):
        return in_order(y, mine, other, 1)

    def split_pairs(weight):
        low = weight.astype(LOW)
        return (
            columns(low, [j * pair + (1 - y) * HEAD_DIM for j in range(pairs)], HEAD_DIM),
            columns(low, [j * pair + y * HEAD_DIM for j in range(pairs)], HEAD_DIM),
        )

    def all_pairs(mine, theirs):
        even, odd = jnp.where(c == 0, mine, theirs), jnp.where(c == 0, theirs, mine)
        whole = jnp.concatenate(
            [even[:, :block], odd[:, :block], even[:, block:], odd[:, block:]], axis=1
        )

        def part(t_bit):
            starts = [8 * j + 4 * c + 2 * k + t_bit for j in range(3) for k in range(2)]
            return columns(whole, [start * HEAD_DIM for start in starts], HEAD_DIM)

        return part(1 - t), part(t)

    def split_rows(weight):
        low = weight.astype(LOW)
        return half(low, 0, 1 - y), half(low, 0, y)

    def unit_columns(low, t_bit, y_bit):
        return columns(low, [(4 * j + 2 * t_bit + y_bit) * unit for j in range(2)], unit)

    def split_in(weight):
        low = weight.astype(LOW)
        return (
            unit_columns(low, 1 - t, y),
            unit_columns(low, t, y),
            jnp.concatenate(
                [unit_columns(low, 1 - t, 1 - y), unit_columns(low, t, 1 - y)], axis=1
            ),
        )

    def norm_low(values, ids):
        normed, inverse = normalize(values.astype(FULL))
        extra = jnp.tile(ids.astype(LOW), (16, width // ROWS))
        return jnp.concatenate([relative(normed.astype(LOW)), extra], axis=0), inverse

    given, kept = steps.do(split_pairs, master_qkv)
    pairs_y = swap(given, MASK_Y)
    lowered_one, inverse_one = steps.do(norm_low, inputs, segment_ids)
    given, out_kept = steps.do(split_rows, master_out)
    pairs_mine = steps.do(in_columns, kept, pairs_y)
    pairs_core = swap(pairs_mine, MASK_C)
    out_y = swap(given, MASK_Y)
    give_t, in_kept, give_y = steps.do(split_in, master_in)
    given, pairs_kept = steps.do(all_pairs, pairs_mine, pairs_core)
    pairs_t = swap(given, MASK_T)
    give_down, down_kept = steps.do(split_rows, master_down)
    out_y = steps.wait(out_y)

    qkv, out = Spread(), Spread()
    qkv.piece(steps, in_rows, pairs_kept, pairs_t)
    qkv.send_hi(steps)
    qkv.send_x(steps)
    in_t = swap(steps.wait(give_t), MASK_T)
    tokens_one = Tokens(lowered_one)
    tokens_one.send_y(steps)
    out.piece(steps, in_columns, out_kept, out_y)
    in_t = steps.wait(in_t)
    tokens_one.send_t(steps)
    qkv.core(steps, 0)
    qkv.core(steps, 2)
    out.send_x(steps)
    tokens_one.from_y = steps.wait(tokens_one.from_y)
    in_y = swap(steps.wait(give_y), MASK_Y)
    qkv.relay(steps)
    a = Gather(steps, in_rows, in_kept, in_t)
    out.send_hi(steps)
    tokens_one.second(steps)
    qkv.core(steps, 1)
    out.mine[1] = steps.wait(out.mine[1])
    qkv.core(steps, 3)
    out.relay(steps)
    in_y = steps.wait(in_y)
    in_b_t = swap(steps.do(lambda v: v[:, :middle], in_y), MASK_T)
    rows_one = tokens_one.rows(steps)
    down_y = swap(steps.wait(give_down), MASK_Y)

    def attention_mask(own, from_y, from_t, upper):
        segments = jnp.stack(
            [own[ROWS], from_y[ROWS], upper[ROWS // 2], from_t[ROWS]], axis=0
        )[:, :ROWS]
        at = jnp.arange(ROWS)
        allowed = (segments[:, :, None] == segments[:, None, :]) & (at[None, :] <= at[:, None])
        return allowed.astype(FULL).reshape(4 * ROWS, ROWS)

    mask = steps.do(
        attention_mask, tokens_one.values, tokens_one.from_y, tokens_one.from_t, tokens_one.upper
    )
    cosine, sine = signed_tables()
    b = Gather(steps, lambda v, other: in_rows(v[:, middle:], other), in_y, in_b_t)
    down = Gather(steps, in_columns, down_kept, down_y)
    qkv_pieces, qkv_bases = split_pieces(qkv.pieces())
    projected = steps.do(
        functools.partial(product_pieces, qkv_bases, scalars), rows_one, *qkv_pieces
    )
    out_mine = steps.do(lambda *parts: assemble(scalars, 1, *parts), *out.mine)
    out_theirs = swap(out_mine, MASK_C)
    lowered, mixed_low = steps.do(attend, projected, mask, cosine, sine)

    def both_cores(mine, theirs):
        cut = mine.shape[0] // 2
        theirs = jnp.concatenate([theirs[cut:], theirs[:cut]], axis=0)
        return jnp.concatenate([mine, theirs], axis=1)

    weight_out = steps.do(both_cores, out_mine, out_theirs)

    def product_out(chunks, side, dtype, operand, weight):
        right = weight[:, side * middle : (side + 1) * middle]
        if chunks[0] + 1 == chunks[1]:
            left = operand[chunks[0] * ROWS : (chunks[1] + 1) * ROWS]
            return dot(left, right).astype(dtype)
        parts = [dot(operand[at * ROWS : (at + 1) * ROWS], right) for at in chunks]
        return jnp.concatenate(parts, axis=0).astype(dtype)

    sum_out = Sum(product_out, mixed_low, weight_out)
    sum_out.first(steps)
    sum_out.send()
    sum_out.own(steps)
    sum_out.second(steps)

    def norm_stream(values, *parts):
        stream = values.astype(FULL) + core_natural(*sum_out.total(*parts))
        normed, inverse = normalize(stream)
        return relative(normed.astype(LOW)), stream, inverse

    lowered_two, stream, inverse_two = steps.do(norm_stream, inputs, *sum_out.parts())
    tokens_two = Tokens(lowered_two)
    tokens_two.send(steps)
    tokens_two.second(steps)
    rows_two = tokens_two.rows(steps)
    tokens_cotangent = Tokens(steps.do(core_first, cotangent))
    tokens_cotangent.send(steps)

    pieces_a, pieces_b = a.pieces(), b.pieces()
    in_pieces, in_bases = split_pieces(
        [*pieces_a[:4], *pieces_b[:4], *pieces_a[4:], *pieces_b[4:]]
    )
    gate, upper, active = steps.do(
        functools.partial(unit_forward, in_bases, scalars), rows_two, *in_pieces
    )
    tokens_cotangent.second(steps)
    rows_cotangent = tokens_cotangent.rows(steps)
    scatter_down = Scatter(scalars, active, rows_cotangent, True)
    scatter_down.core(steps)
    down_pieces, down_bases = split_pieces(down.pieces())

    grad_a, grad_b = steps.do(
        functools.partial(unit_back, down_bases, scalars), rows_cotangent, gate, upper, *down_pieces
    )

    def product_units(chunks, side, dtype, grad_a, grad_b, *arrays):
        at = slice(2 * side, 2 * side + 2)
        pieces = list(zip(arrays, in_bases))
        return product_back(
            scalars,
            chunks,
            dtype,
            [
                (grad_a, 0, *pieces[0:4][at]),
                (grad_b, 0, *pieces[4:8][at]),
                (grad_a, 1, *pieces[8:12][at]),
                (grad_b, 1, *pieces[12:16][at]),
            ],
        )

    sum_two = Sum(product_units, grad_a, grad_b, *in_pieces)
    sum_two.first(steps)
    sum_two.send()
    scatter_down.send(steps)
    scatter_a = Scatter(scalars, rows_two, grad_a, False)
    scatter_a.core(steps)
    sum_two.own(steps)
    sum_two.second(steps)
    scatter_b = Scatter(scalars, rows_two, grad_b, False)
    scatter_b.core(steps)
    scatter_a.send(steps)

    def stream_back(grad, stream, inverse, *parts):
        normed = (stream - jnp.mean(stream, axis=-1, keepdims=True)) * inverse
        total = natural(jnp.concatenate(sum_two.total(*parts), axis=1))
        result = grad.astype(FULL) + norm_back(normed, inverse, total)
        return core_first(result.astype(LOW)), result

    stream_grad_low, stream_grad = steps.do(
        stream_back, cotangent, stream, inverse_two, *sum_two.parts()
    )
    tokens_stream = Tokens(stream_grad_low)
    tokens_stream.send(steps)
    scatter_b.send(steps)

    def product_final(chunks, side, dtype, active, *pieces):
        at = slice(4 * side, 4 * side + 4)
        return product_forward(chunks, dtype, down_bases[at], scalars, active, *pieces[at])

    sum_final = Sum(product_final, active, *down_pieces)
    sum_final.first(steps)
    tokens_stream.second(steps)
    sum_final.own(steps)
    rows_stream = tokens_stream.rows(steps)
    sum_final.release(steps)
    sum_final.send()

    mixed_grad = steps.do(
        lambda rows, weight: dot_back(rows, weight).astype(LOW), rows_stream, weight_out
    )
    projected_grad = steps.do(attend_back, lowered, mask, cosine, sine, mixed_grad)
    sum_qkv = RowSum(
        rows_one, projected_grad[:, : 3 * pair], projected_grad[:, 3 * pair :]
    )
    sum_qkv.core(steps)

    def product_qkv(chunks, side, dtype, gradient, *pieces):
        at = slice(2 * side, 2 * side + 2)
        pieces = [(piece, None) for piece in pieces]
        terms = [(gradient, 0, *pieces[:4][at]), (gradient, 1, *pieces[4:][at])]
        return product_back(scalars, chunks, dtype, terms)

    sum_one = Sum(product_qkv, projected_grad, *qkv.mine, *qkv.theirs)
    sum_one.first(steps)
    sum_final.second(steps)
    sum_weight_out = ColumnSum(mixed_low, rows_stream, c, e, hi, y)
    sum_weight_out.core(steps)
    sum_qkv.across_x(steps)
    sum_one.own(steps)

    def output_of(stream, *parts):
        final = stream + core_natural(*sum_final.total(*parts))
        squares = jnp.stack([jnp.sum(stream * stream), jnp.sum(final * final)]).reshape(1, 2)
        return final.astype(LOW), squares

    output, squares = steps.do(output_of, stream, *sum_final.parts())
    sum_one.release(steps)
    sum_one.send()
    sum_weight_out.across_x(steps)

    sum_one.second(steps)

    sum_qkv.across_hi(steps)

    def input_back(values, inverse, grad, *parts):
        source = values.astype(FULL)
        normed = (source - jnp.mean(source, axis=-1, keepdims=True)) * inverse
        total = natural(jnp.concatenate(sum_one.total(*parts), axis=1))
        return (grad + norm_back(normed, inverse, total)).astype(LOW)

    input_grad = steps.do(input_back, inputs, inverse_one, stream_grad, *sum_one.parts())

    give_down, mine_down = steps.do(
        lambda v: (half(v, 1, 1 - y), half(v, 1, y)), scatter_down.result
    )
    down_y = swap(give_down, MASK_Y)
    given, in_mine = steps.do(
        lambda v: (half(v, 0, 1 - t), half(v, 0, t)), scatter_a.result
    )
    from_t = swap(given, MASK_T)
    given_y, given_both = steps.do(
        lambda v: (half(v, 0, t), half(v, 0, 1 - t)), scatter_b.result
    )
    from_y = swap(given_y, MASK_Y)

    def adam_down(mine, got, *state):
        gradient = in_order(y, mine, got, 0).astype(FULL)
        return (gradient, *adam_step(state[0], gradient, *state[1:], rate))

    step_down = steps.do(adam_down, mine_down, down_y, master_down, first_down, second_down)
    from_t = steps.wait(from_t)
    from_both = swap(steps.wait(given_both), MASK_Y | MASK_T)
    for bit in (MASK_E, MASK_T, MASK_HI, MASK_C, MASK_Y):
        squares = steps.do(jnp.add, squares, swap(squares, bit))
    stream_rms = jnp.sqrt(squares[0] / (ROWS * width * DEVICES))

    def adam_in(mine, from_t, from_y, from_both, *state):
        sides = []
        for bit in range(2):
            same = jnp.where(t == bit, mine, from_t).astype(FULL)
            cross = jnp.where(t == bit, from_y, from_both).astype(FULL)
            sides.append((jnp.where(y == 0, same, cross), jnp.where(y == 0, cross, same)))
        blocks = [
            part[:, j * unit : (j + 1) * unit] for j in range(2) for side in sides for part in side
        ]
        gradient = jnp.concatenate(blocks, axis=1)
        return (gradient, *adam_step(state[0], gradient, *state[1:], rate))

    step_in = steps.do(
        adam_in, in_mine, from_t, from_y, from_both, master_in, first_in, second_in
    )
    sum_weight_out.across_hi(steps)

    def finish_qkv(*parts):
        total = sum_qkv.total(*parts).astype(LOW)
        return half(total, 0, 1 - t), half(total, 0, t)

    given, kept = steps.do(finish_qkv, *sum_qkv.parts())
    pairs_t = swap(given, MASK_T)

    def core_pairs(kept, got):
        even, odd = jnp.where(t == 0, kept, got), jnp.where(t == 0, got, kept)
        return jnp.concatenate(
            [
                part[:, j * HEAD_DIM : (j + 1) * HEAD_DIM]
                for j in range(6)
                for part in (even, odd)
            ],
            axis=1,
        )

    pairs_mine = steps.do(core_pairs, kept, pairs_t)
    pairs_core = swap(pairs_mine, MASK_C)
    sum_weight_out.across_y(steps)

    def split_grad(mine, theirs):
        even, odd = jnp.where(c == 0, mine, theirs), jnp.where(c == 0, theirs, mine)
        whole = jnp.concatenate(
            [
                part[:, j * 2 * pair : (j + 1) * 2 * pair]
                for j in range(3)
                for part in (even, odd)
            ],
            axis=1,
        )
        return (
            lax.dynamic_slice_in_dim(whole, (2 * (1 - y) + c) * block, block, 1),
            lax.dynamic_slice_in_dim(whole, (2 * y + c) * block, block, 1),
        )

    given, kept = steps.do(split_grad, pairs_mine, pairs_core)
    pairs_y = swap(given, MASK_Y)

    def adam_out(mine, from_y, *state):
        gradient = sum_weight_out.whole(mine, from_y)
        return (gradient, *adam_step(state[0], gradient, *state[1:], rate_out))

    step_out = steps.do(
        adam_out,
        sum_weight_out.mine,
        sum_weight_out.from_y,
        master_out,
        first_out,
        second_out,
    )

    def adam_qkv(mine, got, *state):
        even, odd = jnp.where(y == 0, mine, got), jnp.where(y == 0, got, mine)
        gradient = jnp.concatenate(
            [
                part[:, j * HEAD_DIM : (j + 1) * HEAD_DIM]
                for j in range(pairs)
                for part in (even, odd)
            ],
            axis=1,
        ).astype(FULL)
        return (gradient, *adam_step(state[0], gradient, *state[1:], rate))

    step_qkv = steps.do(adam_qkv, kept, pairs_y, master_qkv, first_qkv, second_qkv)
    results = zip(step_qkv, step_out, step_in, step_down)
    grads, updated, moments, variances, narrows = results
    return (output, input_grad, *grads, *updated, *moments, *variances, *narrows, stream_rms)


def solution(mesh):
    shards = split_layer if tuple(mesh.shape.values()) == (4, 8) else gathered_layer
    return jax.shard_map(
        shards,
        mesh=mesh,
        in_specs=(
            P(("rep", "fsdp"), None),
            P(("rep", "fsdp"), None),
            P(("rep", "fsdp"), None),
            P("fsdp", "rep"),
            P("fsdp", "rep"),
            P("fsdp", "rep"),
            P("fsdp", "rep"),
            P("fsdp", "rep"),
            P("fsdp", "rep"),
            P("fsdp", "rep"),
            P("fsdp", "rep"),
            P("fsdp", "rep"),
            P("fsdp", "rep"),
            P("fsdp", "rep"),
            P("fsdp", "rep"),
        ),
        out_specs=(
            P(("rep", "fsdp"), None),
            P(("rep", "fsdp"), None),
            P("fsdp", "rep"),
            P("fsdp", "rep"),
            P("fsdp", "rep"),
            P("fsdp", "rep"),
            P("fsdp", "rep"),
            P("fsdp", "rep"),
            P("fsdp", "rep"),
            P("fsdp", "rep"),
            P("fsdp", "rep"),
            P("fsdp", "rep"),
            P("fsdp", "rep"),
            P("fsdp", "rep"),
            P("fsdp", "rep"),
            P("fsdp", "rep"),
            P("fsdp", "rep"),
            P("fsdp", "rep"),
            P("fsdp", "rep"),
            P("fsdp", "rep"),
            P("fsdp", "rep"),
            P("fsdp", "rep"),
            P(),
        ),
        check_vma=False,
    )
```

```python
import functools

import jax
import jax.numpy as jnp
import numpy as np
from jax import lax
from jax.experimental import pallas as pl
from jax.experimental.pallas import tpu as pltpu
from jax.sharding import PartitionSpec as P

HEADS = 16
HEAD_DIM = 128
STEP = 10


beta_one = 0.9
beta_two = 0.95
rate = 0.02
rate_out = 0.08
decay = 0.1
epsilon = 1e-08


def normalize(values):
    centered = values - jnp.mean(values, axis=-1, keepdims=True)
    inverse = lax.rsqrt(jnp.mean(centered * centered, axis=-1, keepdims=True) + 1e-05)
    return (centered * inverse, inverse)


def norm_back(normed, inverse, gradient):
    first = jnp.mean(gradient, axis=-1, keepdims=True)
    second = jnp.mean(gradient * normed, axis=-1, keepdims=True)
    return inverse * (gradient - first - normed * second)


def rotate(values):
    half = values.shape[-1] // 2
    return jnp.concatenate([-values[..., half:], values[..., :half]], axis=-1)


def rotate_back(values):
    half = values.shape[-1] // 2
    return jnp.concatenate([values[..., half:], -values[..., :half]], axis=-1)


def rotary_tables(length, size):
    half = size // 2
    freqs = 10000.0 ** (-(jnp.arange(half, dtype=jnp.float32) * 2.0) / size)
    angles = jnp.arange(length, dtype=jnp.float32)[:, None] * freqs[None, :]
    cosine = jnp.concatenate([jnp.cos(angles), jnp.cos(angles)], axis=-1)[:, None, :]
    sine = jnp.concatenate([jnp.sin(angles), jnp.sin(angles)], axis=-1)[:, None, :]
    return (cosine, sine)


def group_gradient(operand, gradient):
    return lax.psum_scatter(
        lax.dot_general(
            operand, gradient, (((0,), (0,)), ((), ())), preferred_element_type=jnp.float32
        ).astype(jnp.bfloat16),
        "fsdp",
        scatter_dimension=0,
        tiled=True,
    ).astype(jnp.float32)


def adam_step(master, gradient, first, second, step_rate):
    moment = beta_one * first + (1.0 - beta_one) * gradient
    variance = beta_two * second + (1.0 - beta_two) * gradient * gradient
    update = (
        moment / (1.0 - beta_one**STEP) / (jnp.sqrt(variance / (1.0 - beta_two**STEP)) + epsilon)
    )
    updated = master - step_rate * (update + decay * master)
    return (updated, moment, variance, updated.astype(jnp.bfloat16))


def gathered_layer(
    inputs,
    cotangent,
    segment_ids,
    master_qkv,
    master_out,
    master_in,
    master_down,
    first_qkv,
    first_out,
    first_in,
    first_down,
    second_qkv,
    second_out,
    second_in,
    second_down,
):
    copies = (
        lax.all_gather(master_qkv.astype(jnp.bfloat16), "rep", axis=1, tiled=True),
        lax.all_gather(master_out.astype(jnp.bfloat16), "rep", axis=1, tiled=True),
        lax.all_gather(master_in.astype(jnp.bfloat16), "rep", axis=1, tiled=True),
        lax.all_gather(master_down.astype(jnp.bfloat16), "rep", axis=1, tiled=True),
    )

    def forward_product(operand, number):
        portion = copies[number]
        return jnp.dot(
            operand,
            lax.all_gather(portion, "fsdp", axis=0, tiled=True),
            preferred_element_type=jnp.float32,
        )

    def backward_product(gradient, number):
        return lax.dot_general(
            gradient,
            lax.all_gather(copies[number], "fsdp", axis=0, tiled=True),
            (((1,), (1,)), ((), ())),
            preferred_element_type=jnp.float32,
        )

    def weight_gradient(operand, gradient):
        return group_gradient(operand, gradient)

    length = inputs.shape[0]
    width = inputs.shape[1]
    scale = HEAD_DIM ** (-0.5)
    cosine, sine = rotary_tables(length, HEAD_DIM)
    segments = segment_ids[0]
    places = jnp.arange(length)
    allowed = (segments[:, None] == segments[None, :]) & (places[None, :] <= places[:, None])
    source = inputs.astype(jnp.float32)
    normed_one, inverse_one = normalize(source)
    lowered_one = normed_one.astype(jnp.bfloat16)
    projected = forward_product(lowered_one, 0)
    queries = projected[:, :width].reshape(length, HEADS, HEAD_DIM)
    keys = projected[:, width : 2 * width].reshape(length, HEADS, HEAD_DIM)
    values = projected[:, 2 * width :].reshape(length, HEADS, HEAD_DIM).astype(jnp.bfloat16)
    queries = (queries * cosine + rotate(queries) * sine).astype(jnp.bfloat16)
    keys = (keys * cosine + rotate(keys) * sine).astype(jnp.bfloat16)
    scores = jnp.einsum("shd,thd->hst", queries, keys, preferred_element_type=jnp.float32) * scale
    scores = jnp.where(allowed[None], scores, -1e30)
    probability = jax.nn.softmax(scores, axis=-1)
    prob_low = probability.astype(jnp.bfloat16)
    mixed = jnp.einsum("hst,thd->shd", prob_low, values, preferred_element_type=jnp.float32)
    mixed_low = mixed.reshape(length, width).astype(jnp.bfloat16)
    stream = source + forward_product(mixed_low, 1)
    normed_two, inverse_two = normalize(stream)
    lowered_two = normed_two.astype(jnp.bfloat16)
    gate_up = forward_product(lowered_two, 2)
    hidden = gate_up.shape[1] // 2
    gate = gate_up[:, :hidden]
    upper = gate_up[:, hidden:]
    sigmoid_gate = jax.nn.sigmoid(gate)
    silu_gate = gate * sigmoid_gate
    active_low = (silu_gate * upper).astype(jnp.bfloat16)
    final = stream + forward_product(active_low, 3)
    output = final.astype(jnp.bfloat16)
    summed_squares = lax.psum((jnp.sum(stream * stream), jnp.sum(final * final)), ("rep", "fsdp"))
    entries = length * width * lax.axis_size("rep") * lax.axis_size("fsdp")
    stream_rms = jnp.sqrt(jnp.stack(summed_squares) / entries)
    grad_down = weight_gradient(active_low, cotangent)
    active_grad = backward_product(cotangent, 3)
    gate_grad = active_grad * upper * sigmoid_gate * (1.0 + gate * (1.0 - sigmoid_gate))
    upper_grad = active_grad * silu_gate
    gate_up_grad = jnp.concatenate([gate_grad, upper_grad], axis=1).astype(jnp.bfloat16)
    grad_in = weight_gradient(lowered_two, gate_up_grad)
    lowered_two_grad = backward_product(gate_up_grad, 2)
    stream_grad = cotangent.astype(jnp.float32) + norm_back(
        normed_two, inverse_two, lowered_two_grad
    )
    stream_grad_low = stream_grad.astype(jnp.bfloat16)
    grad_out = weight_gradient(mixed_low, stream_grad_low)
    mixed_grad = backward_product(stream_grad_low, 1)
    mixed_grad_low = mixed_grad.reshape(length, HEADS, HEAD_DIM).astype(jnp.bfloat16)
    prob_grad = jnp.einsum(
        "shd,thd->hst", mixed_grad_low, values, preferred_element_type=jnp.float32
    )
    score_grad = probability * (
        prob_grad - jnp.sum(probability * prob_grad, axis=-1, keepdims=True)
    )
    score_grad_low = score_grad.astype(jnp.bfloat16)
    query_grad = (
        jnp.einsum("hst,thd->shd", score_grad_low, keys, preferred_element_type=jnp.float32) * scale
    )
    key_grad = (
        jnp.einsum("hst,shd->thd", score_grad_low, queries, preferred_element_type=jnp.float32)
        * scale
    )
    value_grad = jnp.einsum(
        "hst,shd->thd", prob_low, mixed_grad_low, preferred_element_type=jnp.float32
    )
    query_grad = query_grad * cosine + rotate_back(query_grad * sine)
    key_grad = key_grad * cosine + rotate_back(key_grad * sine)
    projected_grad = jnp.concatenate(
        [
            query_grad.reshape(length, width),
            key_grad.reshape(length, width),
            value_grad.reshape(length, width),
        ],
        axis=1,
    ).astype(jnp.bfloat16)
    grad_qkv = weight_gradient(lowered_one, projected_grad)
    lowered_one_grad = backward_product(projected_grad, 0)
    input_grad = (stream_grad + norm_back(normed_one, inverse_one, lowered_one_grad)).astype(
        jnp.bfloat16
    )
    summed = (
        lax.psum(grad_qkv.astype(jnp.bfloat16), "rep").astype(jnp.float32),
        lax.psum(grad_out.astype(jnp.bfloat16), "rep").astype(jnp.float32),
        lax.psum(grad_in.astype(jnp.bfloat16), "rep").astype(jnp.float32),
        lax.psum(grad_down.astype(jnp.bfloat16), "rep").astype(jnp.float32),
    )
    group = lax.axis_index("rep")
    reduced = tuple(
        (
            lax.dynamic_slice_in_dim(
                full,
                group * (full.shape[1] // lax.axis_size("rep")),
                full.shape[1] // lax.axis_size("rep"),
                1,
            )
            for full in summed
        )
    )
    updated_qkv, moment_qkv, variance_qkv, narrow_qkv = adam_step(
        master_qkv, reduced[0], first_qkv, second_qkv, rate
    )
    updated_out, moment_out, variance_out, narrow_out = adam_step(
        master_out, reduced[1], first_out, second_out, rate_out
    )
    updated_in, moment_in, variance_in, narrow_in = adam_step(
        master_in, reduced[2], first_in, second_in, rate
    )
    updated_down, moment_down, variance_down, narrow_down = adam_step(
        master_down, reduced[3], first_down, second_down, rate
    )
    return (
        output,
        input_grad,
        reduced[0],
        reduced[1],
        reduced[2],
        reduced[3],
        updated_qkv,
        updated_out,
        updated_in,
        updated_down,
        moment_qkv,
        moment_out,
        moment_in,
        moment_down,
        variance_qkv,
        variance_out,
        variance_in,
        variance_down,
        narrow_qkv,
        narrow_out,
        narrow_in,
        narrow_down,
        stream_rms,
    )


ALL = ("rep", "fsdp")
MASK_Y, MASK_C, MASK_HI, MASK_E, MASK_T = 16, 8, 4, 2, 1
DEVICES = 32
ROWS = 256
FULL = jnp.float32
LOW = jnp.bfloat16


def swap(values, mask):
    return lax.ppermute(values, ALL, [(i, i ^ mask) for i in range(DEVICES)])


def half(values, axis, bit):
    size = values.shape[axis] // 2
    return lax.dynamic_slice_in_dim(values, bit * size, size, axis)


class Steps:
    def __init__(self):
        self.last = ()

    def do(self, work, *values):
        values, _ = lax.optimization_barrier((values, self.last))
        result = work(*values)
        self.last = (jax.tree.leaves(result)[0],)
        return result

    def wait(self, value):
        return self.do(lambda v: v, value)


def columns(values, starts, width):
    return jnp.concatenate(
        [lax.dynamic_slice_in_dim(values, start, width, 1) for start in starts], axis=1
    )


def in_order(bit, mine, other, axis):
    first = jnp.where(bit == 0, mine, other)
    second = jnp.where(bit == 0, other, mine)
    return jnp.concatenate([first, second], axis=axis)


def dot(left, right):
    return jnp.dot(left, right, preferred_element_type=FULL)


def dot_back(left, right):
    return lax.dot_general(left, right, (((1,), (1,)), ((), ())), preferred_element_type=FULL)


def dot_tokens(left, right):
    return lax.dot_general(left, right, (((0,), (0,)), ((), ())), preferred_element_type=FULL)


def low_dot_tokens(left, right):
    return dot_tokens(left, right).astype(LOW)


class Tokens:
    def __init__(self, values):
        self.values = values

    def send_y(self, steps):
        self.from_y = swap(steps.wait(self.values), MASK_Y)

    def send_t(self, steps):
        self.from_t = swap(steps.wait(self.values), MASK_T)

    def send(self, steps):
        self.values = steps.wait(self.values)
        self.from_y = swap(self.values, MASK_Y)
        self.from_t = swap(self.values, MASK_T)

    def second(self, steps):
        cut = ROWS // 2

        def parts(from_t, from_y):
            upper = from_t[:cut]
            if from_t.shape[0] > ROWS:
                upper = jnp.concatenate([upper, from_t[ROWS:]], axis=0)
            return upper, from_y[cut:ROWS]

        upper, lower = steps.do(parts, self.from_t, self.from_y)
        self.upper = swap(upper, MASK_Y)
        self.lower = swap(lower, MASK_T)

    def rows(self, steps):
        cut = ROWS // 2
        return steps.do(
            functools.partial(join_rows, (ROWS, ROWS, cut, cut, ROWS)),
            self.values,
            self.from_y,
            self.upper,
            self.lower,
            self.from_t,
        )


class Sum:
    def __init__(self, product, *values):
        self.product = product
        self.values = values

    def first(self, steps):
        self.give_y, self.give_t = steps.do(
            lambda *v: (self.product((1, 2), 0, LOW, *v), self.product((2, 3), 1, LOW, *v)),
            *self.values,
        )

    def release(self, steps):
        self.give_y, self.give_t = steps.do(lambda *v: v, self.give_y, self.give_t)

    def send(self):
        self.got_y = swap(self.give_y, MASK_Y)
        self.got_t = swap(self.give_t, MASK_T)

    def own(self, steps):
        self.mine = steps.do(
            lambda *v: (self.product((0, 3), 0, FULL, *v), self.product((0, 1), 1, FULL, *v)),
            *self.values,
        )

    def second(self, steps):
        give_t, give_y = steps.do(
            lambda got_y, got_t, side_0, side_1: (
                (side_0[ROWS:] + got_y[ROWS:].astype(FULL)).astype(LOW),
                (side_1[ROWS:] + got_t[:ROWS].astype(FULL)).astype(LOW),
            ),
            self.got_y,
            self.got_t,
            *self.mine,
        )
        self.last_t = swap(give_t, MASK_T)
        self.last_y = swap(give_y, MASK_Y)

    def total(self, side_0, side_1, got_y, got_t, last_t, last_y):
        return (
            side_0[:ROWS] + got_y[:ROWS].astype(FULL) + last_t.astype(FULL),
            side_1[:ROWS] + got_t[ROWS:].astype(FULL) + last_y.astype(FULL),
        )

    def parts(self):
        return (*self.mine, self.got_y, self.got_t, self.last_t, self.last_y)


GROUPS = [
    [16 * y + 8 * c + 4 * hi + 2 * e + t for c in (0, 1) for hi in (0, 1) for e in (0, 1)]
    for y in (0, 1)
    for t in (0, 1)
]


class Gather:
    def __init__(self, steps, work, *values):
        piece = steps.do(work, *values)
        self.whole = lax.all_gather(piece, ALL, axis=0, tiled=True, axis_index_groups=GROUPS)

    def pieces(self):
        return [(self.whole, AT_NUMBERS + at) for at in range(8)]


QUARTETS = [
    [16 * y + 8 * c + 4 * hi + 2 * e + t for hi in (0, 1) for e in (0, 1)]
    for y in (0, 1)
    for c in (0, 1)
    for t in (0, 1)
]


class Scatter:
    def __init__(self, product, *values):
        self.product, self.values = product, values

    def core(self, steps):
        self.from_core = swap(
            steps.do(functools.partial(self.product, 1), *self.values), MASK_C
        )

    def send(self, steps):
        self.result = lax.psum_scatter(
            steps.do(functools.partial(self.product, 0), *self.values, self.from_core),
            ALL,
            scatter_dimension=0,
            tiled=True,
            axis_index_groups=QUARTETS,
        )


def split_pieces(pieces):
    return [array for array, _ in pieces], tuple(base for _, base in pieces)


VMEM_LIMIT = 56 * 2**20


def compiler_params():
    return pltpu.CompilerParams(vmem_limit_bytes=VMEM_LIMIT)


def fixed(shape):
    return pl.BlockSpec(shape, lambda i, *_: (0, 0), pipeline_mode=pl.Buffered(1))


TILE = 256


def join_kernel(*refs):
    at = 0
    for ref in refs[:-1]:
        rows = ref.shape[0]
        refs[-1][at : at + rows, :] = ref[...]
        at += rows


def join_rows(sizes, *parts):
    width = parts[0].shape[1]
    tile = width // 4
    rows = sum(sizes)
    return pl.pallas_call(
        join_kernel,
        grid=(4,),
        in_specs=[pl.BlockSpec((size, tile), lambda i: (0, i)) for size in sizes],
        out_specs=pl.BlockSpec((rows, tile), lambda i: (0, i)),
        out_shape=jax.ShapeDtypeStruct((rows, width), parts[0].dtype),
        compiler_params=compiler_params(),
        cost_estimate=cost(0, 4 * rows * width),
    )(*parts)


def heads_kernel(scalars, rows, gradient, mixed, stream, *refs):
    out = refs[-1]
    width = gradient.shape[1]
    total = dot_tokens(rows[...], gradient[...])
    weight = dot_tokens(mixed[...], stream[...])
    if len(refs) == 2:
        total = total + refs[0][:, :width].astype(FULL)
    out[:, :width] = total.astype(LOW)
    rest = out.shape[1] - width
    for at in range(4):
        part = weight[:, at * rest : (at + 1) * rest]
        place = slice(at * HEAD_DIM, (at + 1) * HEAD_DIM)
        if len(refs) == 2:
            part = part + refs[0][place, width:].astype(FULL)
        out[place, width:] = part.astype(LOW)


def scatter_heads(scalars, side, rows, gradient, mixed, stream, *adds):
    tokens, depth = rows.shape
    block, width = depth // 4, gradient.shape[1] // 2
    middle = stream.shape[1] // 2
    out = pl.BlockSpec((block, middle), lambda i, s: (s[AT_FOURTHS + i], 0))

    def side_of(size):
        return pl.BlockSpec((tokens, size), lambda i, s: (0, side), pipeline_mode=pl.Buffered(1))

    return pl.pallas_call(
        heads_kernel,
        grid_spec=pltpu.PrefetchScalarGridSpec(
            num_scalar_prefetch=1,
            grid=(4,),
            in_specs=[
                pl.BlockSpec((tokens, block), lambda i, s: (0, i)),
                side_of(width),
                pl.BlockSpec((tokens, HEAD_DIM), lambda i, s: (0, s[i])),
                side_of(middle),
            ]
            + [out] * len(adds),
            out_specs=out,
        ),
        out_shape=jax.ShapeDtypeStruct((depth, middle), LOW),
        compiler_params=compiler_params(),
        cost_estimate=cost(8 * tokens * block * middle, 2 * tokens * (depth + 2 * middle)),
    )(scalars, rows, gradient, mixed, stream, *adds)


def scatter_kernel(scalars, operand, gradient, *refs):
    total = dot_tokens(operand[...], gradient[...])
    for ref in refs[:-1]:
        total = total + ref[...].astype(FULL)
    refs[-1][...] = total.astype(refs[-1].dtype)


def scatter_blocks(scalars, placed, side, operand, gradient, *adds):
    tokens, depth = operand.shape
    block, width = depth // 4, gradient.shape[1] // 2
    out = pl.BlockSpec((block, width), lambda i, s: (s[AT_FOURTHS + i], 0))
    return pl.pallas_call(
        scatter_kernel,
        grid_spec=pltpu.PrefetchScalarGridSpec(
            num_scalar_prefetch=1,
            grid=(4,),
            in_specs=[
                pl.BlockSpec((tokens, block), lambda i, s: (0, s[i] if placed else i)),
                pl.BlockSpec(
                    (tokens, width), lambda i, s: (0, side), pipeline_mode=pl.Buffered(1)
                ),
            ]
            + [out] * len(adds),
            out_specs=out,
        ),
        out_shape=jax.ShapeDtypeStruct((4 * block, width), LOW),
        compiler_params=compiler_params(),
        cost_estimate=cost(
            8 * tokens * block * width, 2 * (4 * tokens * block + tokens * width + 8 * block * width)
        ),
    )(scalars, operand, gradient, *adds)


COST_SHARE = 0.25


def cost(flops, size, transcendentals=0):
    return pl.CostEstimate(
        flops=int(COST_SHARE * flops),
        bytes_accessed=int(COST_SHARE * size),
        transcendentals=int(COST_SHARE * transcendentals),
    )


def piece_sum(rows, pieces):
    depth = pieces[0].shape[0]
    total = dot(rows[:, :depth], pieces[0][...])
    for at in range(1, len(pieces)):
        total = total + dot(rows[:, at * depth : (at + 1) * depth], pieces[at][...])
    return total


PIECE = 2 * ROWS


def piece_block(rows, width, base, place, size=PIECE):
    def index(i, scalars):
        row, column = place(i, scalars)
        return (row + scalars[base] * (size // rows), column)

    return pl.BlockSpec((rows, width), index)


def piece_tiles(base, side, tiles, size=PIECE):
    return piece_block(
        size, TILE, base, lambda i, _: (0, jnp.clip(i - side * tiles, 0, tiles - 1)), size
    )


AT_Y, AT_NUMBERS, AT_FOURTHS, AT_T = 4, 5, 13, 17


def divided_sum(scalars, rows, pieces):
    total = 0.0
    for at, piece in enumerate(pieces):
        start = pl.multiple_of((at - at % 2 + (scalars[AT_T] ^ (at % 2))) * ROWS, ROWS)
        total = total + dot(rows[:, pl.ds(start, ROWS)], piece[...])
    return total


def pieces_kernel(tiles, scalars, rows, *refs):
    for side in range(2):

        @pl.when(pl.program_id(0) // tiles == side)
        def _(side=side):
            refs[8][...] = piece_sum(rows, refs[4 * side : 4 * side + 4])


def product_pieces(bases, scalars, rows, *pieces):
    tokens, depth = rows.shape
    width = pieces[0].shape[1]
    tiles = width // TILE
    return pl.pallas_call(
        functools.partial(pieces_kernel, tiles),
        grid_spec=pltpu.PrefetchScalarGridSpec(
            num_scalar_prefetch=1,
            grid=(2 * tiles,),
            in_specs=[fixed(rows.shape)]
            + [piece_tiles(base, at // 4, tiles) for at, base in enumerate(bases)],
            out_specs=pl.BlockSpec((tokens, TILE), lambda i, *_: (0, i)),
        ),
        out_shape=jax.ShapeDtypeStruct((tokens, 2 * width), FULL),
        compiler_params=compiler_params(),
        cost_estimate=cost(4 * tokens * depth * width, 2 * depth * (tokens + 2 * width)),
    )(scalars, rows, *pieces)


def unit_kernel(tiles, scalars, rows, *refs):
    gate, upper, active = refs[24:]
    for side in range(2):

        @pl.when(pl.program_id(0) // tiles == side)
        def _(side=side):
            a = divided_sum(scalars, rows, refs[12 * side : 12 * side + 8])
            b = piece_sum(rows, refs[12 * side + 8 : 12 * side + 12])
            gated = jnp.where(scalars[AT_Y] == 0, a, b)
            raised = jnp.where(scalars[AT_Y] == 0, b, a)
            gate[...] = gated.astype(LOW)
            upper[...] = raised.astype(LOW)
            active[...] = (gated * jax.nn.sigmoid(gated) * raised).astype(LOW)


def unit_forward(scalars, rows, *pieces):
    tokens, depth = rows.shape
    width = pieces[0].shape[1]
    tiles = width // TILE
    in_specs = [fixed(rows.shape)]
    for side in range(2):
        at = AT_NUMBERS + 4 * side
        in_specs += [piece_tiles(at + k // 2, side, tiles, ROWS) for k in range(8)]
        in_specs += [piece_tiles(at + k, side, tiles) for k in range(4)]
    out = pl.BlockSpec((tokens, TILE), lambda i, *_: (0, i))
    shape = jax.ShapeDtypeStruct((tokens, 2 * width), LOW)
    return pl.pallas_call(
        functools.partial(unit_kernel, tiles),
        grid_spec=pltpu.PrefetchScalarGridSpec(
            num_scalar_prefetch=1,
            grid=(2 * tiles,),
            in_specs=in_specs,
            out_specs=[out, out, out],
        ),
        out_shape=[shape, shape, shape],
        compiler_params=compiler_params(),
        cost_estimate=cost(
            8 * tokens * depth * width, 2 * depth * (tokens + 4 * width) + 12 * tokens * width
        ),
    )(scalars, rows, *pieces)


def unit_back_kernel(scalars, own, other, *refs):
    gate, upper, grad_a, grad_b = refs[8:]
    for at in range(4):

        @pl.when(pl.program_id(0) // 2 == at)
        def _(at=at):
            grad = dot_back(own[...], refs[at][...]) + dot_back(other[...], refs[4 + at][...])
            gated, raised = gate[...].astype(FULL), upper[...].astype(FULL)
            sigmoid = jax.nn.sigmoid(gated)
            gate_grad = grad * raised * sigmoid * (1.0 + gated * (1.0 - sigmoid))
            upper_grad = grad * (gated * sigmoid)
            grad_a[...] = jnp.where(scalars[AT_Y] == 0, gate_grad, upper_grad).astype(LOW)
            grad_b[...] = jnp.where(scalars[AT_Y] == 0, upper_grad, gate_grad).astype(LOW)


def unit_back(bases, scalars, rows, gate, upper, *pieces):
    tokens, depth = rows.shape
    units = gate.shape[1]
    cut = depth // 2
    shape = jax.ShapeDtypeStruct((tokens, units), LOW)
    out = pl.BlockSpec((tokens, TILE), lambda i, scalars: (0, 2 * scalars[i // 2] + i % 2))

    def half_rows(at):
        return pl.BlockSpec((tokens, cut), lambda i, *_: (0, at), pipeline_mode=pl.Buffered(1))

    def units_of(at, base):
        return piece_block(TILE, cut, base, lambda i, _: (jnp.clip(i - 2 * (at % 4), 0, 1), 0))

    return pl.pallas_call(
        unit_back_kernel,
        grid_spec=pltpu.PrefetchScalarGridSpec(
            num_scalar_prefetch=1,
            grid=(8,),
            in_specs=[half_rows(0), half_rows(1)] + [units_of(at, base) for at, base in enumerate(bases)] + [out, out],
            out_specs=[out, out],
        ),
        out_shape=[shape, shape],
        compiler_params=compiler_params(),
        cost_estimate=cost(
            2 * tokens * depth * units, 2 * depth * (tokens + units) + 8 * tokens * units
        ),
    )(scalars, rows, rows, *pieces, gate, upper)


def chunk_rows(left, chunk, width, place):
    return pl.BlockSpec(
        (ROWS, width), lambda i, scalars: (chunk, place(scalars)), pipeline_mode=pl.Buffered(1)
    )


def back_kernel(chunks, counts, _, *refs):
    terms = len(counts)
    lefts, rights, out = refs[: chunks * terms], refs[chunks * terms : -1], refs[-1]
    for step in range(4):

        @pl.when(pl.program_id(0) == step)
        def _(step=step):
            for chunk in range(chunks):
                total, first = 0.0, 0
                for term, count in enumerate(counts):
                    right = rights[first + step * count // 4]
                    total = total + dot_back(lefts[chunk * terms + term][...], right[...])
                    first += count
                out[chunk * ROWS : (chunk + 1) * ROWS, :] = total.astype(out.dtype)


def product_back(scalars, chunks, dtype, terms):
    in_specs, values = [], []
    for chunk in chunks:
        for left, at, _ in terms:
            in_specs.append(chunk_rows(left, chunk, left.shape[1] // 2, lambda s, at=at: at))
            values.append(left)
    depth = 0
    for left, _, pieces in terms:
        depth += left.shape[1] // 2
        for piece, base in pieces:
            if len(pieces) == 4:
                spec = piece_block(ROWS, piece.shape[1], base, lambda i, s: (0, 0), ROWS)
            else:
                spec = piece_block(
                    ROWS, piece.shape[1], base, lambda i, s: (s[AT_T] ^ (i % 2), 0)
                )
            in_specs.append(spec)
            values.append(piece)
    rows, width = len(chunks) * ROWS, 4 * TILE
    counts = [len(pieces) for _, _, pieces in terms]
    return pl.pallas_call(
        functools.partial(back_kernel, len(chunks), counts),
        grid_spec=pltpu.PrefetchScalarGridSpec(
            num_scalar_prefetch=1,
            grid=(4,),
            in_specs=in_specs,
            out_specs=pl.BlockSpec(
                (rows, TILE), lambda i, s: (0, i - i % 2 + (s[AT_T] ^ (i % 2)))
            ),
        ),
        out_shape=jax.ShapeDtypeStruct((rows, width), dtype),
        compiler_params=compiler_params(),
        cost_estimate=cost(2 * rows * depth * width, 2 * depth * (rows + width) + 4 * rows * width),
    )(scalars, *values)


def forward_kernel(chunks, _, *refs):
    lefts, rights, out = refs[: chunks * 4], refs[chunks * 4 : -1], refs[-1]
    for chunk in range(chunks):
        total = dot(lefts[4 * chunk][...], rights[0][...])
        for at in range(1, 4):
            total = total + dot(lefts[4 * chunk + at][...], rights[at][...])
        out[chunk * ROWS : (chunk + 1) * ROWS, :] = total.astype(out.dtype)


def product_forward(chunks, dtype, bases, scalars, left, *pieces):
    depth, width = PIECE, pieces[0].shape[1]
    in_specs = [
        chunk_rows(left, chunk, depth, lambda scalars, at=at: scalars[at])
        for chunk in chunks
        for at in range(4)
    ] + [piece_block(PIECE, TILE, base, lambda i, _: (0, i)) for base in bases]
    rows = len(chunks) * ROWS
    return pl.pallas_call(
        functools.partial(forward_kernel, len(chunks)),
        grid_spec=pltpu.PrefetchScalarGridSpec(
            num_scalar_prefetch=1,
            grid=(width // TILE,),
            in_specs=in_specs,
            out_specs=pl.BlockSpec((rows, TILE), lambda i, *_: (0, i)),
        ),
        out_shape=jax.ShapeDtypeStruct((rows, width), dtype),
        compiler_params=compiler_params(),
        cost_estimate=cost(
            8 * rows * depth * width, 8 * depth * (rows + width) + 4 * rows * width
        ),
    )(scalars, *([left] * (4 * len(chunks))), *pieces)


def signed_tables():
    cosine, sine = rotary_tables(ROWS, HEAD_DIM)
    sign = jnp.concatenate(
        [-jnp.ones((HEAD_DIM // 2,), FULL), jnp.ones((HEAD_DIM // 2,), FULL)]
    )
    return (cosine[:, 0, :], sine[:, 0, :] * sign)


SCALE = HEAD_DIM ** (-0.5)
GROUP_HEADS = 4
GROUP_WIDTH = GROUP_HEADS * HEAD_DIM


def softmax_rows(query, key, allowed):
    scores = dot_back(query, key) * SCALE
    scores = jnp.where(allowed, scores, -1e30)
    weights = jnp.exp(scores - jnp.max(scores, axis=-1, keepdims=True))
    return weights / jnp.sum(weights, axis=-1, keepdims=True)


SIDE_WIDTH = 6 * HEAD_DIM


def head_columns(side, which, head):
    start = side * SIDE_WIDTH + (2 * which + head) * HEAD_DIM
    return slice(start, start + HEAD_DIM)


def mixed_columns(side, head):
    start = (2 * side + head) * HEAD_DIM
    return slice(start, start + HEAD_DIM)


def attend_kernel(projected, mask, cosine, sine, lowered, mixed):
    allowed = mask[...] > 0.0
    cos, sin = cosine[...], sine[...]
    for side in range(2):
        for head in range(2):

            def rope(which):
                values = projected[:, head_columns(side, which, head)]
                return (values * cos + pltpu.roll(values, HEAD_DIM // 2, 1) * sin).astype(LOW)

            query, key = rope(0), rope(1)
            value = projected[:, head_columns(side, 2, head)].astype(LOW)
            probability = softmax_rows(query, key, allowed)
            lowered[:, head_columns(side, 0, head)] = query
            lowered[:, head_columns(side, 1, head)] = key
            lowered[:, head_columns(side, 2, head)] = value
            mixed[:, mixed_columns(side, head)] = dot(probability.astype(LOW), value).astype(LOW)


def attend_back_kernel(lowered, mask, cosine, sine, mixed_grad, projected_grad):
    allowed = mask[...] > 0.0
    cos, sin = cosine[...], sine[...]
    for side in range(2):
        for head in range(2):
            query = lowered[:, head_columns(side, 0, head)]
            key = lowered[:, head_columns(side, 1, head)]
            value = lowered[:, head_columns(side, 2, head)]
            grad = mixed_grad[:, mixed_columns(side, head)]
            probability = softmax_rows(query, key, allowed)
            prob_grad = dot_back(grad, value)
            inner = jnp.sum(probability * prob_grad, axis=-1, keepdims=True)
            score_grad = (probability * (prob_grad - inner)).astype(LOW)
            query_grad = dot(score_grad, key) * SCALE
            key_grad = dot_tokens(score_grad, query) * SCALE
            value_grad = dot_tokens(probability.astype(LOW), grad)

            def unrope(values):
                return (values * cos - pltpu.roll(values, HEAD_DIM // 2, 1) * sin).astype(LOW)

            projected_grad[:, head_columns(side, 0, head)] = unrope(query_grad)
            projected_grad[:, head_columns(side, 1, head)] = unrope(key_grad)
            projected_grad[:, head_columns(side, 2, head)] = value_grad.astype(LOW)


def row_block(width):
    return pl.BlockSpec((ROWS, width), lambda i: (i, 0))


def whole_block(width):
    return pl.BlockSpec((ROWS, width), lambda i: (0, 0))


def attend(projected, mask, cosine, sine):
    rows = projected.shape[0]
    return pl.pallas_call(
        attend_kernel,
        grid=(rows // ROWS,),
        in_specs=[
            row_block(2 * SIDE_WIDTH),
            row_block(ROWS),
            whole_block(HEAD_DIM),
            whole_block(HEAD_DIM),
        ],
        out_specs=[row_block(2 * SIDE_WIDTH), row_block(GROUP_WIDTH)],
        out_shape=[
            jax.ShapeDtypeStruct((rows, 2 * SIDE_WIDTH), LOW),
            jax.ShapeDtypeStruct((rows, GROUP_WIDTH), LOW),
        ],
        compiler_params=compiler_params(),
        cost_estimate=cost(
            4 * rows * ROWS * GROUP_WIDTH, rows * GROUP_WIDTH * 20, rows * ROWS * GROUP_HEADS
        ),
    )(projected, mask, cosine, sine)


def attend_back(lowered, mask, cosine, sine, mixed_grad):
    rows = lowered.shape[0]
    return pl.pallas_call(
        attend_back_kernel,
        grid=(rows // ROWS,),
        in_specs=[
            row_block(2 * SIDE_WIDTH),
            row_block(ROWS),
            whole_block(HEAD_DIM),
            whole_block(HEAD_DIM),
            row_block(GROUP_WIDTH),
        ],
        out_specs=row_block(2 * SIDE_WIDTH),
        out_shape=jax.ShapeDtypeStruct((rows, 2 * SIDE_WIDTH), LOW),
        compiler_params=compiler_params(),
        cost_estimate=cost(
            10 * rows * ROWS * GROUP_WIDTH, rows * GROUP_WIDTH * 14, rows * ROWS * GROUP_HEADS
        ),
    )(lowered, mask, cosine, sine, mixed_grad)


def split_layer(
    inputs,
    cotangent,
    segment_ids,
    master_qkv,
    master_out,
    master_in,
    master_down,
    first_qkv,
    first_out,
    first_in,
    first_down,
    second_qkv,
    second_out,
    second_in,
    second_down,
):
    rep, fsdp = lax.axis_index("rep"), lax.axis_index("fsdp")
    y, c = rep // 2, rep % 2
    hi, e, t = fsdp // 4, (fsdp // 2) % 2, fsdp % 2
    width = inputs.shape[1]
    middle = width // 2
    unit = width // 4
    pair = 2 * HEAD_DIM
    pairs = master_qkv.shape[1] // pair
    block = pairs * HEAD_DIM
    steps = Steps()

    def relative(values):
        starts = [
            4 * (hi ^ at_hi) + 2 * (e ^ at_e) + at_t
            for at_e in (0, 1)
            for at_hi in (0, 1)
            for at_t in (0, 1)
        ]
        return columns(values, [start * ROWS for start in starts], ROWS)

    def natural(values):
        starts = [
            4 * (e ^ at_e) + 2 * (hi ^ at_hi) + at_t
            for at_hi in (0, 1)
            for at_e in (0, 1)
            for at_t in (0, 1)
        ]
        return columns(values, [start * ROWS for start in starts], ROWS)

    def core_first(values):
        return columns(values, [c * unit, (2 + c) * unit, (1 - c) * unit, (3 - c) * unit], unit)

    def core_natural(own, other):
        even, odd = jnp.where(c == 0, own, other), jnp.where(c == 0, other, own)
        return jnp.concatenate(
            [even[:, :unit], odd[:, :unit], even[:, unit:], odd[:, unit:]], axis=1
        )

    places = [2 * ((hi ^ at_hi) ^ c) + (e ^ at_e) for at_e in (0, 1) for at_hi in (0, 1)]
    numbers = [
        4 * (c ^ at_c) + 2 * (hi ^ at_hi) + (e ^ at_e)
        for at_c in (0, 1)
        for at_e in (0, 1)
        for at_hi in (0, 1)
    ]
    fourths = [2 * (hi ^ at_hi) + (e ^ at_e) for at_e in (0, 1) for at_hi in (0, 1)]
    scalars = jnp.stack([*places, y, *numbers, *fourths, t]).astype(jnp.int32)

    def in_rows(mine, other):
        return in_order(t, mine, other, 0)

    def in_columns(mine, other):
        return in_order(y, mine, other, 1)

    def split_pairs(weight):
        low = weight.astype(LOW)
        return (
            columns(low, [j * pair + (1 - y) * HEAD_DIM for j in range(pairs)], HEAD_DIM),
            columns(low, [j * pair + y * HEAD_DIM for j in range(pairs)], HEAD_DIM),
        )

    def all_pairs(mine, theirs):
        even, odd = jnp.where(c == 0, mine, theirs), jnp.where(c == 0, theirs, mine)
        whole = jnp.concatenate(
            [even[:, :block], odd[:, :block], even[:, block:], odd[:, block:]], axis=1
        )

        def part(t_bit):
            starts = [8 * j + 4 * c + 2 * k + t_bit for j in range(3) for k in range(2)]
            return columns(whole, [start * HEAD_DIM for start in starts], HEAD_DIM)

        return part(1 - t), part(t)

    def split_rows(weight):
        low = weight.astype(LOW)
        return half(low, 0, 1 - y), half(low, 0, y)

    def unit_columns(low, t_bit, y_bit):
        return columns(low, [(4 * j + 2 * t_bit + y_bit) * unit for j in range(2)], unit)

    def split_in(weight):
        low = weight.astype(LOW)
        return (
            unit_columns(low, 1 - t, y),
            jnp.concatenate(
                [unit_columns(low, 1 - t, 1 - y), unit_columns(low, t, 1 - y)], axis=1
            ),
        )

    def norm_low(values, ids):
        normed, inverse = normalize(values.astype(FULL))
        extra = jnp.tile(ids.astype(LOW), (16, width // ROWS))
        return jnp.concatenate([relative(normed.astype(LOW)), extra], axis=0), inverse

    a_own = Gather(steps, lambda v: unit_columns(v, t, y).astype(LOW), master_in)
    given, kept = steps.do(split_pairs, master_qkv)
    pairs_y = swap(given, MASK_Y)
    give_t, give_y = steps.do(split_in, master_in)
    lowered_one, inverse_one = steps.do(norm_low, inputs, segment_ids)
    given, out_kept = steps.do(split_rows, master_out)
    pairs_mine = steps.do(in_columns, kept, pairs_y)
    pairs_core = swap(pairs_mine, MASK_C)
    out_y = swap(given, MASK_Y)
    tokens_one = Tokens(lowered_one)
    tokens_one.send_y(steps)
    given, pairs_kept = steps.do(all_pairs, pairs_mine, pairs_core)
    pairs_t = swap(given, MASK_T)
    give_down, down_kept = steps.do(split_rows, master_down)
    a_own.whole = steps.wait(a_own.whole)
    qkv = Gather(steps, in_rows, pairs_kept, pairs_t)
    in_t = swap(steps.wait(give_t), MASK_T)
    out = Gather(steps, in_columns, out_kept, out_y)
    tokens_one.send_t(steps)
    a_other = Gather(steps, lambda v: v, in_t)
    tokens_one.from_y = steps.wait(tokens_one.from_y)
    in_y = swap(steps.wait(give_y), MASK_Y)
    tokens_one.second(steps)
    in_y = steps.wait(in_y)
    in_b_t = swap(steps.do(lambda v: v[:, :middle], in_y), MASK_T)
    down_y = swap(steps.wait(give_down), MASK_Y)
    rows_one = tokens_one.rows(steps)

    def attention_mask(own, from_y, from_t, upper):
        segments = jnp.stack(
            [own[ROWS], from_y[ROWS], upper[ROWS // 2], from_t[ROWS]], axis=0
        )[:, :ROWS]
        at = jnp.arange(ROWS)
        allowed = (segments[:, :, None] == segments[:, None, :]) & (at[None, :] <= at[:, None])
        return allowed.astype(FULL).reshape(4 * ROWS, ROWS)

    mask = steps.do(
        attention_mask, tokens_one.values, tokens_one.from_y, tokens_one.from_t, tokens_one.upper
    )
    cosine, sine = signed_tables()
    b = Gather(steps, lambda v, other: in_rows(v[:, middle:], other), in_y, in_b_t)
    down = Gather(steps, in_columns, down_kept, down_y)
    qkv_pieces, qkv_bases = split_pieces(qkv.pieces())
    projected = steps.do(
        functools.partial(product_pieces, qkv_bases, scalars), rows_one, *qkv_pieces
    )
    lowered, mixed_low = steps.do(attend, projected, mask, cosine, sine)

    def join_out(whole):
        rows = pair

        def block(core, half_at):
            start = (core * 2 + (half_at ^ c)) * rows
            return lax.dynamic_slice_in_dim(whole, start, rows, 0)

        return jnp.concatenate(
            [jnp.concatenate([block(c, k), block(1 - c, k)], axis=1) for k in (0, 1)], axis=0
        )

    weight_out = steps.do(join_out, out.whole)

    def product_out(chunks, side, dtype, operand, weight):
        right = weight[:, side * middle : (side + 1) * middle]
        if chunks[0] + 1 == chunks[1]:
            left = operand[chunks[0] * ROWS : (chunks[1] + 1) * ROWS]
            return dot(left, right).astype(dtype)
        parts = [dot(operand[at * ROWS : (at + 1) * ROWS], right) for at in chunks]
        return jnp.concatenate(parts, axis=0).astype(dtype)

    sum_out = Sum(product_out, mixed_low, weight_out)
    sum_out.first(steps)
    sum_out.send()
    sum_out.own(steps)
    sum_out.second(steps)

    def norm_stream(values, *parts):
        stream = values.astype(FULL) + core_natural(*sum_out.total(*parts))
        normed, inverse = normalize(stream)
        return relative(normed.astype(LOW)), stream, inverse

    lowered_two, stream, inverse_two = steps.do(norm_stream, inputs, *sum_out.parts())
    tokens_two = Tokens(lowered_two)
    tokens_two.send(steps)
    tokens_two.second(steps)
    rows_two = tokens_two.rows(steps)
    tokens_cotangent = Tokens(steps.do(core_first, cotangent))
    tokens_cotangent.send(steps)

    halves = [
        piece for two in zip(a_own.pieces(), a_other.pieces()) for piece in two
    ]
    pieces_b = b.pieces()
    in_pieces, in_bases = split_pieces([*halves[:8], *pieces_b[:4], *halves[8:], *pieces_b[4:]])
    gate, upper, active = steps.do(
        functools.partial(unit_forward, scalars), rows_two, *in_pieces
    )
    tokens_cotangent.second(steps)
    rows_cotangent = tokens_cotangent.rows(steps)
    placed_blocks = functools.partial(scatter_blocks, scalars, True)
    piece_blocks = functools.partial(scatter_blocks, scalars, False)
    scatter_down = Scatter(placed_blocks, active, rows_cotangent)
    scatter_down.core(steps)
    scatter_down.send(steps)
    down_pieces, down_bases = split_pieces(down.pieces())

    grad_a, grad_b = steps.do(
        functools.partial(unit_back, down_bases, scalars), rows_cotangent, gate, upper, *down_pieces
    )

    def product_units(chunks, side, dtype, grad_a, grad_b, *arrays):
        at = slice(2 * side, 2 * side + 2)
        halves = slice(4 * side, 4 * side + 4)
        pieces = list(zip(arrays, in_bases))
        terms = [
            (grad_a, 0, pieces[0:8][halves]),
            (grad_b, 0, pieces[8:12][at]),
            (grad_a, 1, pieces[12:20][halves]),
            (grad_b, 1, pieces[20:24][at]),
        ]
        return product_back(scalars, chunks, dtype, terms)

    sum_two = Sum(product_units, grad_a, grad_b, *in_pieces)
    sum_two.first(steps)
    sum_two.send()
    scatter_a = Scatter(piece_blocks, rows_two, grad_a)
    scatter_a.core(steps)
    sum_two.own(steps)
    scatter_a.send(steps)
    sum_two.second(steps)
    scatter_b = Scatter(piece_blocks, rows_two, grad_b)
    scatter_b.core(steps)

    def stream_back(grad, stream, inverse, *parts):
        normed = (stream - jnp.mean(stream, axis=-1, keepdims=True)) * inverse
        total = natural(jnp.concatenate(sum_two.total(*parts), axis=1))
        result = grad.astype(FULL) + norm_back(normed, inverse, total)
        return core_first(result.astype(LOW)), result

    stream_grad_low, stream_grad = steps.do(
        stream_back, cotangent, stream, inverse_two, *sum_two.parts()
    )
    tokens_stream = Tokens(stream_grad_low)
    tokens_stream.send(steps)
    scatter_b.send(steps)

    def product_final(chunks, side, dtype, active, *pieces):
        at = slice(4 * side, 4 * side + 4)
        return product_forward(chunks, dtype, down_bases[at], scalars, active, *pieces[at])

    sum_final = Sum(product_final, active, *down_pieces)
    sum_final.first(steps)
    tokens_stream.second(steps)
    sum_final.own(steps)
    rows_stream = tokens_stream.rows(steps)
    sum_final.release(steps)
    sum_final.send()

    mixed_grad = steps.do(
        lambda rows, weight: dot_back(rows, weight).astype(LOW), rows_stream, weight_out
    )
    projected_grad = steps.do(attend_back, lowered, mask, cosine, sine, mixed_grad)
    scatter_attention = Scatter(
        functools.partial(scatter_heads, scalars), rows_one, projected_grad, mixed_low, rows_stream
    )
    scatter_attention.core(steps)

    def product_qkv(chunks, side, dtype, gradient, *arrays):
        at = slice(2 * side, 2 * side + 2)
        pieces = list(zip(arrays, qkv_bases))
        terms = [(gradient, 0, pieces[:4][at]), (gradient, 1, pieces[4:][at])]
        return product_back(scalars, chunks, dtype, terms)

    sum_one = Sum(product_qkv, projected_grad, *qkv_pieces)
    sum_one.first(steps)
    scatter_attention.send(steps)

    def output_of(stream, *parts):
        final = stream + core_natural(*sum_final.total(*parts))
        squares = jnp.stack([jnp.sum(stream * stream), jnp.sum(final * final)]).reshape(1, 2)
        return final.astype(LOW), squares

    def input_back(values, inverse, grad, *parts):
        source = values.astype(FULL)
        normed = (source - jnp.mean(source, axis=-1, keepdims=True)) * inverse
        total = natural(jnp.concatenate(sum_one.total(*parts), axis=1))
        return (grad + norm_back(normed, inverse, total)).astype(LOW)

    def adam_down(mine, got, *state):
        gradient = in_order(y, mine, got, 0).astype(FULL)
        return (gradient, *adam_step(state[0], gradient, *state[1:], rate))

    def adam_in(mine, from_t, from_y, from_both, *state):
        sides = []
        for bit in range(2):
            same = jnp.where(t == bit, mine, from_t).astype(FULL)
            cross = jnp.where(t == bit, from_y, from_both).astype(FULL)
            sides.append((jnp.where(y == 0, same, cross), jnp.where(y == 0, cross, same)))
        blocks = [
            part[:, j * unit : (j + 1) * unit] for j in range(2) for side in sides for part in side
        ]
        gradient = jnp.concatenate(blocks, axis=1)
        return (gradient, *adam_step(state[0], gradient, *state[1:], rate))

    def split_attention(total):
        parts = total[:, : 3 * pair]
        out_rows = jnp.concatenate(
            [total[j * HEAD_DIM : (j + 1) * HEAD_DIM, 3 * pair :] for j in range(4)], axis=1
        )
        return (
            half(parts, 0, 1 - t),
            half(parts, 0, t),
            half(out_rows, 1, 1 - y),
            half(out_rows, 1, y),
        )

    def core_pairs(kept, got):
        even, odd = jnp.where(t == 0, kept, got), jnp.where(t == 0, got, kept)
        return jnp.concatenate(
            [
                part[:, j * HEAD_DIM : (j + 1) * HEAD_DIM]
                for j in range(6)
                for part in (even, odd)
            ],
            axis=1,
        )

    def split_grad(mine, theirs):
        even, odd = jnp.where(c == 0, mine, theirs), jnp.where(c == 0, theirs, mine)
        whole = jnp.concatenate(
            [
                part[:, j * 2 * pair : (j + 1) * 2 * pair]
                for j in range(3)
                for part in (even, odd)
            ],
            axis=1,
        )
        return (
            lax.dynamic_slice_in_dim(whole, (2 * (1 - y) + c) * block, block, 1),
            lax.dynamic_slice_in_dim(whole, (2 * y + c) * block, block, 1),
        )

    def adam_out(mine, got, *state):
        gradient = in_order(y, mine, got, 0).astype(FULL)
        return (gradient, *adam_step(state[0], gradient, *state[1:], rate_out))

    def adam_qkv(mine, got, *state):
        even, odd = jnp.where(y == 0, mine, got), jnp.where(y == 0, got, mine)
        gradient = jnp.concatenate(
            [
                part[:, j * HEAD_DIM : (j + 1) * HEAD_DIM]
                for j in range(pairs)
                for part in (even, odd)
            ],
            axis=1,
        ).astype(FULL)
        return (gradient, *adam_step(state[0], gradient, *state[1:], rate))

    def share(squares, bit):
        return steps.do(jnp.add, squares, swap(squares, bit))

    sum_final.second(steps)
    sum_one.release(steps)
    sum_one.send()
    sum_one.own(steps)
    give_down, mine_down = steps.do(
        lambda v: (half(v, 1, 1 - y), half(v, 1, y)), scatter_down.result
    )
    down_y = swap(give_down, MASK_Y)
    given, in_mine = steps.do(
        lambda v: (half(v, 0, 1 - t), half(v, 0, t)), scatter_a.result
    )
    from_t = swap(given, MASK_T)
    output, squares = steps.do(output_of, stream, *sum_final.parts())
    sum_one.second(steps)
    squares = share(squares, MASK_E)
    given_y, given_both = steps.do(
        lambda v: (half(v, 0, t), half(v, 0, 1 - t)), scatter_b.result
    )
    from_y = swap(given_y, MASK_Y)
    from_both = swap(given_both, MASK_Y | MASK_T)
    step_down = steps.do(adam_down, mine_down, down_y, master_down, first_down, second_down)
    squares = share(squares, MASK_T)
    input_grad = steps.do(input_back, inputs, inverse_one, stream_grad, *sum_one.parts())
    squares = share(squares, MASK_HI)
    given, kept, give_out, mine_out = steps.do(split_attention, scatter_attention.result)
    pairs_t = swap(given, MASK_T)
    out_y = swap(give_out, MASK_Y)
    squares = share(squares, MASK_C)
    step_in = steps.do(
        adam_in, in_mine, from_t, from_y, from_both, master_in, first_in, second_in
    )
    pairs_mine = steps.do(core_pairs, kept, pairs_t)
    pairs_core = swap(pairs_mine, MASK_C)
    step_out = steps.do(adam_out, mine_out, out_y, master_out, first_out, second_out)
    given, kept = steps.do(split_grad, pairs_mine, pairs_core)
    pairs_y = swap(given, MASK_Y)
    squares = share(squares, MASK_Y)
    stream_rms = jnp.sqrt(squares[0] / (ROWS * width * DEVICES))
    step_qkv = steps.do(adam_qkv, kept, pairs_y, master_qkv, first_qkv, second_qkv)
    results = zip(step_qkv, step_out, step_in, step_down)
    grads, updated, moments, variances, narrows = results
    return (output, input_grad, *grads, *updated, *moments, *variances, *narrows, stream_rms)


def solution(mesh):
    shards = split_layer if tuple(mesh.shape.values()) == (4, 8) else gathered_layer
    return jax.shard_map(
        shards,
        mesh=mesh,
        in_specs=(
            P(("rep", "fsdp"), None),
            P(("rep", "fsdp"), None),
            P(("rep", "fsdp"), None),
            P("fsdp", "rep"),
            P("fsdp", "rep"),
            P("fsdp", "rep"),
            P("fsdp", "rep"),
            P("fsdp", "rep"),
            P("fsdp", "rep"),
            P("fsdp", "rep"),
            P("fsdp", "rep"),
            P("fsdp", "rep"),
            P("fsdp", "rep"),
            P("fsdp", "rep"),
            P("fsdp", "rep"),
        ),
        out_specs=(
            P(("rep", "fsdp"), None),
            P(("rep", "fsdp"), None),
            P("fsdp", "rep"),
            P("fsdp", "rep"),
            P("fsdp", "rep"),
            P("fsdp", "rep"),
            P("fsdp", "rep"),
            P("fsdp", "rep"),
            P("fsdp", "rep"),
            P("fsdp", "rep"),
            P("fsdp", "rep"),
            P("fsdp", "rep"),
            P("fsdp", "rep"),
            P("fsdp", "rep"),
            P("fsdp", "rep"),
            P("fsdp", "rep"),
            P("fsdp", "rep"),
            P("fsdp", "rep"),
            P("fsdp", "rep"),
            P("fsdp", "rep"),
            P("fsdp", "rep"),
            P("fsdp", "rep"),
            P(),
        ),
        check_vma=False,
    )
```

```python
import collections
import functools

import jax
import jax.numpy as jnp
import numpy as np
from jax import lax
from jax.experimental import pallas as pl
from jax.experimental.pallas import tpu as pltpu
from jax.sharding import PartitionSpec as P

HEADS = 16
HEAD_DIM = 128
STEP = 10


beta_one = 0.9
beta_two = 0.95
rate = 0.02
rate_out = 0.08
decay = 0.1
epsilon = 1e-08


def normalize(values):
    centered = values - jnp.mean(values, axis=-1, keepdims=True)
    inverse = lax.rsqrt(jnp.mean(centered * centered, axis=-1, keepdims=True) + 1e-05)
    return (centered * inverse, inverse)


def norm_back(normed, inverse, gradient):
    first = jnp.mean(gradient, axis=-1, keepdims=True)
    second = jnp.mean(gradient * normed, axis=-1, keepdims=True)
    return inverse * (gradient - first - normed * second)


def rotate(values):
    half = values.shape[-1] // 2
    return jnp.concatenate([-values[..., half:], values[..., :half]], axis=-1)


def rotate_back(values):
    half = values.shape[-1] // 2
    return jnp.concatenate([values[..., half:], -values[..., :half]], axis=-1)


def rotary_tables(length, size):
    half = size // 2
    freqs = 10000.0 ** (-(jnp.arange(half, dtype=jnp.float32) * 2.0) / size)
    angles = jnp.arange(length, dtype=jnp.float32)[:, None] * freqs[None, :]
    cosine = jnp.concatenate([jnp.cos(angles), jnp.cos(angles)], axis=-1)[:, None, :]
    sine = jnp.concatenate([jnp.sin(angles), jnp.sin(angles)], axis=-1)[:, None, :]
    return (cosine, sine)


def group_gradient(operand, gradient):
    return lax.psum_scatter(
        lax.dot_general(
            operand, gradient, (((0,), (0,)), ((), ())), preferred_element_type=jnp.float32
        ).astype(jnp.bfloat16),
        "fsdp",
        scatter_dimension=0,
        tiled=True,
    ).astype(jnp.float32)


def adam_step(master, gradient, first, second, step_rate):
    moment = beta_one * first + (1.0 - beta_one) * gradient
    variance = beta_two * second + (1.0 - beta_two) * gradient * gradient
    update = (
        moment / (1.0 - beta_one**STEP) / (jnp.sqrt(variance / (1.0 - beta_two**STEP)) + epsilon)
    )
    updated = master - step_rate * (update + decay * master)
    return (updated, moment, variance, updated.astype(jnp.bfloat16))


def gathered_layer(
    inputs,
    cotangent,
    segment_ids,
    master_qkv,
    master_out,
    master_in,
    master_down,
    first_qkv,
    first_out,
    first_in,
    first_down,
    second_qkv,
    second_out,
    second_in,
    second_down,
):
    copies = (
        lax.all_gather(master_qkv.astype(jnp.bfloat16), "rep", axis=1, tiled=True),
        lax.all_gather(master_out.astype(jnp.bfloat16), "rep", axis=1, tiled=True),
        lax.all_gather(master_in.astype(jnp.bfloat16), "rep", axis=1, tiled=True),
        lax.all_gather(master_down.astype(jnp.bfloat16), "rep", axis=1, tiled=True),
    )

    def forward_product(operand, number):
        portion = copies[number]
        return jnp.dot(
            operand,
            lax.all_gather(portion, "fsdp", axis=0, tiled=True),
            preferred_element_type=jnp.float32,
        )

    def backward_product(gradient, number):
        return lax.dot_general(
            gradient,
            lax.all_gather(copies[number], "fsdp", axis=0, tiled=True),
            (((1,), (1,)), ((), ())),
            preferred_element_type=jnp.float32,
        )

    def weight_gradient(operand, gradient):
        return group_gradient(operand, gradient)

    length = inputs.shape[0]
    width = inputs.shape[1]
    scale = HEAD_DIM ** (-0.5)
    cosine, sine = rotary_tables(length, HEAD_DIM)
    segments = segment_ids[0]
    places = jnp.arange(length)
    allowed = (segments[:, None] == segments[None, :]) & (places[None, :] <= places[:, None])
    source = inputs.astype(jnp.float32)
    normed_one, inverse_one = normalize(source)
    lowered_one = normed_one.astype(jnp.bfloat16)
    projected = forward_product(lowered_one, 0)
    queries = projected[:, :width].reshape(length, HEADS, HEAD_DIM)
    keys = projected[:, width : 2 * width].reshape(length, HEADS, HEAD_DIM)
    values = projected[:, 2 * width :].reshape(length, HEADS, HEAD_DIM).astype(jnp.bfloat16)
    queries = (queries * cosine + rotate(queries) * sine).astype(jnp.bfloat16)
    keys = (keys * cosine + rotate(keys) * sine).astype(jnp.bfloat16)
    scores = jnp.einsum("shd,thd->hst", queries, keys, preferred_element_type=jnp.float32) * scale
    scores = jnp.where(allowed[None], scores, -1e30)
    probability = jax.nn.softmax(scores, axis=-1)
    prob_low = probability.astype(jnp.bfloat16)
    mixed = jnp.einsum("hst,thd->shd", prob_low, values, preferred_element_type=jnp.float32)
    mixed_low = mixed.reshape(length, width).astype(jnp.bfloat16)
    stream = source + forward_product(mixed_low, 1)
    normed_two, inverse_two = normalize(stream)
    lowered_two = normed_two.astype(jnp.bfloat16)
    gate_up = forward_product(lowered_two, 2)
    hidden = gate_up.shape[1] // 2
    gate = gate_up[:, :hidden]
    upper = gate_up[:, hidden:]
    sigmoid_gate = jax.nn.sigmoid(gate)
    silu_gate = gate * sigmoid_gate
    active_low = (silu_gate * upper).astype(jnp.bfloat16)
    final = stream + forward_product(active_low, 3)
    output = final.astype(jnp.bfloat16)
    summed_squares = lax.psum((jnp.sum(stream * stream), jnp.sum(final * final)), ("rep", "fsdp"))
    entries = length * width * lax.axis_size("rep") * lax.axis_size("fsdp")
    stream_rms = jnp.sqrt(jnp.stack(summed_squares) / entries)
    grad_down = weight_gradient(active_low, cotangent)
    active_grad = backward_product(cotangent, 3)
    gate_grad = active_grad * upper * sigmoid_gate * (1.0 + gate * (1.0 - sigmoid_gate))
    upper_grad = active_grad * silu_gate
    gate_up_grad = jnp.concatenate([gate_grad, upper_grad], axis=1).astype(jnp.bfloat16)
    grad_in = weight_gradient(lowered_two, gate_up_grad)
    lowered_two_grad = backward_product(gate_up_grad, 2)
    stream_grad = cotangent.astype(jnp.float32) + norm_back(
        normed_two, inverse_two, lowered_two_grad
    )
    stream_grad_low = stream_grad.astype(jnp.bfloat16)
    grad_out = weight_gradient(mixed_low, stream_grad_low)
    mixed_grad = backward_product(stream_grad_low, 1)
    mixed_grad_low = mixed_grad.reshape(length, HEADS, HEAD_DIM).astype(jnp.bfloat16)
    prob_grad = jnp.einsum(
        "shd,thd->hst", mixed_grad_low, values, preferred_element_type=jnp.float32
    )
    score_grad = probability * (
        prob_grad - jnp.sum(probability * prob_grad, axis=-1, keepdims=True)
    )
    score_grad_low = score_grad.astype(jnp.bfloat16)
    query_grad = (
        jnp.einsum("hst,thd->shd", score_grad_low, keys, preferred_element_type=jnp.float32) * scale
    )
    key_grad = (
        jnp.einsum("hst,shd->thd", score_grad_low, queries, preferred_element_type=jnp.float32)
        * scale
    )
    value_grad = jnp.einsum(
        "hst,shd->thd", prob_low, mixed_grad_low, preferred_element_type=jnp.float32
    )
    query_grad = query_grad * cosine + rotate_back(query_grad * sine)
    key_grad = key_grad * cosine + rotate_back(key_grad * sine)
    projected_grad = jnp.concatenate(
        [
            query_grad.reshape(length, width),
            key_grad.reshape(length, width),
            value_grad.reshape(length, width),
        ],
        axis=1,
    ).astype(jnp.bfloat16)
    grad_qkv = weight_gradient(lowered_one, projected_grad)
    lowered_one_grad = backward_product(projected_grad, 0)
    input_grad = (stream_grad + norm_back(normed_one, inverse_one, lowered_one_grad)).astype(
        jnp.bfloat16
    )
    summed = (
        lax.psum(grad_qkv.astype(jnp.bfloat16), "rep").astype(jnp.float32),
        lax.psum(grad_out.astype(jnp.bfloat16), "rep").astype(jnp.float32),
        lax.psum(grad_in.astype(jnp.bfloat16), "rep").astype(jnp.float32),
        lax.psum(grad_down.astype(jnp.bfloat16), "rep").astype(jnp.float32),
    )
    group = lax.axis_index("rep")
    reduced = tuple(
        (
            lax.dynamic_slice_in_dim(
                full,
                group * (full.shape[1] // lax.axis_size("rep")),
                full.shape[1] // lax.axis_size("rep"),
                1,
            )
            for full in summed
        )
    )
    updated_qkv, moment_qkv, variance_qkv, narrow_qkv = adam_step(
        master_qkv, reduced[0], first_qkv, second_qkv, rate
    )
    updated_out, moment_out, variance_out, narrow_out = adam_step(
        master_out, reduced[1], first_out, second_out, rate_out
    )
    updated_in, moment_in, variance_in, narrow_in = adam_step(
        master_in, reduced[2], first_in, second_in, rate
    )
    updated_down, moment_down, variance_down, narrow_down = adam_step(
        master_down, reduced[3], first_down, second_down, rate
    )
    return (
        output,
        input_grad,
        reduced[0],
        reduced[1],
        reduced[2],
        reduced[3],
        updated_qkv,
        updated_out,
        updated_in,
        updated_down,
        moment_qkv,
        moment_out,
        moment_in,
        moment_down,
        variance_qkv,
        variance_out,
        variance_in,
        variance_down,
        narrow_qkv,
        narrow_out,
        narrow_in,
        narrow_down,
        stream_rms,
    )


ALL = ("rep", "fsdp")
MASK_Y, MASK_C, MASK_HI, MASK_E, MASK_T = 16, 8, 4, 2, 1
DEVICES = 32
ROWS = 256
FULL = jnp.float32
LOW = jnp.bfloat16


def swap(values, mask):
    return lax.ppermute(values, ALL, [(i, i ^ mask) for i in range(DEVICES)])


def half(values, axis, bit):
    size = values.shape[axis] // 2
    return lax.dynamic_slice_in_dim(values, bit * size, size, axis)


class Steps:
    def __init__(self):
        self.last = ()

    def do(self, work, *values):
        values, _ = lax.optimization_barrier((values, self.last))
        result = work(*values)
        self.last = (jax.tree.leaves(result)[0],)
        return result

    def wait(self, value):
        return self.do(lambda v: v, value)


def columns(values, starts, width):
    return jnp.concatenate(
        [lax.dynamic_slice_in_dim(values, start, width, 1) for start in starts], axis=1
    )


def in_order(bit, mine, other, axis):
    first = jnp.where(bit == 0, mine, other)
    second = jnp.where(bit == 0, other, mine)
    return jnp.concatenate([first, second], axis=axis)


def dot(left, right):
    return jnp.dot(left, right, preferred_element_type=FULL)


def dot_back(left, right):
    return lax.dot_general(left, right, (((1,), (1,)), ((), ())), preferred_element_type=FULL)


def dot_tokens(left, right):
    return lax.dot_general(left, right, (((0,), (0,)), ((), ())), preferred_element_type=FULL)


def low_dot_tokens(left, right):
    return dot_tokens(left, right).astype(LOW)


class Tokens:
    def __init__(self, values):
        self.values = values

    def send_y(self, steps):
        self.from_y = swap(steps.wait(self.values), MASK_Y)

    def send_t(self, steps):
        self.from_t = swap(steps.wait(self.values), MASK_T)

    def send(self, steps):
        self.values = steps.wait(self.values)
        self.from_y = swap(self.values, MASK_Y)
        self.from_t = swap(self.values, MASK_T)

    def second(self, steps):
        cut = ROWS // 2

        def parts(from_t, from_y):
            upper = from_t[:cut]
            if from_t.shape[0] > ROWS:
                upper = jnp.concatenate([upper, from_t[ROWS:]], axis=0)
            return upper, from_y[cut:ROWS]

        upper, lower = steps.do(parts, self.from_t, self.from_y)
        self.upper = swap(upper, MASK_Y)
        self.lower = swap(lower, MASK_T)

    def rows(self, steps):
        cut = ROWS // 2
        return steps.do(
            functools.partial(join_rows, (ROWS, ROWS, cut, cut, ROWS)),
            self.values,
            self.from_y,
            self.upper,
            self.lower,
            self.from_t,
        )


class Sum:
    def __init__(self, product, *values):
        self.product = product
        self.values = values

    def first(self, steps):
        self.first_y(steps)
        self.first_t(steps)

    def first_y(self, steps):
        self.give_y = steps.do(lambda *v: self.product((1, 2), 0, LOW, *v), *self.values)

    def first_t(self, steps):
        self.give_t = steps.do(lambda *v: self.product((2, 3), 1, LOW, *v), *self.values)

    def release(self, steps):
        self.give_y, self.give_t = steps.do(lambda *v: v, self.give_y, self.give_t)

    def send(self):
        self.got_y = swap(self.give_y, MASK_Y)
        self.got_t = swap(self.give_t, MASK_T)

    def own(self, steps):
        self.mine = steps.do(
            lambda *v: (self.product((0, 3), 0, FULL, *v), self.product((0, 1), 1, FULL, *v)),
            *self.values,
        )

    def second(self, steps):
        give_t, give_y = steps.do(
            lambda got_y, got_t, side_0, side_1: (
                (side_0[ROWS:] + got_y[ROWS:].astype(FULL)).astype(LOW),
                (side_1[ROWS:] + got_t[:ROWS].astype(FULL)).astype(LOW),
            ),
            self.got_y,
            self.got_t,
            *self.mine,
        )
        self.last_t = swap(give_t, MASK_T)
        self.last_y = swap(give_y, MASK_Y)

    def total(self, side_0, side_1, got_y, got_t, last_t, last_y):
        return (
            side_0[:ROWS] + got_y[:ROWS].astype(FULL) + last_t.astype(FULL),
            side_1[:ROWS] + got_t[ROWS:].astype(FULL) + last_y.astype(FULL),
        )

    def parts(self):
        return (*self.mine, self.got_y, self.got_t, self.last_t, self.last_y)


GROUPS = [
    [16 * y + 8 * c + 4 * hi + 2 * e + t for c in (0, 1) for hi in (0, 1) for e in (0, 1)]
    for y in (0, 1)
    for t in (0, 1)
]


class Gather:
    def __init__(self, steps, work, *values):
        piece = steps.do(work, *values)
        self.size = piece.shape[0]
        self.whole = lax.all_gather(piece, ALL, axis=0, tiled=True, axis_index_groups=GROUPS)

    def parts(self, rows, first=0):
        return [Part(self.whole, self.size, rows, first, AT_NUMBERS + at) for at in range(8)]


Part = collections.namedtuple("Part", ("array", "size", "rows", "first", "base"))


def part_block(part, rows, width, place):
    def index(i, scalars):
        row, column = place(i, scalars)
        return (scalars[part.base] * (part.size // rows) + part.first // rows + row, column)

    return pl.BlockSpec((rows, width), index)


QUARTETS = [
    [16 * y + 8 * c + 4 * hi + 2 * e + t for hi in (0, 1) for e in (0, 1)]
    for y in (0, 1)
    for c in (0, 1)
    for t in (0, 1)
]


class Scatter:
    def __init__(self, product, *values):
        self.product, self.values = product, values

    def core(self, steps):
        self.from_core = swap(
            steps.do(functools.partial(self.product, 1), *self.values), MASK_C
        )

    def send(self, steps):
        self.result = lax.psum_scatter(
            steps.do(functools.partial(self.product, 0), *self.values, self.from_core),
            ALL,
            scatter_dimension=0,
            tiled=True,
            axis_index_groups=QUARTETS,
        )


VMEM_LIMIT = 56 * 2**20


def compiler_params():
    return pltpu.CompilerParams(vmem_limit_bytes=VMEM_LIMIT)


def fixed(shape):
    return pl.BlockSpec(shape, lambda i, *_: (0, 0), pipeline_mode=pl.Buffered(1))


TILE = 256


def join_kernel(*refs):
    at = 0
    for ref in refs[:-1]:
        rows = ref.shape[0]
        refs[-1][at : at + rows, :] = ref[...]
        at += rows


def join_rows(sizes, *parts):
    width = parts[0].shape[1]
    tile = width // 4
    rows = sum(sizes)
    return pl.pallas_call(
        join_kernel,
        grid=(4,),
        in_specs=[pl.BlockSpec((size, tile), lambda i: (0, i)) for size in sizes],
        out_specs=pl.BlockSpec((rows, tile), lambda i: (0, i)),
        out_shape=jax.ShapeDtypeStruct((rows, width), parts[0].dtype),
        compiler_params=compiler_params(),
        cost_estimate=cost(0, 4 * rows * width),
    )(*parts)


def heads_kernel(scalars, rows, gradient, mixed, stream, *refs):
    out = refs[-1]
    width = gradient.shape[1]
    total = dot_tokens(rows[...], gradient[...])
    weight = dot_tokens(mixed[...], stream[...])
    if len(refs) == 2:
        total = total + refs[0][:, :width].astype(FULL)
    out[:, :width] = total.astype(LOW)
    rest = out.shape[1] - width
    for at in range(4):
        part = weight[:, at * rest : (at + 1) * rest]
        place = slice(at * HEAD_DIM, (at + 1) * HEAD_DIM)
        if len(refs) == 2:
            part = part + refs[0][place, width:].astype(FULL)
        out[place, width:] = part.astype(LOW)


def scatter_heads(scalars, side, rows, gradient, mixed, stream, *adds):
    tokens, depth = rows.shape
    block, width = depth // 4, gradient.shape[1] // 2
    middle = stream.shape[1] // 2
    out = pl.BlockSpec((block, middle), lambda i, s: (s[AT_FOURTHS + i], 0))

    def side_of(size):
        return pl.BlockSpec((tokens, size), lambda i, s: (0, side), pipeline_mode=pl.Buffered(1))

    return pl.pallas_call(
        heads_kernel,
        grid_spec=pltpu.PrefetchScalarGridSpec(
            num_scalar_prefetch=1,
            grid=(4,),
            in_specs=[
                pl.BlockSpec((tokens, block), lambda i, s: (0, i)),
                side_of(width),
                pl.BlockSpec((tokens, HEAD_DIM), lambda i, s: (0, s[i])),
                side_of(middle),
            ]
            + [out] * len(adds),
            out_specs=out,
        ),
        out_shape=jax.ShapeDtypeStruct((depth, middle), LOW),
        compiler_params=compiler_params(),
        cost_estimate=cost(8 * tokens * block * middle, 2 * tokens * (depth + 2 * middle)),
    )(scalars, rows, gradient, mixed, stream, *adds)


def scatter_kernel(scalars, operand, gradient, *refs):
    total = dot_tokens(operand[...], gradient[...])
    for ref in refs[:-1]:
        total = total + ref[...].astype(FULL)
    refs[-1][...] = total.astype(refs[-1].dtype)


def scatter_blocks(scalars, placed, side, operand, gradient, *adds):
    tokens, depth = operand.shape
    block, width = depth // 4, gradient.shape[1] // 2
    out = pl.BlockSpec((block, width), lambda i, s: (s[AT_FOURTHS + i], 0))
    return pl.pallas_call(
        scatter_kernel,
        grid_spec=pltpu.PrefetchScalarGridSpec(
            num_scalar_prefetch=1,
            grid=(4,),
            in_specs=[
                pl.BlockSpec((tokens, block), lambda i, s: (0, s[i] if placed else i)),
                pl.BlockSpec(
                    (tokens, width), lambda i, s: (0, side), pipeline_mode=pl.Buffered(1)
                ),
            ]
            + [out] * len(adds),
            out_specs=out,
        ),
        out_shape=jax.ShapeDtypeStruct((4 * block, width), LOW),
        compiler_params=compiler_params(),
        cost_estimate=cost(
            8 * tokens * block * width, 2 * (4 * tokens * block + tokens * width + 8 * block * width)
        ),
    )(scalars, operand, gradient, *adds)


COST_SHARE = 1.0


def cost(flops, size, transcendentals=0):
    return pl.CostEstimate(
        flops=int(COST_SHARE * flops),
        bytes_accessed=int(COST_SHARE * size),
        transcendentals=int(COST_SHARE * transcendentals),
    )


def piece_sum(rows, pieces):
    depth = pieces[0].shape[0]
    total = dot(rows[:, :depth], pieces[0][...])
    for at in range(1, len(pieces)):
        total = total + dot(rows[:, at * depth : (at + 1) * depth], pieces[at][...])
    return total


PIECE = 2 * ROWS


def part_tiles(part, side, tiles):
    return part_block(
        part, part.rows, TILE, lambda i, _: (0, jnp.clip(i - side * tiles, 0, tiles - 1))
    )


AT_Y, AT_NUMBERS, AT_FOURTHS, AT_T, AT_HEADS = 4, 5, 13, 17, 18


def divided_sum(scalars, rows, pieces):
    total = 0.0
    for at, piece in enumerate(pieces):
        start = pl.multiple_of((at - at % 2 + (scalars[AT_T] ^ (at % 2))) * ROWS, ROWS)
        total = total + dot(rows[:, pl.ds(start, ROWS)], piece[...])
    return total


def pieces_kernel(tiles, scalars, rows, *refs):
    for side in range(2):

        @pl.when(pl.program_id(0) // tiles == side)
        def _(side=side):
            refs[8][...] = piece_sum(rows, refs[4 * side : 4 * side + 4])


def product_pieces(parts, width, scalars, rows, *arrays):
    tokens, depth = rows.shape
    tiles = width // TILE
    return pl.pallas_call(
        functools.partial(pieces_kernel, tiles),
        grid_spec=pltpu.PrefetchScalarGridSpec(
            num_scalar_prefetch=1,
            grid=(2 * tiles,),
            in_specs=[fixed(rows.shape)]
            + [part_tiles(part, at // 4, tiles) for at, part in enumerate(parts)],
            out_specs=pl.BlockSpec((tokens, TILE), lambda i, *_: (0, i)),
        ),
        out_shape=jax.ShapeDtypeStruct((tokens, 2 * width), FULL),
        compiler_params=compiler_params(),
        cost_estimate=cost(4 * tokens * depth * width, 2 * depth * (tokens + 2 * width)),
    )(scalars, rows, *arrays)


def heads_join_kernel(scalars, piece, out):
    for at in range(4):
        out[:, at * TILE : (at + 1) * TILE] = piece[at * HEAD_DIM : (at + 1) * HEAD_DIM, :]


def join_heads(scalars, whole):
    return pl.pallas_call(
        heads_join_kernel,
        grid_spec=pltpu.PrefetchScalarGridSpec(
            num_scalar_prefetch=1,
            grid=(8,),
            in_specs=[pl.BlockSpec((PIECE, TILE), lambda i, s: (s[AT_HEADS + i], 3))],
            out_specs=pl.BlockSpec((HEAD_DIM, 4 * TILE), lambda i, s: (i % 4, i // 4)),
        ),
        out_shape=jax.ShapeDtypeStruct((4 * HEAD_DIM, 8 * TILE), LOW),
        compiler_params=compiler_params(),
        cost_estimate=cost(0, 16 * PIECE * TILE * 2),
    )(scalars, whole)


def unit_kernel(tiles, scalars, rows, *refs):
    gate, upper, active = refs[32:]
    for side in range(2):

        @pl.when(pl.program_id(0) // tiles == side)
        def _(side=side):
            a = divided_sum(scalars, rows, refs[16 * side : 16 * side + 8])
            b = piece_sum(rows, refs[16 * side + 8 : 16 * side + 16])
            gated = jnp.where(scalars[AT_Y] == 0, a, b)
            raised = jnp.where(scalars[AT_Y] == 0, b, a)
            gate[...] = gated.astype(LOW)
            upper[...] = raised.astype(LOW)
            active[...] = (gated * jax.nn.sigmoid(gated) * raised).astype(LOW)


def unit_forward(parts, scalars, rows, *arrays):
    tokens, depth = rows.shape
    width = arrays[0].shape[1]
    tiles = width // TILE
    in_specs = [fixed(rows.shape)]
    in_specs += [part_tiles(part, at // 16, tiles) for at, part in enumerate(parts)]
    out = pl.BlockSpec((tokens, TILE), lambda i, *_: (0, i))
    shape = jax.ShapeDtypeStruct((tokens, 2 * width), LOW)
    return pl.pallas_call(
        functools.partial(unit_kernel, tiles),
        grid_spec=pltpu.PrefetchScalarGridSpec(
            num_scalar_prefetch=1,
            grid=(2 * tiles,),
            in_specs=in_specs,
            out_specs=[out, out, out],
        ),
        out_shape=[shape, shape, shape],
        compiler_params=compiler_params(),
        cost_estimate=cost(
            8 * tokens * depth * width, 2 * depth * (tokens + 4 * width) + 12 * tokens * width
        ),
    )(scalars, rows, *arrays)


def unit_back_kernel(scalars, own, other, *refs):
    gate, upper, grad_a, grad_b = refs[8:]
    for at in range(4):

        @pl.when(pl.program_id(0) // 2 == at)
        def _(at=at):
            grad = dot_back(own[...], refs[at][...]) + dot_back(other[...], refs[4 + at][...])
            gated, raised = gate[...].astype(FULL), upper[...].astype(FULL)
            sigmoid = jax.nn.sigmoid(gated)
            gate_grad = grad * raised * sigmoid * (1.0 + gated * (1.0 - sigmoid))
            upper_grad = grad * (gated * sigmoid)
            grad_a[...] = jnp.where(scalars[AT_Y] == 0, gate_grad, upper_grad).astype(LOW)
            grad_b[...] = jnp.where(scalars[AT_Y] == 0, upper_grad, gate_grad).astype(LOW)


def unit_back(parts, scalars, rows, gate, upper, *arrays):
    tokens, depth = rows.shape
    units = gate.shape[1]
    cut = depth // 2
    shape = jax.ShapeDtypeStruct((tokens, units), LOW)
    out = pl.BlockSpec((tokens, TILE), lambda i, scalars: (0, 2 * scalars[i // 2] + i % 2))

    def half_rows(at):
        return pl.BlockSpec((tokens, cut), lambda i, *_: (0, at), pipeline_mode=pl.Buffered(1))

    def units_of(at, part):
        return part_block(part, TILE, cut, lambda i, _: (jnp.clip(i - 2 * (at % 4), 0, 1), 0))

    return pl.pallas_call(
        unit_back_kernel,
        grid_spec=pltpu.PrefetchScalarGridSpec(
            num_scalar_prefetch=1,
            grid=(8,),
            in_specs=[half_rows(0), half_rows(1)] + [units_of(at, part) for at, part in enumerate(parts)] + [out, out],
            out_specs=[out, out],
        ),
        out_shape=[shape, shape],
        compiler_params=compiler_params(),
        cost_estimate=cost(
            2 * tokens * depth * units, 2 * depth * (tokens + units) + 8 * tokens * units
        ),
    )(scalars, rows, rows, *arrays, gate, upper)


def chunk_rows(left, chunk, width, place):
    return pl.BlockSpec(
        (ROWS, width), lambda i, scalars: (chunk, place(scalars)), pipeline_mode=pl.Buffered(1)
    )


def back_kernel(chunks, counts, _, *refs):
    terms = len(counts)
    lefts, rights, out = refs[: chunks * terms], refs[chunks * terms : -1], refs[-1]
    for step in range(4):

        @pl.when(pl.program_id(0) == step)
        def _(step=step):
            for chunk in range(chunks):
                total, first = 0.0, 0
                for term, count in enumerate(counts):
                    right = rights[first + step * count // 4]
                    total = total + dot_back(lefts[chunk * terms + term][...], right[...])
                    first += count
                out[chunk * ROWS : (chunk + 1) * ROWS, :] = total.astype(out.dtype)


def product_back(scalars, chunks, dtype, terms):
    in_specs, values = [], []
    for chunk in chunks:
        for left, at, _ in terms:
            in_specs.append(chunk_rows(left, chunk, left.shape[1] // 2, lambda s, at=at: at))
            values.append(left)
    depth = 0
    for left, _, parts in terms:
        size = left.shape[1] // 2
        depth += size
        for part in parts:
            if len(parts) == 4:
                spec = part_block(part, ROWS, size, lambda i, s: (0, 0))
            else:
                spec = part_block(part, ROWS, size, lambda i, s: (s[AT_T] ^ (i % 2), 0))
            in_specs.append(spec)
            values.append(part.array)
    rows, width = len(chunks) * ROWS, 4 * TILE
    counts = [len(parts) for _, _, parts in terms]
    return pl.pallas_call(
        functools.partial(back_kernel, len(chunks), counts),
        grid_spec=pltpu.PrefetchScalarGridSpec(
            num_scalar_prefetch=1,
            grid=(4,),
            in_specs=in_specs,
            out_specs=pl.BlockSpec(
                (rows, TILE), lambda i, s: (0, i - i % 2 + (s[AT_T] ^ (i % 2)))
            ),
        ),
        out_shape=jax.ShapeDtypeStruct((rows, width), dtype),
        compiler_params=compiler_params(),
        cost_estimate=cost(2 * rows * depth * width, 2 * depth * (rows + width) + 4 * rows * width),
    )(scalars, *values)


def forward_kernel(chunks, _, *refs):
    lefts, rights, out = refs[: chunks * 4], refs[chunks * 4 : -1], refs[-1]
    for chunk in range(chunks):
        total = dot(lefts[4 * chunk][...], rights[0][...])
        for at in range(1, 4):
            total = total + dot(lefts[4 * chunk + at][...], rights[at][...])
        out[chunk * ROWS : (chunk + 1) * ROWS, :] = total.astype(out.dtype)


def product_forward(chunks, dtype, parts, scalars, left, *arrays):
    depth, width = PIECE, arrays[0].shape[1]
    in_specs = [
        chunk_rows(left, chunk, depth, lambda scalars, at=at: scalars[at])
        for chunk in chunks
        for at in range(4)
    ] + [part_block(part, PIECE, TILE, lambda i, _: (0, i)) for part in parts]
    rows = len(chunks) * ROWS
    return pl.pallas_call(
        functools.partial(forward_kernel, len(chunks)),
        grid_spec=pltpu.PrefetchScalarGridSpec(
            num_scalar_prefetch=1,
            grid=(width // TILE,),
            in_specs=in_specs,
            out_specs=pl.BlockSpec((rows, TILE), lambda i, *_: (0, i)),
        ),
        out_shape=jax.ShapeDtypeStruct((rows, width), dtype),
        compiler_params=compiler_params(),
        cost_estimate=cost(
            8 * rows * depth * width, 8 * depth * (rows + width) + 4 * rows * width
        ),
    )(scalars, *([left] * (4 * len(chunks))), *arrays)


def signed_tables():
    cosine, sine = rotary_tables(ROWS, HEAD_DIM)
    sign = jnp.concatenate(
        [-jnp.ones((HEAD_DIM // 2,), FULL), jnp.ones((HEAD_DIM // 2,), FULL)]
    )
    return (cosine[:, 0, :], sine[:, 0, :] * sign)


SCALE = HEAD_DIM ** (-0.5)
GROUP_HEADS = 4
GROUP_WIDTH = GROUP_HEADS * HEAD_DIM


def softmax_rows(query, key, allowed):
    scores = dot_back(query, key) * SCALE
    scores = jnp.where(allowed, scores, -1e30)
    weights = jnp.exp(scores - jnp.max(scores, axis=-1, keepdims=True))
    return weights / jnp.sum(weights, axis=-1, keepdims=True)


SIDE_WIDTH = 6 * HEAD_DIM


def head_columns(side, which, head):
    start = side * SIDE_WIDTH + (2 * which + head) * HEAD_DIM
    return slice(start, start + HEAD_DIM)


def mixed_columns(side, head):
    start = (2 * side + head) * HEAD_DIM
    return slice(start, start + HEAD_DIM)


def attend_kernel(projected, mask, cosine, sine, lowered, mixed):
    allowed = mask[...] > 0.0
    cos, sin = cosine[...], sine[...]
    for side in range(2):
        for head in range(2):

            def rope(which):
                values = projected[:, head_columns(side, which, head)]
                return (values * cos + pltpu.roll(values, HEAD_DIM // 2, 1) * sin).astype(LOW)

            query, key = rope(0), rope(1)
            value = projected[:, head_columns(side, 2, head)].astype(LOW)
            probability = softmax_rows(query, key, allowed)
            lowered[:, head_columns(side, 0, head)] = query
            lowered[:, head_columns(side, 1, head)] = key
            lowered[:, head_columns(side, 2, head)] = value
            mixed[:, mixed_columns(side, head)] = dot(probability.astype(LOW), value).astype(LOW)


def attend_back_kernel(lowered, mask, cosine, sine, mixed_grad, projected_grad):
    allowed = mask[...] > 0.0
    cos, sin = cosine[...], sine[...]
    for side in range(2):
        for head in range(2):
            query = lowered[:, head_columns(side, 0, head)]
            key = lowered[:, head_columns(side, 1, head)]
            value = lowered[:, head_columns(side, 2, head)]
            grad = mixed_grad[:, mixed_columns(side, head)]
            probability = softmax_rows(query, key, allowed)
            prob_grad = dot_back(grad, value)
            inner = jnp.sum(probability * prob_grad, axis=-1, keepdims=True)
            score_grad = (probability * (prob_grad - inner)).astype(LOW)
            query_grad = dot(score_grad, key) * SCALE
            key_grad = dot_tokens(score_grad, query) * SCALE
            value_grad = dot_tokens(probability.astype(LOW), grad)

            def unrope(values):
                return (values * cos - pltpu.roll(values, HEAD_DIM // 2, 1) * sin).astype(LOW)

            projected_grad[:, head_columns(side, 0, head)] = unrope(query_grad)
            projected_grad[:, head_columns(side, 1, head)] = unrope(key_grad)
            projected_grad[:, head_columns(side, 2, head)] = value_grad.astype(LOW)


def row_block(width):
    return pl.BlockSpec((ROWS, width), lambda i: (i, 0))


def whole_block(width):
    return pl.BlockSpec((ROWS, width), lambda i: (0, 0))


def attend(projected, mask, cosine, sine):
    rows = projected.shape[0]
    return pl.pallas_call(
        attend_kernel,
        grid=(rows // ROWS,),
        in_specs=[
            row_block(2 * SIDE_WIDTH),
            row_block(ROWS),
            whole_block(HEAD_DIM),
            whole_block(HEAD_DIM),
        ],
        out_specs=[row_block(2 * SIDE_WIDTH), row_block(GROUP_WIDTH)],
        out_shape=[
            jax.ShapeDtypeStruct((rows, 2 * SIDE_WIDTH), LOW),
            jax.ShapeDtypeStruct((rows, GROUP_WIDTH), LOW),
        ],
        compiler_params=compiler_params(),
        cost_estimate=cost(
            4 * rows * ROWS * GROUP_WIDTH, rows * GROUP_WIDTH * 20, rows * ROWS * GROUP_HEADS
        ),
    )(projected, mask, cosine, sine)


def attend_back(lowered, mask, cosine, sine, mixed_grad):
    rows = lowered.shape[0]
    return pl.pallas_call(
        attend_back_kernel,
        grid=(rows // ROWS,),
        in_specs=[
            row_block(2 * SIDE_WIDTH),
            row_block(ROWS),
            whole_block(HEAD_DIM),
            whole_block(HEAD_DIM),
            row_block(GROUP_WIDTH),
        ],
        out_specs=row_block(2 * SIDE_WIDTH),
        out_shape=jax.ShapeDtypeStruct((rows, 2 * SIDE_WIDTH), LOW),
        compiler_params=compiler_params(),
        cost_estimate=cost(
            10 * rows * ROWS * GROUP_WIDTH, rows * GROUP_WIDTH * 14, rows * ROWS * GROUP_HEADS
        ),
    )(lowered, mask, cosine, sine, mixed_grad)


def split_layer(
    inputs,
    cotangent,
    segment_ids,
    master_qkv,
    master_out,
    master_in,
    master_down,
    first_qkv,
    first_out,
    first_in,
    first_down,
    second_qkv,
    second_out,
    second_in,
    second_down,
):
    rep, fsdp = lax.axis_index("rep"), lax.axis_index("fsdp")
    y, c = rep // 2, rep % 2
    hi, e, t = fsdp // 4, (fsdp // 2) % 2, fsdp % 2
    width = inputs.shape[1]
    middle = width // 2
    unit = width // 4
    pair = 2 * HEAD_DIM
    pairs = master_qkv.shape[1] // pair
    block = pairs * HEAD_DIM
    steps = Steps()

    def relative(values):
        starts = [
            4 * (hi ^ at_hi) + 2 * (e ^ at_e) + at_t
            for at_e in (0, 1)
            for at_hi in (0, 1)
            for at_t in (0, 1)
        ]
        return columns(values, [start * ROWS for start in starts], ROWS)

    def natural(values):
        starts = [
            4 * (e ^ at_e) + 2 * (hi ^ at_hi) + at_t
            for at_hi in (0, 1)
            for at_e in (0, 1)
            for at_t in (0, 1)
        ]
        return columns(values, [start * ROWS for start in starts], ROWS)

    def core_first(values):
        return columns(values, [c * unit, (2 + c) * unit, (1 - c) * unit, (3 - c) * unit], unit)

    def core_natural(own, other):
        even, odd = jnp.where(c == 0, own, other), jnp.where(c == 0, other, own)
        return jnp.concatenate(
            [even[:, :unit], odd[:, :unit], even[:, unit:], odd[:, unit:]], axis=1
        )

    places = [2 * ((hi ^ at_hi) ^ c) + (e ^ at_e) for at_e in (0, 1) for at_hi in (0, 1)]
    numbers = [
        4 * (c ^ at_c) + 2 * (hi ^ at_hi) + (e ^ at_e)
        for at_c in (0, 1)
        for at_e in (0, 1)
        for at_hi in (0, 1)
    ]
    fourths = [2 * (hi ^ at_hi) + (e ^ at_e) for at_e in (0, 1) for at_hi in (0, 1)]
    heads = [
        4 * (c ^ at_c) + 2 * (at_hi ^ c) + at_e
        for at_c in (0, 1)
        for at_hi in (0, 1)
        for at_e in (0, 1)
    ]
    scalars = jnp.stack([*places, y, *numbers, *fourths, t, *heads]).astype(jnp.int32)

    def in_rows(mine, other):
        return in_order(t, mine, other, 0)

    def in_columns(mine, other):
        return in_order(y, mine, other, 1)

    def split_pairs(weight):
        low = weight.astype(LOW)
        return (
            columns(low, [j * pair + (1 - y) * HEAD_DIM for j in range(pairs)], HEAD_DIM),
            columns(low, [j * pair + y * HEAD_DIM for j in range(pairs)], HEAD_DIM),
        )

    def all_pairs(mine, theirs):
        even, odd = jnp.where(c == 0, mine, theirs), jnp.where(c == 0, theirs, mine)
        whole = jnp.concatenate(
            [even[:, :block], odd[:, :block], even[:, block:], odd[:, block:]], axis=1
        )

        def part(t_bit):
            starts = [8 * j + 4 * c + 2 * k + t_bit for j in range(3) for k in range(2)]
            return columns(whole, [start * HEAD_DIM for start in starts], HEAD_DIM)

        return part(1 - t), part(t)

    def split_rows(weight):
        low = weight.astype(LOW)
        return half(low, 0, 1 - y), half(low, 0, y)

    def unit_columns(low, t_bit, y_bit):
        return columns(low, [(4 * j + 2 * t_bit + y_bit) * unit for j in range(2)], unit)

    def split_in(weight):
        low = weight.astype(LOW)
        return (
            unit_columns(low, 1 - t, y),
            jnp.concatenate(
                [unit_columns(low, 1 - t, 1 - y), unit_columns(low, t, 1 - y)], axis=1
            ),
        )

    def norm_low(values, ids):
        normed, inverse = normalize(values.astype(FULL))
        extra = jnp.tile(ids.astype(LOW), (16, width // ROWS))
        return jnp.concatenate([relative(normed.astype(LOW)), extra], axis=0), inverse

    def attention_piece(kept, got, out_kept, out_y):
        rows = in_columns(out_kept, out_y)
        stacked = jnp.concatenate(
            [rows[:, j * pair : (j + 1) * pair] for j in range(width // 2 // pair)], axis=0
        )
        return jnp.concatenate([in_rows(kept, got), stacked], axis=1)

    def other_piece(in_t, in_y, in_b_t):
        return jnp.concatenate([in_t, in_rows(in_y[:, middle:], in_b_t)], axis=0)

    a_own = Gather(steps, lambda v: unit_columns(v, t, y).astype(LOW), master_in)
    given, kept = steps.do(split_pairs, master_qkv)
    pairs_y = swap(given, MASK_Y)
    give_t, give_y = steps.do(split_in, master_in)
    lowered_one, inverse_one = steps.do(norm_low, inputs, segment_ids)
    given, out_kept = steps.do(split_rows, master_out)
    pairs_mine = steps.do(in_columns, kept, pairs_y)
    pairs_core = swap(pairs_mine, MASK_C)
    out_y = swap(given, MASK_Y)
    tokens_one = Tokens(lowered_one)
    tokens_one.send_y(steps)
    given, pairs_kept = steps.do(all_pairs, pairs_mine, pairs_core)
    pairs_t = swap(given, MASK_T)
    give_down, down_kept = steps.do(split_rows, master_down)
    qkv = Gather(steps, attention_piece, pairs_kept, pairs_t, out_kept, out_y)
    tokens_one.from_y = steps.wait(tokens_one.from_y)
    tokens_one.send_t(steps)
    a_own.whole = steps.wait(a_own.whole)
    in_y = swap(steps.wait(give_y), MASK_Y)
    tokens_one.second(steps)
    in_t = swap(steps.wait(give_t), MASK_T)
    in_y = steps.wait(in_y)
    in_b_t = swap(steps.do(lambda v: v[:, :middle], in_y), MASK_T)
    down_y = swap(steps.wait(give_down), MASK_Y)
    rows_one = tokens_one.rows(steps)

    def attention_mask(own, from_y, from_t, upper):
        segments = jnp.stack(
            [own[ROWS], from_y[ROWS], upper[ROWS // 2], from_t[ROWS]], axis=0
        )[:, :ROWS]
        at = jnp.arange(ROWS)
        allowed = (segments[:, :, None] == segments[:, None, :]) & (at[None, :] <= at[:, None])
        return allowed.astype(FULL).reshape(4 * ROWS, ROWS)

    mask = steps.do(
        attention_mask, tokens_one.values, tokens_one.from_y, tokens_one.from_t, tokens_one.upper
    )
    cosine, sine = signed_tables()
    a_b = Gather(steps, other_piece, in_t, in_y, in_b_t)
    down = Gather(steps, in_columns, down_kept, down_y)
    qkv_parts = qkv.parts(PIECE)
    qkv_arrays = [part.array for part in qkv_parts]
    projected = steps.do(
        functools.partial(product_pieces, qkv_parts, 3 * pair, scalars), rows_one, *qkv_arrays
    )
    lowered, mixed_low = steps.do(attend, projected, mask, cosine, sine)

    weight_out = steps.do(functools.partial(join_heads, scalars), qkv.whole)

    def product_out(chunks, side, dtype, operand, weight):
        right = weight[:, side * middle : (side + 1) * middle]
        if chunks[0] + 1 == chunks[1]:
            left = operand[chunks[0] * ROWS : (chunks[1] + 1) * ROWS]
            return dot(left, right).astype(dtype)
        parts = [dot(operand[at * ROWS : (at + 1) * ROWS], right) for at in chunks]
        return jnp.concatenate(parts, axis=0).astype(dtype)

    sum_out = Sum(product_out, mixed_low, weight_out)
    sum_out.first(steps)
    sum_out.send()
    sum_out.own(steps)
    sum_out.second(steps)

    def norm_stream(values, *parts):
        stream = values.astype(FULL) + core_natural(*sum_out.total(*parts))
        normed, inverse = normalize(stream)
        return relative(normed.astype(LOW)), stream, inverse

    lowered_two, stream, inverse_two = steps.do(norm_stream, inputs, *sum_out.parts())
    tokens_two = Tokens(lowered_two)
    tokens_two.send(steps)
    tokens_two.second(steps)
    rows_two = tokens_two.rows(steps)
    tokens_cotangent = Tokens(steps.do(core_first, cotangent))
    tokens_cotangent.send(steps)

    own_a, other_a = a_own.parts(ROWS), a_b.parts(ROWS)
    even_b, odd_b = a_b.parts(ROWS, ROWS), a_b.parts(ROWS, 2 * ROWS)

    def in_turn(first, second, side):
        at = slice(4 * side, 4 * side + 4)
        return [part for two in zip(first[at], second[at]) for part in two]

    in_parts = [
        part
        for side in (0, 1)
        for kind in ((own_a, other_a), (even_b, odd_b))
        for part in in_turn(*kind, side)
    ]
    in_arrays = [part.array for part in in_parts]
    gate, upper, active = steps.do(
        functools.partial(unit_forward, in_parts, scalars), rows_two, *in_arrays
    )
    tokens_cotangent.second(steps)
    rows_cotangent = tokens_cotangent.rows(steps)
    placed_blocks = functools.partial(scatter_blocks, scalars, True)
    piece_blocks = functools.partial(scatter_blocks, scalars, False)
    scatter_down = Scatter(placed_blocks, active, rows_cotangent)
    scatter_down.core(steps)
    scatter_down.send(steps)
    down_parts = down.parts(PIECE)
    down_arrays = [part.array for part in down_parts]

    grad_a, grad_b = steps.do(
        functools.partial(unit_back, down_parts, scalars), rows_cotangent, gate, upper, *down_arrays
    )

    def placed_parts(parts, arrays):
        return [part._replace(array=array) for part, array in zip(parts, arrays)]

    def product_units(chunks, side, dtype, grad_a, grad_b, *arrays):
        parts = placed_parts(in_parts, arrays)
        terms = []
        for core in (0, 1):
            at = 16 * core + 4 * side
            whole_b = [part._replace(rows=PIECE) for part in parts[at + 8 : at + 12 : 2]]
            terms += [(grad_a, core, parts[at : at + 4]), (grad_b, core, whole_b)]
        return product_back(scalars, chunks, dtype, terms)

    sum_two = Sum(product_units, grad_a, grad_b, *in_arrays)
    sum_two.first(steps)
    sum_two.send()
    scatter_a = Scatter(piece_blocks, rows_two, grad_a)
    scatter_a.core(steps)
    sum_two.own(steps)
    scatter_a.send(steps)
    sum_two.second(steps)
    scatter_b = Scatter(piece_blocks, rows_two, grad_b)
    scatter_b.core(steps)

    def stream_back(grad, stream, inverse, *parts):
        normed = (stream - jnp.mean(stream, axis=-1, keepdims=True)) * inverse
        total = natural(jnp.concatenate(sum_two.total(*parts), axis=1))
        result = grad.astype(FULL) + norm_back(normed, inverse, total)
        return core_first(result.astype(LOW)), result

    stream_grad_low, stream_grad = steps.do(
        stream_back, cotangent, stream, inverse_two, *sum_two.parts()
    )
    tokens_stream = Tokens(stream_grad_low)
    tokens_stream.send(steps)
    scatter_b.send(steps)

    def product_final(chunks, side, dtype, active, *arrays):
        at = slice(4 * side, 4 * side + 4)
        return product_forward(chunks, dtype, down_parts[at], scalars, active, *arrays[at])

    sum_final = Sum(product_final, active, *down_arrays)
    sum_final.first(steps)
    give_down, mine_down = steps.do(
        lambda v: (half(v, 1, 1 - y), half(v, 1, y)), scatter_down.result
    )
    down_y = swap(give_down, MASK_Y)
    given, in_mine = steps.do(
        lambda v: (half(v, 0, 1 - t), half(v, 0, t)), scatter_a.result
    )
    from_t = swap(given, MASK_T)
    tokens_stream.second(steps)
    sum_final.own(steps)
    rows_stream = tokens_stream.rows(steps)
    sum_final.release(steps)
    sum_final.send()

    mixed_grad = steps.do(
        lambda rows, weight: dot_back(rows, weight).astype(LOW), rows_stream, weight_out
    )
    projected_grad = steps.do(attend_back, lowered, mask, cosine, sine, mixed_grad)
    down_y, from_t = steps.do(lambda *v: v, down_y, from_t)
    scatter_attention = Scatter(
        functools.partial(scatter_heads, scalars), rows_one, projected_grad, mixed_low, rows_stream
    )
    scatter_attention.core(steps)

    def product_qkv(chunks, side, dtype, gradient, *arrays):
        parts = placed_parts(qkv_parts, arrays)
        terms = [
            (gradient, core, parts[4 * core + 2 * side : 4 * core + 2 * side + 2])
            for core in (0, 1)
        ]
        return product_back(scalars, chunks, dtype, terms)

    sum_one = Sum(product_qkv, projected_grad, *qkv_arrays)
    def output_of(stream, *parts):
        final = stream + core_natural(*sum_final.total(*parts))
        squares = jnp.stack([jnp.sum(stream * stream), jnp.sum(final * final)]).reshape(1, 2)
        return final.astype(LOW), squares

    def input_back(values, inverse, grad, *parts):
        source = values.astype(FULL)
        normed = (source - jnp.mean(source, axis=-1, keepdims=True)) * inverse
        total = natural(jnp.concatenate(sum_one.total(*parts), axis=1))
        return (grad + norm_back(normed, inverse, total)).astype(LOW)

    def adam_down(mine, got, *state):
        gradient = in_order(y, mine, got, 0).astype(FULL)
        return (gradient, *adam_step(state[0], gradient, *state[1:], rate))

    def adam_in(mine, from_t, from_y, from_both, *state):
        sides = []
        for bit in range(2):
            same = jnp.where(t == bit, mine, from_t).astype(FULL)
            cross = jnp.where(t == bit, from_y, from_both).astype(FULL)
            sides.append((jnp.where(y == 0, same, cross), jnp.where(y == 0, cross, same)))
        blocks = [
            part[:, j * unit : (j + 1) * unit] for j in range(2) for side in sides for part in side
        ]
        gradient = jnp.concatenate(blocks, axis=1)
        return (gradient, *adam_step(state[0], gradient, *state[1:], rate))

    def split_attention(total):
        parts = total[:, : 3 * pair]
        out_rows = jnp.concatenate(
            [total[j * HEAD_DIM : (j + 1) * HEAD_DIM, 3 * pair :] for j in range(4)], axis=1
        )
        return (
            half(parts, 0, 1 - t),
            half(parts, 0, t),
            half(out_rows, 1, 1 - y),
            half(out_rows, 1, y),
        )

    def core_pairs(kept, got):
        even, odd = jnp.where(t == 0, kept, got), jnp.where(t == 0, got, kept)
        return jnp.concatenate(
            [
                part[:, j * HEAD_DIM : (j + 1) * HEAD_DIM]
                for j in range(6)
                for part in (even, odd)
            ],
            axis=1,
        )

    def split_grad(mine, theirs):
        even, odd = jnp.where(c == 0, mine, theirs), jnp.where(c == 0, theirs, mine)
        whole = jnp.concatenate(
            [
                part[:, j * 2 * pair : (j + 1) * 2 * pair]
                for j in range(3)
                for part in (even, odd)
            ],
            axis=1,
        )
        return (
            lax.dynamic_slice_in_dim(whole, (2 * (1 - y) + c) * block, block, 1),
            lax.dynamic_slice_in_dim(whole, (2 * y + c) * block, block, 1),
        )

    def adam_out(mine, got, *state):
        gradient = in_order(y, mine, got, 0).astype(FULL)
        return (gradient, *adam_step(state[0], gradient, *state[1:], rate_out))

    def adam_qkv(mine, got, *state):
        even, odd = jnp.where(y == 0, mine, got), jnp.where(y == 0, got, mine)
        gradient = jnp.concatenate(
            [
                part[:, j * HEAD_DIM : (j + 1) * HEAD_DIM]
                for j in range(pairs)
                for part in (even, odd)
            ],
            axis=1,
        ).astype(FULL)
        return (gradient, *adam_step(state[0], gradient, *state[1:], rate))

    def share(squares, bit):
        return steps.do(jnp.add, squares, swap(squares, bit))

    sum_one.first_y(steps)
    scatter_attention.send(steps)
    sum_one.first_t(steps)
    sum_final.second(steps)
    given_y, given_both = steps.do(
        lambda v: (half(v, 0, t), half(v, 0, 1 - t)), scatter_b.result
    )
    from_y = swap(given_y, MASK_Y)
    from_both = swap(given_both, MASK_Y | MASK_T)
    sum_one.release(steps)
    sum_one.send()
    sum_one.own(steps)
    output, squares = steps.do(output_of, stream, *sum_final.parts())
    squares = share(squares, MASK_E)
    step_down = steps.do(adam_down, mine_down, down_y, master_down, first_down, second_down)
    squares = share(squares, MASK_T)
    step_in = steps.do(
        adam_in, in_mine, from_t, from_y, from_both, master_in, first_in, second_in
    )
    squares = share(squares, MASK_HI)
    given, kept, give_out, mine_out = steps.do(split_attention, scatter_attention.result)
    pairs_t = swap(given, MASK_T)
    out_y = swap(give_out, MASK_Y)
    sum_one.second(steps)
    pairs_mine = steps.do(core_pairs, kept, pairs_t)
    pairs_core = swap(pairs_mine, MASK_C)
    squares = share(squares, MASK_C)
    step_out = steps.do(adam_out, mine_out, out_y, master_out, first_out, second_out)
    given, kept = steps.do(split_grad, pairs_mine, pairs_core)
    pairs_y = swap(given, MASK_Y)
    input_grad = steps.do(input_back, inputs, inverse_one, stream_grad, *sum_one.parts())
    squares = share(squares, MASK_Y)
    stream_rms = jnp.sqrt(squares[0] / (ROWS * width * DEVICES))
    step_qkv = steps.do(adam_qkv, kept, pairs_y, master_qkv, first_qkv, second_qkv)
    results = zip(step_qkv, step_out, step_in, step_down)
    grads, updated, moments, variances, narrows = results
    return (output, input_grad, *grads, *updated, *moments, *variances, *narrows, stream_rms)


def solution(mesh):
    shards = split_layer if tuple(mesh.shape.values()) == (4, 8) else gathered_layer
    return jax.shard_map(
        shards,
        mesh=mesh,
        in_specs=(
            P(("rep", "fsdp"), None),
            P(("rep", "fsdp"), None),
            P(("rep", "fsdp"), None),
            P("fsdp", "rep"),
            P("fsdp", "rep"),
            P("fsdp", "rep"),
            P("fsdp", "rep"),
            P("fsdp", "rep"),
            P("fsdp", "rep"),
            P("fsdp", "rep"),
            P("fsdp", "rep"),
            P("fsdp", "rep"),
            P("fsdp", "rep"),
            P("fsdp", "rep"),
            P("fsdp", "rep"),
        ),
        out_specs=(
            P(("rep", "fsdp"), None),
            P(("rep", "fsdp"), None),
            P("fsdp", "rep"),
            P("fsdp", "rep"),
            P("fsdp", "rep"),
            P("fsdp", "rep"),
            P("fsdp", "rep"),
            P("fsdp", "rep"),
            P("fsdp", "rep"),
            P("fsdp", "rep"),
            P("fsdp", "rep"),
            P("fsdp", "rep"),
            P("fsdp", "rep"),
            P("fsdp", "rep"),
            P("fsdp", "rep"),
            P("fsdp", "rep"),
            P("fsdp", "rep"),
            P("fsdp", "rep"),
            P("fsdp", "rep"),
            P("fsdp", "rep"),
            P("fsdp", "rep"),
            P("fsdp", "rep"),
            P(),
        ),
        check_vma=False,
    )
```

```python
import collections
import functools

import jax
import jax.numpy as jnp
import numpy as np
from jax import lax
from jax.experimental import pallas as pl
from jax.experimental.pallas import tpu as pltpu
from jax.sharding import PartitionSpec as P

HEADS = 16
HEAD_DIM = 128
STEP = 10


beta_one = 0.9
beta_two = 0.95
rate = 0.02
rate_out = 0.08
decay = 0.1
epsilon = 1e-08


def normalize(values):
    centered = values - jnp.mean(values, axis=-1, keepdims=True)
    inverse = lax.rsqrt(jnp.mean(centered * centered, axis=-1, keepdims=True) + 1e-05)
    return (centered * inverse, inverse)


def norm_back(normed, inverse, gradient):
    first = jnp.mean(gradient, axis=-1, keepdims=True)
    second = jnp.mean(gradient * normed, axis=-1, keepdims=True)
    return inverse * (gradient - first - normed * second)


def rotate(values):
    half = values.shape[-1] // 2
    return jnp.concatenate([-values[..., half:], values[..., :half]], axis=-1)


def rotate_back(values):
    half = values.shape[-1] // 2
    return jnp.concatenate([values[..., half:], -values[..., :half]], axis=-1)


def rotary_tables(length, size):
    half = size // 2
    freqs = 10000.0 ** (-(jnp.arange(half, dtype=jnp.float32) * 2.0) / size)
    angles = jnp.arange(length, dtype=jnp.float32)[:, None] * freqs[None, :]
    cosine = jnp.concatenate([jnp.cos(angles), jnp.cos(angles)], axis=-1)[:, None, :]
    sine = jnp.concatenate([jnp.sin(angles), jnp.sin(angles)], axis=-1)[:, None, :]
    return (cosine, sine)


def group_gradient(operand, gradient):
    return lax.psum_scatter(
        lax.dot_general(
            operand, gradient, (((0,), (0,)), ((), ())), preferred_element_type=jnp.float32
        ).astype(jnp.bfloat16),
        "fsdp",
        scatter_dimension=0,
        tiled=True,
    ).astype(jnp.float32)


def adam_step(master, gradient, first, second, step_rate):
    moment = beta_one * first + (1.0 - beta_one) * gradient
    variance = beta_two * second + (1.0 - beta_two) * gradient * gradient
    update = (
        moment / (1.0 - beta_one**STEP) / (jnp.sqrt(variance / (1.0 - beta_two**STEP)) + epsilon)
    )
    updated = master - step_rate * (update + decay * master)
    return (updated, moment, variance, updated.astype(jnp.bfloat16))


def gathered_layer(
    inputs,
    cotangent,
    segment_ids,
    master_qkv,
    master_out,
    master_in,
    master_down,
    first_qkv,
    first_out,
    first_in,
    first_down,
    second_qkv,
    second_out,
    second_in,
    second_down,
):
    copies = (
        lax.all_gather(master_qkv.astype(jnp.bfloat16), "rep", axis=1, tiled=True),
        lax.all_gather(master_out.astype(jnp.bfloat16), "rep", axis=1, tiled=True),
        lax.all_gather(master_in.astype(jnp.bfloat16), "rep", axis=1, tiled=True),
        lax.all_gather(master_down.astype(jnp.bfloat16), "rep", axis=1, tiled=True),
    )

    def forward_product(operand, number):
        portion = copies[number]
        return jnp.dot(
            operand,
            lax.all_gather(portion, "fsdp", axis=0, tiled=True),
            preferred_element_type=jnp.float32,
        )

    def backward_product(gradient, number):
        return lax.dot_general(
            gradient,
            lax.all_gather(copies[number], "fsdp", axis=0, tiled=True),
            (((1,), (1,)), ((), ())),
            preferred_element_type=jnp.float32,
        )

    def weight_gradient(operand, gradient):
        return group_gradient(operand, gradient)

    length = inputs.shape[0]
    width = inputs.shape[1]
    scale = HEAD_DIM ** (-0.5)
    cosine, sine = rotary_tables(length, HEAD_DIM)
    segments = segment_ids[0]
    places = jnp.arange(length)
    allowed = (segments[:, None] == segments[None, :]) & (places[None, :] <= places[:, None])
    source = inputs.astype(jnp.float32)
    normed_one, inverse_one = normalize(source)
    lowered_one = normed_one.astype(jnp.bfloat16)
    projected = forward_product(lowered_one, 0)
    queries = projected[:, :width].reshape(length, HEADS, HEAD_DIM)
    keys = projected[:, width : 2 * width].reshape(length, HEADS, HEAD_DIM)
    values = projected[:, 2 * width :].reshape(length, HEADS, HEAD_DIM).astype(jnp.bfloat16)
    queries = (queries * cosine + rotate(queries) * sine).astype(jnp.bfloat16)
    keys = (keys * cosine + rotate(keys) * sine).astype(jnp.bfloat16)
    scores = jnp.einsum("shd,thd->hst", queries, keys, preferred_element_type=jnp.float32) * scale
    scores = jnp.where(allowed[None], scores, -1e30)
    probability = jax.nn.softmax(scores, axis=-1)
    prob_low = probability.astype(jnp.bfloat16)
    mixed = jnp.einsum("hst,thd->shd", prob_low, values, preferred_element_type=jnp.float32)
    mixed_low = mixed.reshape(length, width).astype(jnp.bfloat16)
    stream = source + forward_product(mixed_low, 1)
    normed_two, inverse_two = normalize(stream)
    lowered_two = normed_two.astype(jnp.bfloat16)
    gate_up = forward_product(lowered_two, 2)
    hidden = gate_up.shape[1] // 2
    gate = gate_up[:, :hidden]
    upper = gate_up[:, hidden:]
    sigmoid_gate = jax.nn.sigmoid(gate)
    silu_gate = gate * sigmoid_gate
    active_low = (silu_gate * upper).astype(jnp.bfloat16)
    final = stream + forward_product(active_low, 3)
    output = final.astype(jnp.bfloat16)
    summed_squares = lax.psum((jnp.sum(stream * stream), jnp.sum(final * final)), ("rep", "fsdp"))
    entries = length * width * lax.axis_size("rep") * lax.axis_size("fsdp")
    stream_rms = jnp.sqrt(jnp.stack(summed_squares) / entries)
    grad_down = weight_gradient(active_low, cotangent)
    active_grad = backward_product(cotangent, 3)
    gate_grad = active_grad * upper * sigmoid_gate * (1.0 + gate * (1.0 - sigmoid_gate))
    upper_grad = active_grad * silu_gate
    gate_up_grad = jnp.concatenate([gate_grad, upper_grad], axis=1).astype(jnp.bfloat16)
    grad_in = weight_gradient(lowered_two, gate_up_grad)
    lowered_two_grad = backward_product(gate_up_grad, 2)
    stream_grad = cotangent.astype(jnp.float32) + norm_back(
        normed_two, inverse_two, lowered_two_grad
    )
    stream_grad_low = stream_grad.astype(jnp.bfloat16)
    grad_out = weight_gradient(mixed_low, stream_grad_low)
    mixed_grad = backward_product(stream_grad_low, 1)
    mixed_grad_low = mixed_grad.reshape(length, HEADS, HEAD_DIM).astype(jnp.bfloat16)
    prob_grad = jnp.einsum(
        "shd,thd->hst", mixed_grad_low, values, preferred_element_type=jnp.float32
    )
    score_grad = probability * (
        prob_grad - jnp.sum(probability * prob_grad, axis=-1, keepdims=True)
    )
    score_grad_low = score_grad.astype(jnp.bfloat16)
    query_grad = (
        jnp.einsum("hst,thd->shd", score_grad_low, keys, preferred_element_type=jnp.float32) * scale
    )
    key_grad = (
        jnp.einsum("hst,shd->thd", score_grad_low, queries, preferred_element_type=jnp.float32)
        * scale
    )
    value_grad = jnp.einsum(
        "hst,shd->thd", prob_low, mixed_grad_low, preferred_element_type=jnp.float32
    )
    query_grad = query_grad * cosine + rotate_back(query_grad * sine)
    key_grad = key_grad * cosine + rotate_back(key_grad * sine)
    projected_grad = jnp.concatenate(
        [
            query_grad.reshape(length, width),
            key_grad.reshape(length, width),
            value_grad.reshape(length, width),
        ],
        axis=1,
    ).astype(jnp.bfloat16)
    grad_qkv = weight_gradient(lowered_one, projected_grad)
    lowered_one_grad = backward_product(projected_grad, 0)
    input_grad = (stream_grad + norm_back(normed_one, inverse_one, lowered_one_grad)).astype(
        jnp.bfloat16
    )
    summed = (
        lax.psum(grad_qkv.astype(jnp.bfloat16), "rep").astype(jnp.float32),
        lax.psum(grad_out.astype(jnp.bfloat16), "rep").astype(jnp.float32),
        lax.psum(grad_in.astype(jnp.bfloat16), "rep").astype(jnp.float32),
        lax.psum(grad_down.astype(jnp.bfloat16), "rep").astype(jnp.float32),
    )
    group = lax.axis_index("rep")
    reduced = tuple(
        (
            lax.dynamic_slice_in_dim(
                full,
                group * (full.shape[1] // lax.axis_size("rep")),
                full.shape[1] // lax.axis_size("rep"),
                1,
            )
            for full in summed
        )
    )
    updated_qkv, moment_qkv, variance_qkv, narrow_qkv = adam_step(
        master_qkv, reduced[0], first_qkv, second_qkv, rate
    )
    updated_out, moment_out, variance_out, narrow_out = adam_step(
        master_out, reduced[1], first_out, second_out, rate_out
    )
    updated_in, moment_in, variance_in, narrow_in = adam_step(
        master_in, reduced[2], first_in, second_in, rate
    )
    updated_down, moment_down, variance_down, narrow_down = adam_step(
        master_down, reduced[3], first_down, second_down, rate
    )
    return (
        output,
        input_grad,
        reduced[0],
        reduced[1],
        reduced[2],
        reduced[3],
        updated_qkv,
        updated_out,
        updated_in,
        updated_down,
        moment_qkv,
        moment_out,
        moment_in,
        moment_down,
        variance_qkv,
        variance_out,
        variance_in,
        variance_down,
        narrow_qkv,
        narrow_out,
        narrow_in,
        narrow_down,
        stream_rms,
    )


ALL = ("rep", "fsdp")
MASK_Y, MASK_C, MASK_HI, MASK_E, MASK_T = 16, 8, 4, 2, 1
DEVICES = 32
ROWS = 256
FULL = jnp.float32
LOW = jnp.bfloat16


def swap(values, mask):
    return lax.ppermute(values, ALL, [(i, i ^ mask) for i in range(DEVICES)])


def half(values, axis, bit):
    size = values.shape[axis] // 2
    return lax.dynamic_slice_in_dim(values, bit * size, size, axis)


class Steps:
    def __init__(self):
        self.last = ()

    def do(self, work, *values):
        values, _ = lax.optimization_barrier((values, self.last))
        result = work(*values)
        self.last = (jax.tree.leaves(result)[0],)
        return result

    def wait(self, value):
        return self.do(lambda v: v, value)


def columns(values, starts, width):
    return jnp.concatenate(
        [lax.dynamic_slice_in_dim(values, start, width, 1) for start in starts], axis=1
    )


def in_order(bit, mine, other, axis):
    first = jnp.where(bit == 0, mine, other)
    second = jnp.where(bit == 0, other, mine)
    return jnp.concatenate([first, second], axis=axis)


def dot(left, right):
    return jnp.dot(left, right, preferred_element_type=FULL)


def dot_back(left, right):
    return lax.dot_general(left, right, (((1,), (1,)), ((), ())), preferred_element_type=FULL)


def dot_tokens(left, right):
    return lax.dot_general(left, right, (((0,), (0,)), ((), ())), preferred_element_type=FULL)


def low_dot_tokens(left, right):
    return dot_tokens(left, right).astype(LOW)


class Tokens:
    def __init__(self, values):
        self.values = values

    def send_y(self, steps):
        self.from_y = swap(steps.wait(self.values), MASK_Y)

    def send_t(self, steps):
        self.from_t = swap(steps.wait(self.values), MASK_T)

    def send(self, steps):
        self.values = steps.wait(self.values)
        self.from_y = swap(self.values, MASK_Y)
        self.from_t = swap(self.values, MASK_T)

    def second(self, steps):
        cut = ROWS // 2

        def parts(from_t, from_y):
            upper = from_t[:cut]
            if from_t.shape[0] > ROWS:
                upper = jnp.concatenate([upper, from_t[ROWS:]], axis=0)
            return upper, from_y[cut:ROWS]

        upper, lower = steps.do(parts, self.from_t, self.from_y)
        self.upper = swap(upper, MASK_Y)
        self.lower = swap(lower, MASK_T)

    def rows(self, steps):
        cut = ROWS // 2
        return steps.do(
            functools.partial(join_rows, (ROWS, ROWS, cut, cut, ROWS)),
            self.values,
            self.from_y,
            self.upper,
            self.lower,
            self.from_t,
        )


class Sum:
    def __init__(self, product, *values):
        self.product = product
        self.values = values

    def first(self, steps):
        self.first_y(steps)
        self.first_t(steps)

    def first_y(self, steps):
        self.give_y = steps.do(lambda *v: self.product((1, 2), 0, LOW, *v), *self.values)

    def first_t(self, steps):
        self.give_t = steps.do(lambda *v: self.product((2, 3), 1, LOW, *v), *self.values)

    def release(self, steps):
        self.give_y, self.give_t = steps.do(lambda *v: v, self.give_y, self.give_t)

    def send(self):
        self.got_y = swap(self.give_y, MASK_Y)
        self.got_t = swap(self.give_t, MASK_T)

    def own(self, steps):
        self.mine = steps.do(
            lambda *v: (self.product((0, 3), 0, FULL, *v), self.product((0, 1), 1, FULL, *v)),
            *self.values,
        )

    def second(self, steps):
        give_t, give_y = steps.do(
            lambda got_y, got_t, side_0, side_1: (
                (side_0[ROWS:] + got_y[ROWS:].astype(FULL)).astype(LOW),
                (side_1[ROWS:] + got_t[:ROWS].astype(FULL)).astype(LOW),
            ),
            self.got_y,
            self.got_t,
            *self.mine,
        )
        self.last_t = swap(give_t, MASK_T)
        self.last_y = swap(give_y, MASK_Y)

    def total(self, side_0, side_1, got_y, got_t, last_t, last_y):
        return (
            side_0[:ROWS] + got_y[:ROWS].astype(FULL) + last_t.astype(FULL),
            side_1[:ROWS] + got_t[ROWS:].astype(FULL) + last_y.astype(FULL),
        )

    def parts(self):
        return (*self.mine, self.got_y, self.got_t, self.last_t, self.last_y)


GROUPS = [
    [16 * y + 8 * c + 4 * hi + 2 * e + t for c in (0, 1) for hi in (0, 1) for e in (0, 1)]
    for y in (0, 1)
    for t in (0, 1)
]


class Gather:
    def __init__(self, steps, work, *values):
        piece = steps.do(work, *values)
        self.size = piece.shape[0]
        self.whole = lax.all_gather(piece, ALL, axis=0, tiled=True, axis_index_groups=GROUPS)

    def parts(self, rows, first=0):
        return [Part(self.whole, self.size, rows, first, AT_NUMBERS + at) for at in range(8)]


Part = collections.namedtuple("Part", ("array", "size", "rows", "first", "base"))


def part_block(part, rows, width, place):
    def index(i, scalars):
        row, column = place(i, scalars)
        return (scalars[part.base] * (part.size // rows) + part.first // rows + row, column)

    return pl.BlockSpec((rows, width), index)


QUARTETS = [
    [16 * y + 8 * c + 4 * hi + 2 * e + t for hi in (0, 1) for e in (0, 1)]
    for y in (0, 1)
    for c in (0, 1)
    for t in (0, 1)
]


class Scatter:
    def __init__(self, product, *values):
        self.product, self.values = product, values

    def core(self, steps):
        self.from_core = swap(
            steps.do(functools.partial(self.product, 1), *self.values), MASK_C
        )

    def send(self, steps):
        self.result = lax.psum_scatter(
            steps.do(functools.partial(self.product, 0), *self.values, self.from_core),
            ALL,
            scatter_dimension=0,
            tiled=True,
            axis_index_groups=QUARTETS,
        )


VMEM_LIMIT = 56 * 2**20


def compiler_params():
    return pltpu.CompilerParams(vmem_limit_bytes=VMEM_LIMIT)


def fixed(shape):
    return pl.BlockSpec(shape, lambda i, *_: (0, 0), pipeline_mode=pl.Buffered(1))


TILE = 256


def join_kernel(*refs):
    at = 0
    for ref in refs[:-1]:
        rows = ref.shape[0]
        refs[-1][at : at + rows, :] = ref[...]
        at += rows


def join_rows(sizes, *parts):
    width = parts[0].shape[1]
    tile = width // 4
    rows = sum(sizes)
    return pl.pallas_call(
        join_kernel,
        grid=(4,),
        in_specs=[pl.BlockSpec((size, tile), lambda i: (0, i)) for size in sizes],
        out_specs=pl.BlockSpec((rows, tile), lambda i: (0, i)),
        out_shape=jax.ShapeDtypeStruct((rows, width), parts[0].dtype),
        compiler_params=compiler_params(),
        cost_estimate=cost(0, 4 * rows * width),
    )(*parts)


def heads_kernel(scalars, rows, gradient, mixed, stream, *refs):
    out = refs[-1]
    width = gradient.shape[1]
    total = dot_tokens(rows[...], gradient[...])
    weight = dot_tokens(mixed[...], stream[...])
    if len(refs) == 2:
        total = total + refs[0][:, :width].astype(FULL)
    out[:, :width] = total.astype(LOW)
    rest = out.shape[1] - width
    for at in range(4):
        part = weight[:, at * rest : (at + 1) * rest]
        place = slice(at * HEAD_DIM, (at + 1) * HEAD_DIM)
        if len(refs) == 2:
            part = part + refs[0][place, width:].astype(FULL)
        out[place, width:] = part.astype(LOW)


def scatter_heads(scalars, side, rows, gradient, mixed, stream, *adds):
    tokens, depth = rows.shape
    block, width = depth // 4, gradient.shape[1] // 2
    middle = stream.shape[1] // 2
    out = pl.BlockSpec((block, middle), lambda i, s: (s[AT_FOURTHS + i], 0))

    def side_of(size):
        return pl.BlockSpec((tokens, size), lambda i, s: (0, side), pipeline_mode=pl.Buffered(1))

    return pl.pallas_call(
        heads_kernel,
        grid_spec=pltpu.PrefetchScalarGridSpec(
            num_scalar_prefetch=1,
            grid=(4,),
            in_specs=[
                pl.BlockSpec((tokens, block), lambda i, s: (0, i)),
                side_of(width),
                pl.BlockSpec((tokens, HEAD_DIM), lambda i, s: (0, s[i])),
                side_of(middle),
            ]
            + [out] * len(adds),
            out_specs=out,
        ),
        out_shape=jax.ShapeDtypeStruct((depth, middle), LOW),
        compiler_params=compiler_params(),
        cost_estimate=cost(8 * tokens * block * middle, 2 * tokens * (depth + 2 * middle)),
    )(scalars, rows, gradient, mixed, stream, *adds)


def scatter_kernel(scalars, operand, gradient, *refs):
    total = dot_tokens(operand[...], gradient[...])
    for ref in refs[:-1]:
        total = total + ref[...].astype(FULL)
    refs[-1][...] = total.astype(refs[-1].dtype)


def scatter_blocks(scalars, placed, side, operand, gradient, *adds):
    tokens, depth = operand.shape
    block, width = depth // 4, gradient.shape[1] // 2
    out = pl.BlockSpec((block, width), lambda i, s: (s[AT_FOURTHS + i], 0))
    return pl.pallas_call(
        scatter_kernel,
        grid_spec=pltpu.PrefetchScalarGridSpec(
            num_scalar_prefetch=1,
            grid=(4,),
            in_specs=[
                pl.BlockSpec((tokens, block), lambda i, s: (0, s[i] if placed else i)),
                pl.BlockSpec(
                    (tokens, width), lambda i, s: (0, side), pipeline_mode=pl.Buffered(1)
                ),
            ]
            + [out] * len(adds),
            out_specs=out,
        ),
        out_shape=jax.ShapeDtypeStruct((4 * block, width), LOW),
        compiler_params=compiler_params(),
        cost_estimate=cost(
            8 * tokens * block * width, 2 * (4 * tokens * block + tokens * width + 8 * block * width)
        ),
    )(scalars, operand, gradient, *adds)


COST_SHARE = 1.0


def cost(flops, size, transcendentals=0):
    return pl.CostEstimate(
        flops=int(COST_SHARE * flops),
        bytes_accessed=int(COST_SHARE * size),
        transcendentals=int(COST_SHARE * transcendentals),
    )


def piece_sum(rows, pieces):
    depth = pieces[0].shape[0]
    total = dot(rows[:, :depth], pieces[0][...])
    for at in range(1, len(pieces)):
        total = total + dot(rows[:, at * depth : (at + 1) * depth], pieces[at][...])
    return total


PIECE = 2 * ROWS


def part_tiles(part, side, tiles):
    return part_block(
        part, part.rows, TILE, lambda i, _: (0, jnp.clip(i - side * tiles, 0, tiles - 1))
    )


AT_Y, AT_NUMBERS, AT_FOURTHS, AT_T, AT_HEADS = 4, 5, 13, 17, 18


def divided_sum(scalars, rows, pieces):
    total = 0.0
    for at, piece in enumerate(pieces):
        start = pl.multiple_of((at - at % 2 + (scalars[AT_T] ^ (at % 2))) * ROWS, ROWS)
        total = total + dot(rows[:, pl.ds(start, ROWS)], piece[...])
    return total


def pieces_kernel(tiles, scalars, rows, *refs):
    for side in range(2):

        @pl.when(pl.program_id(0) // tiles == side)
        def _(side=side):
            refs[8][...] = piece_sum(rows, refs[4 * side : 4 * side + 4])


def product_pieces(parts, width, scalars, rows, *arrays):
    tokens, depth = rows.shape
    tiles = width // TILE
    return pl.pallas_call(
        functools.partial(pieces_kernel, tiles),
        grid_spec=pltpu.PrefetchScalarGridSpec(
            num_scalar_prefetch=1,
            grid=(2 * tiles,),
            in_specs=[fixed(rows.shape)]
            + [part_tiles(part, at // 4, tiles) for at, part in enumerate(parts)],
            out_specs=pl.BlockSpec((tokens, TILE), lambda i, *_: (0, i)),
        ),
        out_shape=jax.ShapeDtypeStruct((tokens, 2 * width), FULL),
        compiler_params=compiler_params(),
        cost_estimate=cost(4 * tokens * depth * width, 2 * depth * (tokens + 2 * width)),
    )(scalars, rows, *arrays)


def heads_join_kernel(scalars, piece, out):
    for at in range(4):
        out[:, at * TILE : (at + 1) * TILE] = piece[at * HEAD_DIM : (at + 1) * HEAD_DIM, :]


def join_heads(scalars, whole):
    return pl.pallas_call(
        heads_join_kernel,
        grid_spec=pltpu.PrefetchScalarGridSpec(
            num_scalar_prefetch=1,
            grid=(8,),
            in_specs=[pl.BlockSpec((PIECE, TILE), lambda i, s: (s[AT_HEADS + i], 3))],
            out_specs=pl.BlockSpec((HEAD_DIM, 4 * TILE), lambda i, s: (i % 4, i // 4)),
        ),
        out_shape=jax.ShapeDtypeStruct((4 * HEAD_DIM, 8 * TILE), LOW),
        compiler_params=compiler_params(),
        cost_estimate=cost(0, 16 * PIECE * TILE * 2),
    )(scalars, whole)


def unit_kernel(tiles, scalars, rows, *refs):
    gate, upper, active = refs[32:]
    for side in range(2):

        @pl.when(pl.program_id(0) // tiles == side)
        def _(side=side):
            a = divided_sum(scalars, rows, refs[16 * side : 16 * side + 8])
            b = piece_sum(rows, refs[16 * side + 8 : 16 * side + 16])
            gated = jnp.where(scalars[AT_Y] == 0, a, b)
            raised = jnp.where(scalars[AT_Y] == 0, b, a)
            gate[...] = gated.astype(LOW)
            upper[...] = raised.astype(LOW)
            active[...] = (gated * jax.nn.sigmoid(gated) * raised).astype(LOW)


def unit_forward(parts, scalars, rows, *arrays):
    tokens, depth = rows.shape
    width = arrays[0].shape[1]
    tiles = width // TILE
    in_specs = [fixed(rows.shape)]
    in_specs += [part_tiles(part, at // 16, tiles) for at, part in enumerate(parts)]
    out = pl.BlockSpec((tokens, TILE), lambda i, *_: (0, i))
    shape = jax.ShapeDtypeStruct((tokens, 2 * width), LOW)
    return pl.pallas_call(
        functools.partial(unit_kernel, tiles),
        grid_spec=pltpu.PrefetchScalarGridSpec(
            num_scalar_prefetch=1,
            grid=(2 * tiles,),
            in_specs=in_specs,
            out_specs=[out, out, out],
        ),
        out_shape=[shape, shape, shape],
        compiler_params=compiler_params(),
        cost_estimate=cost(
            8 * tokens * depth * width, 2 * depth * (tokens + 4 * width) + 12 * tokens * width
        ),
    )(scalars, rows, *arrays)


def unit_back_kernel(scalars, own, other, *refs):
    gate, upper, grad_a, grad_b = refs[8:]
    for at in range(4):

        @pl.when(pl.program_id(0) // 2 == at)
        def _(at=at):
            grad = dot_back(own[...], refs[at][...]) + dot_back(other[...], refs[4 + at][...])
            gated, raised = gate[...].astype(FULL), upper[...].astype(FULL)
            sigmoid = jax.nn.sigmoid(gated)
            gate_grad = grad * raised * sigmoid * (1.0 + gated * (1.0 - sigmoid))
            upper_grad = grad * (gated * sigmoid)
            grad_a[...] = jnp.where(scalars[AT_Y] == 0, gate_grad, upper_grad).astype(LOW)
            grad_b[...] = jnp.where(scalars[AT_Y] == 0, upper_grad, gate_grad).astype(LOW)


def unit_back(parts, scalars, rows, gate, upper, *arrays):
    tokens, depth = rows.shape
    units = gate.shape[1]
    cut = depth // 2
    shape = jax.ShapeDtypeStruct((tokens, units), LOW)
    out = pl.BlockSpec((tokens, TILE), lambda i, scalars: (0, 2 * scalars[i // 2] + i % 2))

    def half_rows(at):
        return pl.BlockSpec((tokens, cut), lambda i, *_: (0, at), pipeline_mode=pl.Buffered(1))

    def units_of(at, part):
        return part_block(part, TILE, cut, lambda i, _: (jnp.clip(i - 2 * (at % 4), 0, 1), 0))

    return pl.pallas_call(
        unit_back_kernel,
        grid_spec=pltpu.PrefetchScalarGridSpec(
            num_scalar_prefetch=1,
            grid=(8,),
            in_specs=[half_rows(0), half_rows(1)] + [units_of(at, part) for at, part in enumerate(parts)] + [out, out],
            out_specs=[out, out],
        ),
        out_shape=[shape, shape],
        compiler_params=compiler_params(),
        cost_estimate=cost(
            2 * tokens * depth * units, 2 * depth * (tokens + units) + 8 * tokens * units
        ),
    )(scalars, rows, rows, *arrays, gate, upper)


def chunk_rows(left, chunk, width, place):
    return pl.BlockSpec(
        (ROWS, width), lambda i, scalars: (chunk, place(scalars)), pipeline_mode=pl.Buffered(1)
    )


def back_kernel(chunks, counts, _, *refs):
    terms = len(counts)
    lefts, rights, out = refs[: chunks * terms], refs[chunks * terms : -1], refs[-1]
    for step in range(4):

        @pl.when(pl.program_id(0) == step)
        def _(step=step):
            for chunk in range(chunks):
                total, first = 0.0, 0
                for term, count in enumerate(counts):
                    right = rights[first + step * count // 4]
                    total = total + dot_back(lefts[chunk * terms + term][...], right[...])
                    first += count
                out[chunk * ROWS : (chunk + 1) * ROWS, :] = total.astype(out.dtype)


def product_back(scalars, chunks, dtype, terms):
    in_specs, values = [], []
    for chunk in chunks:
        for left, at, _ in terms:
            in_specs.append(chunk_rows(left, chunk, left.shape[1] // 2, lambda s, at=at: at))
            values.append(left)
    depth = 0
    for left, _, parts in terms:
        size = left.shape[1] // 2
        depth += size
        for part in parts:
            if len(parts) == 4:
                spec = part_block(part, ROWS, size, lambda i, s: (0, 0))
            else:
                spec = part_block(part, ROWS, size, lambda i, s: (s[AT_T] ^ (i % 2), 0))
            in_specs.append(spec)
            values.append(part.array)
    rows, width = len(chunks) * ROWS, 4 * TILE
    counts = [len(parts) for _, _, parts in terms]
    return pl.pallas_call(
        functools.partial(back_kernel, len(chunks), counts),
        grid_spec=pltpu.PrefetchScalarGridSpec(
            num_scalar_prefetch=1,
            grid=(4,),
            in_specs=in_specs,
            out_specs=pl.BlockSpec(
                (rows, TILE), lambda i, s: (0, i - i % 2 + (s[AT_T] ^ (i % 2)))
            ),
        ),
        out_shape=jax.ShapeDtypeStruct((rows, width), dtype),
        compiler_params=compiler_params(),
        cost_estimate=cost(2 * rows * depth * width, 2 * depth * (rows + width) + 4 * rows * width),
    )(scalars, *values)


def forward_kernel(chunks, _, *refs):
    lefts, rights, out = refs[: chunks * 4], refs[chunks * 4 : -1], refs[-1]
    for chunk in range(chunks):
        total = dot(lefts[4 * chunk][...], rights[0][...])
        for at in range(1, 4):
            total = total + dot(lefts[4 * chunk + at][...], rights[at][...])
        out[chunk * ROWS : (chunk + 1) * ROWS, :] = total.astype(out.dtype)


def product_forward(chunks, dtype, parts, scalars, left, *arrays):
    depth, width = PIECE, arrays[0].shape[1]
    in_specs = [
        chunk_rows(left, chunk, depth, lambda scalars, at=at: scalars[at])
        for chunk in chunks
        for at in range(4)
    ] + [part_block(part, PIECE, TILE, lambda i, _: (0, i)) for part in parts]
    rows = len(chunks) * ROWS
    return pl.pallas_call(
        functools.partial(forward_kernel, len(chunks)),
        grid_spec=pltpu.PrefetchScalarGridSpec(
            num_scalar_prefetch=1,
            grid=(width // TILE,),
            in_specs=in_specs,
            out_specs=pl.BlockSpec((rows, TILE), lambda i, *_: (0, i)),
        ),
        out_shape=jax.ShapeDtypeStruct((rows, width), dtype),
        compiler_params=compiler_params(),
        cost_estimate=cost(
            8 * rows * depth * width, 8 * depth * (rows + width) + 4 * rows * width
        ),
    )(scalars, *([left] * (4 * len(chunks))), *arrays)


def signed_tables():
    cosine, sine = rotary_tables(ROWS, HEAD_DIM)
    sign = jnp.concatenate(
        [-jnp.ones((HEAD_DIM // 2,), FULL), jnp.ones((HEAD_DIM // 2,), FULL)]
    )
    return (cosine[:, 0, :], sine[:, 0, :] * sign)


SCALE = HEAD_DIM ** (-0.5)
GROUP_HEADS = 4
GROUP_WIDTH = GROUP_HEADS * HEAD_DIM


def softmax_rows(query, key, allowed):
    scores = dot_back(query, key) * SCALE
    scores = jnp.where(allowed, scores, -1e30)
    weights = jnp.exp(scores - jnp.max(scores, axis=-1, keepdims=True))
    return weights / jnp.sum(weights, axis=-1, keepdims=True)


SIDE_WIDTH = 6 * HEAD_DIM


def head_columns(side, which, head):
    start = side * SIDE_WIDTH + (2 * which + head) * HEAD_DIM
    return slice(start, start + HEAD_DIM)


def mixed_columns(side, head):
    start = (2 * side + head) * HEAD_DIM
    return slice(start, start + HEAD_DIM)


def attend_kernel(projected, mask, cosine, sine, lowered, mixed):
    allowed = mask[...] > 0.0
    cos, sin = cosine[...], sine[...]
    for side in range(2):
        for head in range(2):

            def rope(which):
                values = projected[:, head_columns(side, which, head)]
                return (values * cos + pltpu.roll(values, HEAD_DIM // 2, 1) * sin).astype(LOW)

            query, key = rope(0), rope(1)
            value = projected[:, head_columns(side, 2, head)].astype(LOW)
            probability = softmax_rows(query, key, allowed)
            lowered[:, head_columns(side, 0, head)] = query
            lowered[:, head_columns(side, 1, head)] = key
            lowered[:, head_columns(side, 2, head)] = value
            mixed[:, mixed_columns(side, head)] = dot(probability.astype(LOW), value).astype(LOW)


def attend_back_kernel(lowered, mask, cosine, sine, mixed_grad, projected_grad):
    allowed = mask[...] > 0.0
    cos, sin = cosine[...], sine[...]
    for side in range(2):
        for head in range(2):
            query = lowered[:, head_columns(side, 0, head)]
            key = lowered[:, head_columns(side, 1, head)]
            value = lowered[:, head_columns(side, 2, head)]
            grad = mixed_grad[:, mixed_columns(side, head)]
            probability = softmax_rows(query, key, allowed)
            prob_grad = dot_back(grad, value)
            inner = jnp.sum(probability * prob_grad, axis=-1, keepdims=True)
            score_grad = (probability * (prob_grad - inner)).astype(LOW)
            query_grad = dot(score_grad, key) * SCALE
            key_grad = dot_tokens(score_grad, query) * SCALE
            value_grad = dot_tokens(probability.astype(LOW), grad)

            def unrope(values):
                return (values * cos - pltpu.roll(values, HEAD_DIM // 2, 1) * sin).astype(LOW)

            projected_grad[:, head_columns(side, 0, head)] = unrope(query_grad)
            projected_grad[:, head_columns(side, 1, head)] = unrope(key_grad)
            projected_grad[:, head_columns(side, 2, head)] = value_grad.astype(LOW)


def row_block(width):
    return pl.BlockSpec((ROWS, width), lambda i: (i, 0))


def whole_block(width):
    return pl.BlockSpec((ROWS, width), lambda i: (0, 0))


def attend(projected, mask, cosine, sine):
    rows = projected.shape[0]
    return pl.pallas_call(
        attend_kernel,
        grid=(rows // ROWS,),
        in_specs=[
            row_block(2 * SIDE_WIDTH),
            row_block(ROWS),
            whole_block(HEAD_DIM),
            whole_block(HEAD_DIM),
        ],
        out_specs=[row_block(2 * SIDE_WIDTH), row_block(GROUP_WIDTH)],
        out_shape=[
            jax.ShapeDtypeStruct((rows, 2 * SIDE_WIDTH), LOW),
            jax.ShapeDtypeStruct((rows, GROUP_WIDTH), LOW),
        ],
        compiler_params=compiler_params(),
        cost_estimate=cost(
            4 * rows * ROWS * GROUP_WIDTH, rows * GROUP_WIDTH * 20, rows * ROWS * GROUP_HEADS
        ),
    )(projected, mask, cosine, sine)


def attend_back(lowered, mask, cosine, sine, mixed_grad):
    rows = lowered.shape[0]
    return pl.pallas_call(
        attend_back_kernel,
        grid=(rows // ROWS,),
        in_specs=[
            row_block(2 * SIDE_WIDTH),
            row_block(ROWS),
            whole_block(HEAD_DIM),
            whole_block(HEAD_DIM),
            row_block(GROUP_WIDTH),
        ],
        out_specs=row_block(2 * SIDE_WIDTH),
        out_shape=jax.ShapeDtypeStruct((rows, 2 * SIDE_WIDTH), LOW),
        compiler_params=compiler_params(),
        cost_estimate=cost(
            10 * rows * ROWS * GROUP_WIDTH, rows * GROUP_WIDTH * 14, rows * ROWS * GROUP_HEADS
        ),
    )(lowered, mask, cosine, sine, mixed_grad)


def split_layer(
    inputs,
    cotangent,
    segment_ids,
    master_qkv,
    master_out,
    master_in,
    master_down,
    first_qkv,
    first_out,
    first_in,
    first_down,
    second_qkv,
    second_out,
    second_in,
    second_down,
):
    rep, fsdp = lax.axis_index("rep"), lax.axis_index("fsdp")
    y, c = rep // 2, rep % 2
    hi, e, t = fsdp // 4, (fsdp // 2) % 2, fsdp % 2
    width = inputs.shape[1]
    middle = width // 2
    unit = width // 4
    pair = 2 * HEAD_DIM
    pairs = master_qkv.shape[1] // pair
    block = pairs * HEAD_DIM
    steps = Steps()

    def relative(values):
        starts = [
            4 * (hi ^ at_hi) + 2 * (e ^ at_e) + at_t
            for at_e in (0, 1)
            for at_hi in (0, 1)
            for at_t in (0, 1)
        ]
        return columns(values, [start * ROWS for start in starts], ROWS)

    def natural(values):
        starts = [
            4 * (e ^ at_e) + 2 * (hi ^ at_hi) + at_t
            for at_hi in (0, 1)
            for at_e in (0, 1)
            for at_t in (0, 1)
        ]
        return columns(values, [start * ROWS for start in starts], ROWS)

    def core_first(values):
        return columns(values, [c * unit, (2 + c) * unit, (1 - c) * unit, (3 - c) * unit], unit)

    def core_natural(own, other):
        even, odd = jnp.where(c == 0, own, other), jnp.where(c == 0, other, own)
        return jnp.concatenate(
            [even[:, :unit], odd[:, :unit], even[:, unit:], odd[:, unit:]], axis=1
        )

    places = [2 * ((hi ^ at_hi) ^ c) + (e ^ at_e) for at_e in (0, 1) for at_hi in (0, 1)]
    numbers = [
        4 * (c ^ at_c) + 2 * (hi ^ at_hi) + (e ^ at_e)
        for at_c in (0, 1)
        for at_e in (0, 1)
        for at_hi in (0, 1)
    ]
    fourths = [2 * (hi ^ at_hi) + (e ^ at_e) for at_e in (0, 1) for at_hi in (0, 1)]
    heads = [
        4 * (c ^ at_c) + 2 * (at_hi ^ c) + at_e
        for at_c in (0, 1)
        for at_hi in (0, 1)
        for at_e in (0, 1)
    ]
    scalars = jnp.stack([*places, y, *numbers, *fourths, t, *heads]).astype(jnp.int32)

    def in_rows(mine, other):
        return in_order(t, mine, other, 0)

    def in_columns(mine, other):
        return in_order(y, mine, other, 1)

    def split_pairs(weight):
        low = weight.astype(LOW)
        return (
            columns(low, [j * pair + (1 - y) * HEAD_DIM for j in range(pairs)], HEAD_DIM),
            columns(low, [j * pair + y * HEAD_DIM for j in range(pairs)], HEAD_DIM),
        )

    def all_pairs(mine, theirs):
        even, odd = jnp.where(c == 0, mine, theirs), jnp.where(c == 0, theirs, mine)
        whole = jnp.concatenate(
            [even[:, :block], odd[:, :block], even[:, block:], odd[:, block:]], axis=1
        )

        def part(t_bit):
            starts = [8 * j + 4 * c + 2 * k + t_bit for j in range(3) for k in range(2)]
            return columns(whole, [start * HEAD_DIM for start in starts], HEAD_DIM)

        return part(1 - t), part(t)

    def split_rows(weight):
        low = weight.astype(LOW)
        return half(low, 0, 1 - y), half(low, 0, y)

    def unit_columns(low, t_bit, y_bit):
        return columns(low, [(4 * j + 2 * t_bit + y_bit) * unit for j in range(2)], unit)

    def split_in(weight):
        low = weight.astype(LOW)
        return (
            unit_columns(low, 1 - t, y),
            jnp.concatenate(
                [unit_columns(low, 1 - t, 1 - y), unit_columns(low, t, 1 - y)], axis=1
            ),
        )

    def norm_low(values, ids):
        normed, inverse = normalize(values.astype(FULL))
        extra = jnp.tile(ids.astype(LOW), (16, width // ROWS))
        return jnp.concatenate([relative(normed.astype(LOW)), extra], axis=0), inverse

    def attention_piece(kept, got, out_kept, out_y):
        rows = in_columns(out_kept, out_y)
        stacked = jnp.concatenate(
            [rows[:, j * pair : (j + 1) * pair] for j in range(width // 2 // pair)], axis=0
        )
        return jnp.concatenate([in_rows(kept, got), stacked], axis=1)

    def other_piece(in_t, in_y, in_b_t):
        return jnp.concatenate([in_t, in_rows(in_y[:, middle:], in_b_t)], axis=0)

    a_own = Gather(steps, lambda v: unit_columns(v, t, y).astype(LOW), master_in)
    given, kept = steps.do(split_pairs, master_qkv)
    pairs_y = swap(given, MASK_Y)
    give_t, give_y = steps.do(split_in, master_in)
    lowered_one, inverse_one = steps.do(norm_low, inputs, segment_ids)
    given, out_kept = steps.do(split_rows, master_out)
    pairs_mine = steps.do(in_columns, kept, pairs_y)
    pairs_core = swap(pairs_mine, MASK_C)
    out_y = swap(given, MASK_Y)
    tokens_one = Tokens(lowered_one)
    tokens_one.send_y(steps)
    given, pairs_kept = steps.do(all_pairs, pairs_mine, pairs_core)
    pairs_t = swap(given, MASK_T)
    give_down, down_kept = steps.do(split_rows, master_down)
    qkv = Gather(steps, attention_piece, pairs_kept, pairs_t, out_kept, out_y)
    tokens_one.from_y = steps.wait(tokens_one.from_y)
    tokens_one.send_t(steps)
    a_own.whole = steps.wait(a_own.whole)
    in_y = swap(steps.wait(give_y), MASK_Y)
    tokens_one.second(steps)
    in_t = swap(steps.wait(give_t), MASK_T)
    in_y = steps.wait(in_y)
    in_b_t = swap(steps.do(lambda v: v[:, :middle], in_y), MASK_T)
    down_y = swap(steps.wait(give_down), MASK_Y)
    rows_one = tokens_one.rows(steps)

    def attention_mask(own, from_y, from_t, upper):
        segments = jnp.stack(
            [own[ROWS], from_y[ROWS], upper[ROWS // 2], from_t[ROWS]], axis=0
        )[:, :ROWS]
        at = jnp.arange(ROWS)
        allowed = (segments[:, :, None] == segments[:, None, :]) & (at[None, :] <= at[:, None])
        return allowed.astype(FULL).reshape(4 * ROWS, ROWS)

    mask = steps.do(
        attention_mask, tokens_one.values, tokens_one.from_y, tokens_one.from_t, tokens_one.upper
    )
    cosine, sine = signed_tables()
    a_b = Gather(steps, other_piece, in_t, in_y, in_b_t)
    qkv_parts = qkv.parts(PIECE)
    qkv_arrays = [part.array for part in qkv_parts]
    projected = steps.do(
        functools.partial(product_pieces, qkv_parts, 3 * pair, scalars), rows_one, *qkv_arrays
    )
    down = Gather(steps, in_columns, down_kept, down_y)
    lowered, mixed_low = steps.do(attend, projected, mask, cosine, sine)

    weight_out = steps.do(functools.partial(join_heads, scalars), qkv.whole)

    def product_out(chunks, side, dtype, operand, weight):
        right = weight[:, side * middle : (side + 1) * middle]
        if chunks[0] + 1 == chunks[1]:
            left = operand[chunks[0] * ROWS : (chunks[1] + 1) * ROWS]
            return dot(left, right).astype(dtype)
        parts = [dot(operand[at * ROWS : (at + 1) * ROWS], right) for at in chunks]
        return jnp.concatenate(parts, axis=0).astype(dtype)

    sum_out = Sum(product_out, mixed_low, weight_out)
    sum_out.first(steps)
    sum_out.send()
    sum_out.own(steps)
    sum_out.second(steps)

    def norm_stream(values, *parts):
        stream = values.astype(FULL) + core_natural(*sum_out.total(*parts))
        normed, inverse = normalize(stream)
        return relative(normed.astype(LOW)), stream, inverse

    lowered_two, stream, inverse_two = steps.do(norm_stream, inputs, *sum_out.parts())
    tokens_two = Tokens(lowered_two)
    tokens_two.send(steps)
    tokens_two.second(steps)
    rows_two = tokens_two.rows(steps)
    tokens_cotangent = Tokens(steps.do(core_first, cotangent))
    tokens_cotangent.send(steps)

    own_a, other_a = a_own.parts(ROWS), a_b.parts(ROWS)
    even_b, odd_b = a_b.parts(ROWS, ROWS), a_b.parts(ROWS, 2 * ROWS)

    def in_turn(first, second, side):
        at = slice(4 * side, 4 * side + 4)
        return [part for two in zip(first[at], second[at]) for part in two]

    in_parts = [
        part
        for side in (0, 1)
        for kind in ((own_a, other_a), (even_b, odd_b))
        for part in in_turn(*kind, side)
    ]
    in_arrays = [part.array for part in in_parts]
    gate, upper, active = steps.do(
        functools.partial(unit_forward, in_parts, scalars), rows_two, *in_arrays
    )
    tokens_cotangent.second(steps)
    rows_cotangent = tokens_cotangent.rows(steps)
    placed_blocks = functools.partial(scatter_blocks, scalars, True)
    piece_blocks = functools.partial(scatter_blocks, scalars, False)
    scatter_down = Scatter(placed_blocks, active, rows_cotangent)
    scatter_down.core(steps)
    scatter_down.send(steps)
    down_parts = down.parts(PIECE)
    down_arrays = [part.array for part in down_parts]

    grad_a, grad_b = steps.do(
        functools.partial(unit_back, down_parts, scalars), rows_cotangent, gate, upper, *down_arrays
    )

    def placed_parts(parts, arrays):
        return [part._replace(array=array) for part, array in zip(parts, arrays)]

    def product_units(chunks, side, dtype, grad_a, grad_b, *arrays):
        parts = placed_parts(in_parts, arrays)
        terms = []
        for core in (0, 1):
            at = 16 * core + 4 * side
            whole_b = [part._replace(rows=PIECE) for part in parts[at + 8 : at + 12 : 2]]
            terms += [(grad_a, core, parts[at : at + 4]), (grad_b, core, whole_b)]
        return product_back(scalars, chunks, dtype, terms)

    sum_two = Sum(product_units, grad_a, grad_b, *in_arrays)
    sum_two.first(steps)
    sum_two.send()
    scatter_a = Scatter(piece_blocks, rows_two, grad_a)
    scatter_a.core(steps)
    sum_two.own(steps)
    scatter_a.send(steps)
    sum_two.second(steps)
    scatter_b = Scatter(piece_blocks, rows_two, grad_b)
    scatter_b.core(steps)

    def stream_back(grad, stream, inverse, *parts):
        normed = (stream - jnp.mean(stream, axis=-1, keepdims=True)) * inverse
        total = natural(jnp.concatenate(sum_two.total(*parts), axis=1))
        result = grad.astype(FULL) + norm_back(normed, inverse, total)
        return core_first(result.astype(LOW)), result

    stream_grad_low, stream_grad = steps.do(
        stream_back, cotangent, stream, inverse_two, *sum_two.parts()
    )
    tokens_stream = Tokens(stream_grad_low)
    tokens_stream.send(steps)
    scatter_b.send(steps)

    def product_final(chunks, side, dtype, active, *arrays):
        at = slice(4 * side, 4 * side + 4)
        return product_forward(chunks, dtype, down_parts[at], scalars, active, *arrays[at])

    sum_final = Sum(product_final, active, *down_arrays)
    sum_final.first(steps)
    give_down, mine_down = steps.do(
        lambda v: (half(v, 1, 1 - y), half(v, 1, y)), scatter_down.result
    )
    down_y = swap(give_down, MASK_Y)
    given, in_mine = steps.do(
        lambda v: (half(v, 0, 1 - t), half(v, 0, t)), scatter_a.result
    )
    from_t = swap(given, MASK_T)
    tokens_stream.second(steps)
    sum_final.own(steps)
    rows_stream = tokens_stream.rows(steps)
    sum_final.release(steps)
    sum_final.send()

    mixed_grad = steps.do(
        lambda rows, weight: dot_back(rows, weight).astype(LOW), rows_stream, weight_out
    )
    projected_grad = steps.do(attend_back, lowered, mask, cosine, sine, mixed_grad)
    down_y, from_t = steps.do(lambda *v: v, down_y, from_t)
    scatter_attention = Scatter(
        functools.partial(scatter_heads, scalars), rows_one, projected_grad, mixed_low, rows_stream
    )
    scatter_attention.core(steps)

    def product_qkv(chunks, side, dtype, gradient, *arrays):
        parts = placed_parts(qkv_parts, arrays)
        terms = [
            (gradient, core, parts[4 * core + 2 * side : 4 * core + 2 * side + 2])
            for core in (0, 1)
        ]
        return product_back(scalars, chunks, dtype, terms)

    sum_one = Sum(product_qkv, projected_grad, *qkv_arrays)
    def output_of(stream, *parts):
        final = stream + core_natural(*sum_final.total(*parts))
        squares = jnp.stack([jnp.sum(stream * stream), jnp.sum(final * final)]).reshape(1, 2)
        return final.astype(LOW), squares

    def input_back(values, inverse, grad, *parts):
        source = values.astype(FULL)
        normed = (source - jnp.mean(source, axis=-1, keepdims=True)) * inverse
        total = natural(jnp.concatenate(sum_one.total(*parts), axis=1))
        return (grad + norm_back(normed, inverse, total)).astype(LOW)

    def adam_down(mine, got, *state):
        gradient = in_order(y, mine, got, 0).astype(FULL)
        return (gradient, *adam_step(state[0], gradient, *state[1:], rate))

    def adam_in(mine, from_t, from_y, from_both, *state):
        sides = []
        for bit in range(2):
            same = jnp.where(t == bit, mine, from_t).astype(FULL)
            cross = jnp.where(t == bit, from_y, from_both).astype(FULL)
            sides.append((jnp.where(y == 0, same, cross), jnp.where(y == 0, cross, same)))
        blocks = [
            part[:, j * unit : (j + 1) * unit] for j in range(2) for side in sides for part in side
        ]
        gradient = jnp.concatenate(blocks, axis=1)
        return (gradient, *adam_step(state[0], gradient, *state[1:], rate))

    def split_attention(total):
        parts = total[:, : 3 * pair]
        out_rows = jnp.concatenate(
            [total[j * HEAD_DIM : (j + 1) * HEAD_DIM, 3 * pair :] for j in range(4)], axis=1
        )
        return (
            half(parts, 0, 1 - t),
            half(parts, 0, t),
            half(out_rows, 1, 1 - y),
            half(out_rows, 1, y),
        )

    def core_pairs(kept, got):
        even, odd = jnp.where(t == 0, kept, got), jnp.where(t == 0, got, kept)
        return jnp.concatenate(
            [
                part[:, j * HEAD_DIM : (j + 1) * HEAD_DIM]
                for j in range(6)
                for part in (even, odd)
            ],
            axis=1,
        )

    def split_grad(mine, theirs):
        even, odd = jnp.where(c == 0, mine, theirs), jnp.where(c == 0, theirs, mine)
        whole = jnp.concatenate(
            [
                part[:, j * 2 * pair : (j + 1) * 2 * pair]
                for j in range(3)
                for part in (even, odd)
            ],
            axis=1,
        )
        return (
            lax.dynamic_slice_in_dim(whole, (2 * (1 - y) + c) * block, block, 1),
            lax.dynamic_slice_in_dim(whole, (2 * y + c) * block, block, 1),
        )

    def adam_out(mine, got, *state):
        gradient = in_order(y, mine, got, 0).astype(FULL)
        return (gradient, *adam_step(state[0], gradient, *state[1:], rate_out))

    def adam_qkv(mine, got, *state):
        even, odd = jnp.where(y == 0, mine, got), jnp.where(y == 0, got, mine)
        gradient = jnp.concatenate(
            [
                part[:, j * HEAD_DIM : (j + 1) * HEAD_DIM]
                for j in range(pairs)
                for part in (even, odd)
            ],
            axis=1,
        ).astype(FULL)
        return (gradient, *adam_step(state[0], gradient, *state[1:], rate))

    def share(squares, bit):
        return steps.do(jnp.add, squares, swap(squares, bit))

    sum_one.first_y(steps)
    scatter_attention.send(steps)
    sum_one.first_t(steps)
    sum_final.second(steps)
    given_y, given_both = steps.do(
        lambda v: (half(v, 0, t), half(v, 0, 1 - t)), scatter_b.result
    )
    from_y = swap(given_y, MASK_Y)
    from_both = swap(given_both, MASK_Y | MASK_T)
    sum_one.release(steps)
    sum_one.send()
    sum_one.own(steps)
    output, squares = steps.do(output_of, stream, *sum_final.parts())
    squares = share(squares, MASK_E)
    step_down = steps.do(adam_down, mine_down, down_y, master_down, first_down, second_down)
    squares = share(squares, MASK_T)
    step_in = steps.do(
        adam_in, in_mine, from_t, from_y, from_both, master_in, first_in, second_in
    )
    squares = share(squares, MASK_HI)
    given, kept, give_out, mine_out = steps.do(split_attention, scatter_attention.result)
    pairs_t = swap(given, MASK_T)
    out_y = swap(give_out, MASK_Y)
    pairs_mine = steps.do(core_pairs, kept, pairs_t)
    pairs_core = swap(pairs_mine, MASK_C)
    sum_one.second(steps)
    squares = share(squares, MASK_C)
    given, kept = steps.do(split_grad, pairs_mine, pairs_core)
    pairs_y = swap(given, MASK_Y)
    step_out = steps.do(adam_out, mine_out, out_y, master_out, first_out, second_out)
    squares = share(squares, MASK_Y)
    stream_rms = jnp.sqrt(squares[0] / (ROWS * width * DEVICES))
    step_qkv = steps.do(adam_qkv, kept, pairs_y, master_qkv, first_qkv, second_qkv)
    input_grad = steps.do(input_back, inputs, inverse_one, stream_grad, *sum_one.parts())
    results = zip(step_qkv, step_out, step_in, step_down)
    grads, updated, moments, variances, narrows = results
    return (output, input_grad, *grads, *updated, *moments, *variances, *narrows, stream_rms)


def solution(mesh):
    shards = split_layer if tuple(mesh.shape.values()) == (4, 8) else gathered_layer
    return jax.shard_map(
        shards,
        mesh=mesh,
        in_specs=(
            P(("rep", "fsdp"), None),
            P(("rep", "fsdp"), None),
            P(("rep", "fsdp"), None),
            P("fsdp", "rep"),
            P("fsdp", "rep"),
            P("fsdp", "rep"),
            P("fsdp", "rep"),
            P("fsdp", "rep"),
            P("fsdp", "rep"),
            P("fsdp", "rep"),
            P("fsdp", "rep"),
            P("fsdp", "rep"),
            P("fsdp", "rep"),
            P("fsdp", "rep"),
            P("fsdp", "rep"),
        ),
        out_specs=(
            P(("rep", "fsdp"), None),
            P(("rep", "fsdp"), None),
            P("fsdp", "rep"),
            P("fsdp", "rep"),
            P("fsdp", "rep"),
            P("fsdp", "rep"),
            P("fsdp", "rep"),
            P("fsdp", "rep"),
            P("fsdp", "rep"),
            P("fsdp", "rep"),
            P("fsdp", "rep"),
            P("fsdp", "rep"),
            P("fsdp", "rep"),
            P("fsdp", "rep"),
            P("fsdp", "rep"),
            P("fsdp", "rep"),
            P("fsdp", "rep"),
            P("fsdp", "rep"),
            P("fsdp", "rep"),
            P("fsdp", "rep"),
            P("fsdp", "rep"),
            P("fsdp", "rep"),
            P(),
        ),
        check_vma=False,
    )
```
